32 devices in a mesh: dp: 4 (over x, core), fsdp: 8 (over z, y).
Axes of the slice: x: 2, y: 2, z: 4, core: 2. Of those that a mesh axis runs over, the one named last changes fastest.
Arguments:
- residues: bfloat16 [128, 32, 768], P(('dp', 'fsdp')), may hold values from -6 to 6
- pairs: bfloat16 [128, 32, 32, 256], P(('dp', 'fsdp')), may hold values from -6 to 6
- lengths: int32 [128], P(('dp', 'fsdp')), may hold values from 8 to 32, as said below
- time_bins: int32 [128], P(('dp', 'fsdp')), may hold values from 0 to 255
- cath_labels: int32 [128], P(('dp', 'fsdp')), may hold values from 0 to 1471
- residue_cotangent: bfloat16 [128, 32, 768], P(('dp', 'fsdp')), may hold values from -6 to 6
- pair_cotangent: bfloat16 [128, 32, 32, 256], P(('dp', 'fsdp')), may hold values from -6 to 6
- time_table: bfloat16 [256, 768], P('fsdp'), may hold values from -4 to 4
- cath_table: bfloat16 [1472, 768], P('fsdp'), may hold values from -4 to 4
- attn_modulation: bfloat16 [768, 1536], P('fsdp'), may hold values from -0.21875 to 0.21875
- attn_gate: bfloat16 [768, 768], P('fsdp'), may hold values from -0.21875 to 0.21875
- qkv_weight: bfloat16 [768, 2304], P('fsdp'), may hold values from -0.21875 to 0.21875
- bias_gain: bfloat16 [256], P('fsdp'), may hold values from 0.25 to 1.75
- bias_weight: bfloat16 [256, 12], P('fsdp'), may hold values from -0.375 to 0.375
- out_weight: bfloat16 [768, 768], P('fsdp'), may hold values from -1 to 1
- ffn_modulation: bfloat16 [768, 1536], P('fsdp'), may hold values from -0.21875 to 0.21875
- ffn_gate: bfloat16 [768, 768], P('fsdp'), may hold values from -0.21875 to 0.21875
- gate_up: bfloat16 [768, 6144], P('fsdp'), may hold values from -0.21875 to 0.21875
- down_weight: bfloat16 [3072, 768], P('fsdp'), may hold values from -0.3125 to 0.3125
- outer_gain: bfloat16 [768], P('fsdp'), may hold values from 0.25 to 1.75
- outer_weight: bfloat16 [768, 512], P('fsdp'), may hold values from -0.21875 to 0.21875
- outer_out: bfloat16 [256, 256], P('fsdp'), may hold values from -0.375 to 0.375
- pair_gain: bfloat16 [256], P('fsdp'), may hold values from 0.25 to 1.75
- pair_gate_up: bfloat16 [256, 2048], P('fsdp'), may hold values from -0.375 to 0.375
- pair_down: bfloat16 [1024, 256], P('fsdp'), may hold values from -0.3125 to 0.3125
Outputs:
- residues_out: bfloat16 [128, 32, 768], P(('dp', 'fsdp'))
- pairs_out: bfloat16 [128, 32, 32, 256], P(('dp', 'fsdp'))
- residues_grad: float32 [128, 32, 768], P(('dp', 'fsdp'))
- pairs_grad: float32 [128, 32, 32, 256], P(('dp', 'fsdp'))
- grad_time_table: float32 [256, 768], P('fsdp')
- grad_cath_table: float32 [1472, 768], P('fsdp')
- grad_attn_modulation: float32 [768, 1536], P('fsdp')
- grad_attn_gate: float32 [768, 768], P('fsdp')
- grad_qkv_weight: float32 [768, 2304], P('fsdp')
- grad_bias_gain: float32 [256], P('fsdp')
- grad_bias_weight: float32 [256, 12], P('fsdp')
- grad_out_weight: float32 [768, 768], P('fsdp')
- grad_ffn_modulation: float32 [768, 1536], P('fsdp')
- grad_ffn_gate: float32 [768, 768], P('fsdp')
- grad_gate_up: float32 [768, 6144], P('fsdp')
- grad_down_weight: float32 [3072, 768], P('fsdp')
- grad_outer_gain: float32 [768], P('fsdp')
- grad_outer_weight: float32 [768, 512], P('fsdp')
- grad_outer_out: float32 [256, 256], P('fsdp')
- grad_pair_gain: float32 [256], P('fsdp')
- grad_pair_gate_up: float32 [256, 2048], P('fsdp')
- grad_pair_down: float32 [1024, 256], P('fsdp')
The draws below stay inside these ranges and needn't reach their ends.
Inputs may be any that keep to these rules, and one draw needn't show every extreme that they name: `lengths`: each chain holds 32, 16 or 8 residues; slots at and past that number are padding.
All inputs are finite; a program needn't handle non-finite values.
Results may differ from the reference program's by a relative error of at most 0.03.
Values may be sent and summed in bfloat16 or wider, within the bound.
No kernel may reach another device: no remote copies, remote signals or barrier semaphores. Data moves between devices by JAX's collectives and lax.ppermute only.
A program may use at most 256 MiB of HBM per device.

```python
import math
import jax
import jax.numpy as jnp
import numpy as np
from jax import lax

D = 768
HEADS = 12
FFN = 3072
PAIR = 256
PAIR_HID = 1024
CATH_LABELS = 1472
TBINS = 256
LMAX = 32
CHAINS = 128


def draw_lengths(key, part):
    key = jax.random.fold_in(key, 7)
    bucket_level = jax.random.randint(key, (CHAINS,), 0, 3)
    chain_sizes = jnp.where(bucket_level == 0, LMAX, jnp.where(bucket_level == 1, LMAX // 2, LMAX // 4))
    chain_sizes = chain_sizes.at[0].set(LMAX).at[1].set(LMAX // 4)
    return chain_sizes.astype(jnp.int32)


def set_ends(drawn, key, low, largest):
    place = [jax.random.randint(jax.random.fold_in(key, axis), (), 0, length) for axis, length in enumerate(drawn.shape)]
    main_axis = drawn.shape.index(max(drawn.shape))
    beside = place[:main_axis] + [(place[main_axis] + 1) % drawn.shape[main_axis]] + place[main_axis + 1:]
    return drawn.at[tuple(place)].set(low).at[tuple(beside)].set(largest)


def block_levels(key, dims, shards, low, high):
    def one(dim, shards_of):
        draws = jax.random.uniform(jax.random.fold_in(jax.random.fold_in(key, 6), dim), (shards_of,), jnp.float32, low / len(shards), high / len(shards))
        return jnp.repeat(jnp.exp(draws), dims[dim] // shards_of).reshape((-1,) + (1,) * (len(dims) - dim - 1))

    loudness = one(*shards[0])
    for cut in shards[1:]:
        loudness = loudness * one(*cut)
    return loudness


def rank_table(count, slope):
    weights = [(1 << 20) // math.isqrt(rank ** slope) + 1 for rank in range(1, count + 1)]
    scale = 1 + sum(weights) // (1 << 30)
    return np.cumsum(np.array([max(1, weight // scale) for weight in weights]))


def skewed_ids(rng, dims, count, skew):
    grid = rank_table(count, skew)
    lot = jax.random.randint(jax.random.fold_in(rng, 1), dims, 0, int(grid[count - 1]))
    standing = jnp.searchsorted(jnp.asarray(grid, jnp.int32), lot, side="right")
    return jax.random.permutation(jax.random.fold_in(rng, 2), count)[standing].astype(jnp.int32)


def normal_values(rng, extent, deviation, reach, shards=(), dtype=jnp.bfloat16):
    level = block_levels(rng, extent, shards, -0.22, 0.18) if shards else 1.0
    result = jax.random.normal(rng, extent, jnp.float32) * deviation * level
    return jnp.minimum(jnp.maximum(result, -reach), reach).astype(dtype)


def setup_inputs(seed: int = 0) -> dict:
    splits = jax.random.split(jax.random.key(seed), 26)
    return {
        "residues": normal_values(splits[0], (CHAINS, LMAX, D), 1.0, 6.0, ((0, 32),)),
        "pairs": normal_values(splits[1], (CHAINS, LMAX, LMAX, PAIR), 1.0, 6.0, ((0, 32),)),
        "lengths": draw_lengths(jax.random.fold_in(splits[25], 71), 0),
        "time_bins": set_ends(jax.random.randint(splits[3], (CHAINS,), 0, TBINS), jax.random.fold_in(splits[3], 1), 0, TBINS - 1).astype(jnp.int32),
        "cath_labels": set_ends(skewed_ids(splits[4], (CHAINS,), CATH_LABELS, 2), jax.random.fold_in(splits[4], 3), 0, CATH_LABELS - 1).astype(jnp.int32),
        "residue_cotangent": normal_values(splits[5], (CHAINS, LMAX, D), 1.0, 6.0, ((0, 32),)),
        "pair_cotangent": normal_values(splits[6], (CHAINS, LMAX, LMAX, PAIR), 1.0, 6.0, ((0, 32),)),
        "time_table": normal_values(splits[7], (TBINS, D), 0.7, 4.0, ((0, 8),)),
        "cath_table": normal_values(splits[8], (CATH_LABELS, D), 0.7, 4.0, ((0, 8),)),
        "attn_modulation": normal_values(splits[9], (D, 2 * D), D ** -0.5, 0.21875, ((0, 8),)),
        "attn_gate": normal_values(splits[10], (D, D), D ** -0.5, 0.21875, ((0, 8),)),
        "qkv_weight": normal_values(splits[11], (D, 3 * D), D ** -0.5, 0.21875, ((0, 8),)),
        "bias_gain": jnp.clip(1.0 + 0.15 * jax.random.normal(splits[12], (PAIR,), jnp.float32), 0.25, 1.75).astype(jnp.bfloat16),
        "bias_weight": normal_values(splits[13], (PAIR, HEADS), PAIR ** -0.5, 0.375, ((0, 8),)),
        "out_weight": normal_values(splits[14], (D, D), (max(D // 24, 8)) ** -0.5, 1.0, ((0, 8),)),
        "ffn_modulation": normal_values(splits[15], (D, 2 * D), D ** -0.5, 0.21875, ((0, 8),)),
        "ffn_gate": normal_values(splits[16], (D, D), D ** -0.5, 0.21875, ((0, 8),)),
        "gate_up": normal_values(splits[17], (D, 2 * FFN), D ** -0.5, 0.21875, ((0, 8),)),
        "down_weight": normal_values(splits[18], (FFN, D), (FFN // 8) ** -0.5, 0.3125, ((0, 8),)),
        "outer_gain": jnp.clip(1.0 + 0.15 * jax.random.normal(splits[19], (D,), jnp.float32), 0.25, 1.75).astype(jnp.bfloat16),
        "outer_weight": normal_values(splits[20], (D, 2 * PAIR), D ** -0.5, 0.21875, ((0, 8),)),
        "outer_out": normal_values(splits[21], (PAIR, PAIR), PAIR ** -0.5, 0.375, ((0, 8),)),
        "pair_gain": jnp.clip(1.0 + 0.15 * jax.random.normal(splits[22], (PAIR,), jnp.float32), 0.25, 1.75).astype(jnp.bfloat16),
        "pair_gate_up": normal_values(splits[23], (PAIR, 2 * PAIR_HID), PAIR ** -0.5, 0.375, ((0, 8),)),
        "pair_down": normal_values(splits[24], (PAIR_HID, PAIR), (PAIR_HID // 3) ** -0.5, 0.3125, ((0, 8),)),
    }


EPSILON = 1e-05
PRECISE = lax.Precision.HIGHEST

@jax.custom_vjp
def low(v):
    return lax.optimization_barrier(v.astype(jnp.bfloat16)).astype(jnp.float32)

@jax.custom_vjp
def low_back(v):
    return v

def low_keep(v):
    return (low(v), None)

def low_pass(kept, grad):
    return (grad,)

def back_keep(v):
    return (v, None)

def back_low(kept, grad):
    return (low(grad),)
low.defvjp(low_keep, low_pass)
low_back.defvjp(back_keep, back_low)

def normalize(values):
    center = values - lax.optimization_barrier(jnp.mean(values, -1, keepdims=True))
    return center * lax.rsqrt(lax.optimization_barrier(jnp.mean(center * center, -1, keepdims=True)) + EPSILON)

def product(left_side, right_side):
    return jnp.matmul(left_side, right_side, precision=PRECISE)

def activate(values):
    return values * jax.nn.sigmoid(values)

def forward(params, residues, pairs, time_bins, cath_labels, keep_rows):
    time_table, cath_table, attn_modulation, attn_gate, qkv_weight, bias_gain, bias_weight, out_weight, ffn_modulation, ffn_gate, gate_up, down_weight, outer_gain, outer_weight, outer_out, pair_gain, pair_gate_up, pair_down = params
    chains, length, model_width = residues.shape
    head_count = bias_weight.shape[1]
    head_size = model_width // head_count
    hidden = down_weight.shape[0]
    pair_width = outer_out.shape[0]
    pair_hidden = pair_down.shape[0]
    factor = 1.0 / math.sqrt(head_size)
    keep_col = keep_rows[:, :, None]
    keep_pairs = (keep_rows[:, :, None] * keep_rows[:, None, :])[..., None]
    condition = low(time_table[time_bins] + cath_table[cath_labels])
    first_mod = product(condition, attn_modulation)
    first_scale = first_mod[:, None, :model_width]
    first_shift = first_mod[:, None, model_width:]
    first_gate = jax.nn.sigmoid(product(condition, attn_gate))[:, None, :]
    second_mod = product(condition, ffn_modulation)
    second_scale = second_mod[:, None, :model_width]
    second_shift = second_mod[:, None, model_width:]
    second_gate = jax.nn.sigmoid(product(condition, ffn_gate))[:, None, :]
    first_in = low(normalize(residues) * (1.0 + first_scale) + first_shift)
    qkv_all = low(low_back(product(first_in, qkv_weight)))
    queries = qkv_all[..., :model_width].reshape(chains, length, head_count, head_size)
    key_rows = qkv_all[..., model_width:2 * model_width].reshape(chains, length, head_count, head_size)
    value_rows = qkv_all[..., 2 * model_width:].reshape(chains, length, head_count, head_size)
    bias_in = low(normalize(pairs) * bias_gain)
    pair_bias = product(bias_in, bias_weight)
    raw_scores = jnp.einsum('cihe,cjhe->chij', queries, key_rows, precision=PRECISE) * factor
    raw_scores = raw_scores + jnp.transpose(pair_bias, (0, 3, 1, 2))
    scores = low_back(jnp.where(keep_rows[:, None, None, :] > 0, raw_scores, -1000000000.0))
    exp_scores = jnp.exp(scores - lax.optimization_barrier(jnp.max(scores, -1, keepdims=True)))
    attend = low(exp_scores / lax.optimization_barrier(jnp.sum(exp_scores, -1, keepdims=True)))
    attended = jnp.einsum('chij,cjhe->cihe', attend, value_rows, precision=PRECISE)
    attended = low(low_back(attended.reshape(chains, length, model_width)))
    first_out = residues + keep_col * first_gate * low_back(product(attended, out_weight))
    second_in = low(normalize(first_out) * (1.0 + second_scale) + second_shift)
    gate_both = low_back(product(second_in, gate_up))
    hidden_act = low(activate(gate_both[..., :hidden]) * gate_both[..., hidden:])
    second_out = first_out + keep_col * second_gate * low_back(product(hidden_act, down_weight))
    outer_in = low(normalize(second_out) * outer_gain)
    left_right = low_back(product(outer_in, outer_weight))
    outer_prod = low(left_right[:, :, None, :pair_width] * left_right[:, None, :, pair_width:])
    pair_one = pairs + keep_pairs * low_back(product(outer_prod, outer_out))
    pair_in_two = low(normalize(pair_one) * pair_gain)
    pair_both = low_back(product(pair_in_two, pair_gate_up))
    pair_act = low(activate(pair_both[..., :pair_hidden]) * pair_both[..., pair_hidden:])
    pair_two = pair_one + keep_pairs * low_back(product(pair_act, pair_down))
    return (second_out, pair_two)

def group_pass(params, residues, pairs, lengths, time_bins, cath_labels, residue_cot, pair_cot):
    length = residues.shape[1]
    keep_rows = (jnp.arange(length)[None, :] < lengths[:, None]).astype(jnp.float32)

    def apply_layer(weights, res_in, pair_in):
        return forward(weights, res_in, pair_in, time_bins, cath_labels, keep_rows)
    results, pullback = jax.vjp(apply_layer, params, residues, pairs)
    weight_grads, res_grad, pair_grad = pullback((residue_cot, pair_cot))
    return (results[0], results[1], res_grad, pair_grad, weight_grads)

def reference(residues, pairs, lengths, time_bins, cath_labels, residue_cotangent, pair_cotangent, time_table, cath_table, attn_modulation, attn_gate, qkv_weight, bias_gain, bias_weight, out_weight, ffn_modulation, ffn_gate, gate_up, down_weight, outer_gain, outer_weight, outer_out, pair_gain, pair_gate_up, pair_down):
    params = tuple((weight.astype(jnp.float32) for weight in (time_table, cath_table, attn_modulation, attn_gate, qkv_weight, bias_gain, bias_weight, out_weight, ffn_modulation, ffn_gate, gate_up, down_weight, outer_gain, outer_weight, outer_out, pair_gain, pair_gate_up, pair_down)))
    group_size = math.gcd(CHAINS, 8)
    group_count = CHAINS // group_size

    def split_groups(stacked_part):
        return stacked_part.reshape((group_count, group_size) + stacked_part.shape[1:])

    def scan_step(running, block_in):
        res_block, pair_block, len_block, bin_block, label_block, res_cot, pair_cot = block_in
        res_out, pair_out, res_grad, pair_grad, weight_grads = group_pass(params, res_block.astype(jnp.float32), pair_block.astype(jnp.float32), len_block, bin_block, label_block, res_cot.astype(jnp.float32), pair_cot.astype(jnp.float32))
        running = jax.tree.map(lambda earlier, later: earlier + later, running, weight_grads)
        return (running, (res_out.astype(jnp.bfloat16), pair_out.astype(jnp.bfloat16), res_grad, pair_grad))
    zeros_init = jax.tree.map(jnp.zeros_like, params)
    totals, stacked = lax.scan(scan_step, zeros_init, (split_groups(residues), split_groups(pairs), split_groups(lengths), split_groups(time_bins), split_groups(cath_labels), split_groups(residue_cotangent), split_groups(pair_cotangent)))
    merged = jax.tree.map(lambda stacked_part: stacked_part.reshape((CHAINS,) + stacked_part.shape[2:]), stacked)
    return (merged[0], merged[1], merged[2], merged[3], totals[0], totals[1], totals[2], totals[3], totals[4], totals[5], totals[6], totals[7], totals[8], totals[9], totals[10], totals[11], totals[12], totals[13], totals[14], totals[15], totals[16], totals[17])
```

```python
import functools
import math

import jax
import jax.numpy as jnp
from jax import lax
from jax.experimental import pallas as pl
from jax.experimental.pallas import tpu as pltpu
from jax.sharding import PartitionSpec as P

EPSILON = 1e-05
F32 = jnp.float32
BF16 = jnp.bfloat16
VMEM_LIMIT = 56 * 1024 * 1024


def norm_parts(values):
    center = values - jnp.mean(values, -1, keepdims=True)
    inverse = lax.rsqrt(jnp.mean(center * center, -1, keepdims=True) + EPSILON)
    return center * inverse, inverse


def norm_back(normed, inverse, upstream):
    return inverse * (
        upstream
        - jnp.mean(upstream, -1, keepdims=True)
        - normed * jnp.mean(upstream * normed, -1, keepdims=True)
    )


def dot(left, right):
    return jnp.dot(left, right, preferred_element_type=F32)


def dot_nt(left, right):
    return lax.dot_general(left, right, (((1,), (1,)), ((), ())), preferred_element_type=F32)


def dot_tn(left, right):
    return lax.dot_general(left, right, (((0,), (0,)), ((), ())), preferred_element_type=F32)


def params():
    return pltpu.CompilerParams(vmem_limit_bytes=VMEM_LIMIT)


def whole(shape):
    return pl.BlockSpec(shape, lambda *_: (0,) * len(shape))


SMEM = pl.BlockSpec(memory_space=pltpu.SMEM)


def call_whole(kernel, name, outs, *operands):
    specs = [SMEM if a.dtype == jnp.int32 else whole(a.shape) for a in operands]
    return pl.pallas_call(
        kernel,
        grid=(1,),
        name=name,
        in_specs=specs,
        out_specs=[whole(o.shape) for o in outs],
        out_shape=outs,
        compiler_params=params(),
    )(*operands)


def struct(shape, dtype):
    return jax.ShapeDtypeStruct(shape, dtype)


def swap(values, axis, size, bit):
    return lax.ppermute(values, axis, [(i, i ^ bit) for i in range(size)])


def pick(values, index, axis):
    return lax.dynamic_index_in_dim(values, index, axis, keepdims=False)


def ordered(bit, own, other, axis):
    first = jnp.where(bit == 0, own, other)
    second = jnp.where(bit == 0, other, own)
    return jnp.stack([first, second], axis)


class Place:
    def __init__(self, n_dp, n_f):
        self.n_dp, self.n_f, self.ring = n_dp, n_f, n_f // 2
        self.d = lax.axis_index("dp")
        self.f = lax.axis_index("fsdp")
        self.core, self.x = self.d % 2, self.d // 2
        self.y, self.r = self.f % 2, self.f // 2

    def swap_core(self, values):
        return swap(values, "dp", self.n_dp, 1)

    def swap_x(self, values):
        return swap(values, "dp", self.n_dp, 2)

    def swap_y(self, values):
        return swap(values, "fsdp", self.n_f, 1)

    def shift_ring(self, values):
        return lax.ppermute(
            values, "fsdp", [(i, (i + 2) % self.n_f) for i in range(self.n_f)]
        )

    def gather_f(self, values):
        ring = self.ring
        held = jnp.zeros((ring,) + values.shape, values.dtype)
        held = lax.dynamic_update_index_in_dim(held, values, self.r, 0)
        moving = values
        for step in range(ring - 1):
            moving = self.shift_ring(moving)
            held = lax.dynamic_update_index_in_dim(
                held, moving, (self.r - 1 - step) % ring, 0
            )
        both = ordered(self.y, held, self.swap_y(held), 1)
        return both.reshape((self.n_f,) + values.shape)

    def gather_quarters(self, quarter):
        held = self.gather_f(quarter)
        held = ordered(self.x, held, self.swap_x(held), 1)
        held = ordered(self.core, held, self.swap_core(held), 2)
        return held.reshape((self.n_f, 4) + quarter.shape)

    def sum_f(self, values):
        bit = 1
        while bit < self.n_f:
            values = values + swap(values, "fsdp", self.n_f, bit)
            bit *= 2
        return values

    def gather_bits(self, values, axis, size, index):
        held = values[None]
        bit = 1
        while bit < size:
            other = swap(held, axis, size, bit)
            on = (index // bit) % 2
            held = ordered(on, held, other, 0).reshape((2 * held.shape[0],) + values.shape)
            bit *= 2
        return held

    def gather_bits_f(self, values):
        return self.gather_bits(values, "fsdp", self.n_f, self.f)

    def gather_bits_d(self, values):
        return self.gather_bits(values, "dp", self.n_dp, self.d)

    def rows_gather(self, values):
        mine = jnp.concatenate([values, self.swap_x(values)], 0)
        return jnp.concatenate([mine, self.swap_core(mine)], 0)

    def rows_reduce(self, mine, theirs):
        half = mine.shape[0] // 2
        mine = mine + self.swap_core(theirs).astype(F32)
        return mine[:half], self.swap_x(mine[half:].astype(BF16))

    def halve(self, values, axis, index, swapper):
        keep = pick(values, index, axis)
        other = swapper(pick(values, 1 - index, axis))
        return (keep.astype(F32) + other.astype(F32)).astype(BF16)

    def reduce_f(self, values):
        ring = self.ring
        rest = values.shape[1:]
        values = self.halve(values.reshape((ring, 2) + rest), 1, self.y, self.swap_y)
        moving = pick(values, (self.r - 1) % ring, 0)
        for step in range(ring - 1):
            own = pick(values, (self.r - 2 - step) % ring, 0)
            moving = (
                self.shift_ring(moving).astype(F32) + own.astype(F32)
            ).astype(BF16)
        return moving

    def reduce_all(self, values):
        n_f, rows, width = values.shape
        values = values.reshape(n_f, 2, 2, rows // 4, width)
        values = self.halve(values, 2, self.core, self.swap_core)
        values = self.halve(values, 1, self.x, self.swap_x)
        values = self.reduce_f(values)
        return self.spread_d(values).reshape(rows, width)

    def spread_d(self, values):
        held = ordered(self.x, values, self.swap_x(values), 0)
        held = ordered(self.core, held, self.swap_core(held), 1)
        return held.reshape((4,) + values.shape)


def to_blocks(values):
    rows, width = values.shape
    blocks = values.reshape(rows, width // 256, 256)
    return jnp.transpose(blocks, (1, 0, 2)).reshape(rows * (width // 256), 256)


def from_blocks(held, rows, width):
    lead = held.shape[:-2]
    blocks = held.reshape(lead + (width // 256, rows, 256))
    return jnp.swapaxes(blocks, -3, -2).reshape(lead + (rows, width))


def choose_matrix(group, part, member):
    row = lax.broadcasted_iota(jnp.int32, (1536, 384), 0)
    col = lax.broadcasted_iota(jnp.int32, (1536, 384), 1)
    want = (col // part) * group + member * part + col % part
    return jnp.where(row == want, 1.0, 0.0).astype(BF16)


def split_kernel(group, part, place_ref, full_ref, out_ref):
    choose = choose_matrix(group, part, place_ref[0])
    for chunk in range(full_ref.shape[1] // 1536):
        out_ref[:, chunk * 384 : chunk * 384 + 384] = dot(
            full_ref[:, chunk * 1536 : chunk * 1536 + 1536], choose
        ).astype(BF16)


def join_kernel(group, part, pieces_ref, out_ref):
    for member in range(4):
        choose = choose_matrix(group, part, member)
        for chunk in range(out_ref.shape[1] // 1536):
            span = slice(chunk * 1536, chunk * 1536 + 1536)
            term = dot_nt(pieces_ref[member][:, chunk * 384 : chunk * 384 + 384], choose)
            if member == 0:
                out_ref[:, span] = term
            else:
                out_ref[:, span] += term


def bias_kernel(pairs_ref, gain_ref, weight_ref, out_ref):
    normed, _ = norm_parts(pairs_ref[...].astype(F32))
    low = (normed * gain_ref[...]).astype(BF16)
    out_ref[...] = dot_nt(weight_ref[...], low)


def head_mask(heads, length, width):
    head_size = width // heads
    row = lax.broadcasted_iota(jnp.int32, (heads * length, width), 0) // length
    col = lax.broadcasted_iota(jnp.int32, (heads * length, width), 1) // head_size
    return row == col


def spread_heads(rows, mask, heads):
    return jnp.where(mask, jnp.concatenate([rows] * heads, 0), jnp.zeros((), rows.dtype))


def fold_heads(wide, mask, heads):
    kept = jnp.where(mask, wide, 0.0)
    return jnp.sum(kept.reshape(heads, wide.shape[0] // heads, wide.shape[1]), 0)


def keep_of(lengths_ref, chain, length):
    row = lax.broadcasted_iota(jnp.int32, (length, 1), 0)
    return (row < lengths_ref[chain]).astype(F32)


def attention_kernel(
    heads,
    lengths_ref,
    res_ref,
    mod_ref,
    qkv_w_ref,
    out_w_ref,
    bias_ref,
    first_in_ref,
    qkv_ref,
    prob_ref,
    attended_ref,
    branch_ref,
    first_out_ref,
    second_in_ref,
):
    chains, length, width = res_ref.shape
    factor = 1.0 / math.sqrt(width // heads)
    mask = head_mask(heads, length, width)
    for c in range(chains):
        rows = slice(c * length, (c + 1) * length)
        normed, _ = norm_parts(res_ref[c].astype(F32))
        scale = mod_ref[c : c + 1, :width]
        shift = mod_ref[c : c + 1, width : 2 * width]
        first_in_ref[rows] = (normed * (1.0 + scale) + shift).astype(BF16)
    qkv_ref[...] = dot(first_in_ref[...], qkv_w_ref[...]).astype(BF16)
    for c in range(chains):
        rows = slice(c * length, (c + 1) * length)
        queries = spread_heads(qkv_ref[rows, :width], mask, heads)
        keys = qkv_ref[rows, width : 2 * width]
        value_rows = qkv_ref[rows, 2 * width :]
        scores = dot_nt(queries, keys) * factor + bias_ref[c]
        column = lax.broadcasted_iota(jnp.int32, scores.shape, 1)
        scores = jnp.where(column < lengths_ref[c], scores, -1000000000.0)
        exps = jnp.exp(scores - jnp.max(scores, -1, keepdims=True))
        prob = exps / jnp.sum(exps, -1, keepdims=True)
        prob_ref[c] = prob
        wide = dot(prob.astype(BF16), value_rows)
        attended_ref[rows] = fold_heads(wide, mask, heads).astype(BF16)
    branch_ref[...] = dot(attended_ref[...], out_w_ref[...])
    for c in range(chains):
        rows = slice(c * length, (c + 1) * length)
        keep = keep_of(lengths_ref, c, length)
        gate = mod_ref[c : c + 1, 2 * width : 3 * width]
        first_out = res_ref[c].astype(F32) + keep * gate * branch_ref[rows]
        first_out_ref[rows] = first_out
        normed, _ = norm_parts(first_out)
        scale = mod_ref[c : c + 1, 3 * width : 4 * width]
        shift = mod_ref[c : c + 1, 4 * width : 5 * width]
        second_in_ref[rows] = (normed * (1.0 + scale) + shift).astype(BF16)


def silu_parts(gate):
    logistic = jax.nn.sigmoid(gate)
    act = gate * logistic
    return act, logistic + act * (1.0 - logistic)


def transition_kernel(rows_ref, weight_ref, gate_ref, up_ref, hidden_ref, mine_ref, theirs_ref):
    width = rows_ref.shape[1]
    part = (weight_ref.shape[1] - width) // 2
    half = mine_ref.shape[0]
    rows = rows_ref[...]
    gate = dot(rows, weight_ref[:, :part])
    up = dot(rows, weight_ref[:, part : 2 * part])
    gate_ref[...] = gate
    up_ref[...] = up
    hidden = (gate * jax.nn.sigmoid(gate) * up).astype(BF16)
    hidden_ref[...] = hidden
    down = weight_ref[:, 2 * part :]
    mine_ref[...] = dot(hidden[:half], down)
    theirs_ref[...] = dot(hidden[half:], down).astype(BF16)


def outer_kernel(
    lengths_ref,
    first_out_ref,
    branch_own_ref,
    branch_other_ref,
    mod_ref,
    gain_ref,
    weight_ref,
    branch_ref,
    second_out_ref,
    res_out_ref,
    outer_in_ref,
    sides_ref,
):
    chains, width = mod_ref.shape[0], first_out_ref.shape[1]
    length = first_out_ref.shape[0] // chains
    branch = branch_own_ref[...] + branch_other_ref[...].astype(F32)
    branch_ref[...] = branch
    for c in range(chains):
        rows = slice(c * length, (c + 1) * length)
        keep = keep_of(lengths_ref, c, length)
        gate = mod_ref[c : c + 1, 5 * width : 6 * width]
        second_out_ref[rows] = first_out_ref[rows] + keep * gate * branch[rows]
    second_out = second_out_ref[...]
    res_out_ref[...] = second_out.astype(BF16)
    normed, _ = norm_parts(second_out)
    outer_in_ref[...] = (normed * gain_ref[...]).astype(BF16)
    sides_ref[...] = dot(outer_in_ref[...], weight_ref[...])


def pair_kernel(
    lengths_ref,
    left_ref,
    right_ref,
    pairs_ref,
    cot_ref,
    gain_ref,
    outer_w_ref,
    gate_up_ref,
    down_ref,
    pair_out_ref,
    pair_grad_ref,
    left_grad_ref,
    right_grad_ref,
    g_gate_up_ref,
    g_down_ref,
    g_outer_ref,
    g_gain_ref,
    acc_gate_up,
    acc_down,
    acc_outer,
    acc_gain,
):
    chain, block = pl.program_id(0), pl.program_id(1)
    _, count, length, width = pairs_ref.shape
    rows = count * length
    hidden = down_ref.shape[0]
    size = lengths_ref[chain]

    @pl.when((chain == 0) & (block == 0))
    def _():
        acc_gate_up[...] = jnp.zeros_like(acc_gate_up)
        acc_down[...] = jnp.zeros_like(acc_down)
        acc_outer[...] = jnp.zeros_like(acc_outer)
        acc_gain[...] = jnp.zeros_like(acc_gain)

    @pl.when(block == 0)
    def _():
        right_grad_ref[...] = jnp.zeros_like(right_grad_ref)

    @pl.when(block * count >= size)
    def _():
        pair_out_ref[...] = pairs_ref[...]
        pair_grad_ref[...] = cot_ref[...].astype(F32)
        left_grad_ref[...] = jnp.zeros_like(left_grad_ref)

    @pl.when(block * count < size)
    def _():
        row_i = lax.broadcasted_iota(jnp.int32, (count, length, width), 0) + block * count
        row_j = lax.broadcasted_iota(jnp.int32, (count, length, width), 1)
        kept = ((row_i < size) & (row_j < size)).reshape(rows, width)
        left = left_ref[0]
        right = right_ref[0]
        outer = (left[:, None, :] * right[None, :, :]).reshape(rows, width).astype(BF16)
        term = dot(outer, outer_w_ref[...])
        pair_one = pairs_ref[0].reshape(rows, width).astype(F32) + jnp.where(kept, term, 0.0)
        normed, inverse = norm_parts(pair_one)
        gain = gain_ref[...]
        low = (normed * gain).astype(BF16)
        both = dot(low, gate_up_ref[...])
        gate, up = both[:, :hidden], both[:, hidden:]
        act, slope = silu_parts(gate)
        hid = (act * up).astype(BF16)
        pair_two = pair_one + jnp.where(kept, dot(hid, down_ref[...]), 0.0)
        pair_out_ref[0] = pair_two.astype(BF16).reshape(count, length, width)
        cot = cot_ref[0].reshape(rows, width)
        branch_grad = jnp.where(kept, cot, jnp.zeros((), BF16))
        acc_down[...] += dot_tn(branch_grad, hid)
        hid_grad = dot_nt(branch_grad, down_ref[...])
        gate_grad = (hid_grad * up * slope).astype(BF16)
        up_grad = (hid_grad * act).astype(BF16)
        acc_gate_up[:, :hidden] += dot_tn(low, gate_grad)
        acc_gate_up[:, hidden:] += dot_tn(low, up_grad)
        low_grad = dot_nt(gate_grad, gate_up_ref[:, :hidden]) + dot_nt(
            up_grad, gate_up_ref[:, hidden:]
        )
        acc_gain[...] += jnp.sum(low_grad * normed, 0, keepdims=True)
        one_grad = cot.astype(F32) + norm_back(normed, inverse, low_grad * gain)
        pair_grad_ref[0] = one_grad.reshape(count, length, width)
        outer_grad = jnp.where(kept, one_grad, 0.0).astype(BF16)
        acc_outer[...] += dot_tn(outer, outer_grad)
        prod = dot_nt(outer_grad, outer_w_ref[...]).reshape(count, length, width)
        left_grad_ref[0] = jnp.sum(prod * right[None], 1)
        right_grad_ref[0] += jnp.sum(prod * left[:, None, :], 0)

    @pl.when((chain == pl.num_programs(0) - 1) & (block == pl.num_programs(1) - 1))
    def _():
        g_gate_up_ref[...] = acc_gate_up[...].astype(BF16)
        g_down_ref[...] = acc_down[...].astype(BF16)
        g_outer_ref[...] = acc_outer[...].astype(BF16)
        g_gain_ref[...] = acc_gain[...]


def outer_back_kernel(
    lengths_ref,
    left_grad_ref,
    right_grad_ref,
    outer_in_ref,
    weight_ref,
    gain_ref,
    second_out_ref,
    cot_ref,
    branch_ref,
    mod_ref,
    g_weight_ref,
    g_gain_ref,
    second_grad_ref,
    branch_grad_ref,
    gate_pre_ref,
):
    chains, width = mod_ref.shape[0], second_out_ref.shape[1]
    length = second_out_ref.shape[0] // chains
    sides = jnp.concatenate([left_grad_ref[...], right_grad_ref[...]], 1).astype(BF16)
    upstream = dot_nt(sides, weight_ref[...])
    normed, inverse = norm_parts(second_out_ref[...])
    g_gain_ref[...] = jnp.sum(upstream * normed, 0, keepdims=True)
    second_grad_ref[...] = cot_ref[...].astype(F32) + norm_back(
        normed, inverse, upstream * gain_ref[...]
    )
    for c in range(chains):
        rows = slice(c * length, (c + 1) * length)
        keep = keep_of(lengths_ref, c, length)
        gate = mod_ref[c : c + 1, 5 * width : 6 * width]
        grad = keep * second_grad_ref[rows]
        branch_grad_ref[rows] = (gate * grad).astype(BF16)
        gate_pre_ref[c : c + 1] = (
            jnp.sum(branch_ref[rows] * grad, 0, keepdims=True) * gate * (1.0 - gate)
        )
    g_weight_ref[...] = dot_tn(outer_in_ref[...], sides).astype(BF16)


def transition_back_kernel(
    grad_ref, gate_ref, up_ref, weight_ref, gate_grad_ref, up_grad_ref, mine_ref, theirs_ref
):
    part = gate_ref.shape[1]
    half = mine_ref.shape[0]
    hid_grad = dot_nt(grad_ref[...], weight_ref[:, 2 * part :])
    act, slope = silu_parts(gate_ref[...])
    gate_grad = (hid_grad * up_ref[...] * slope).astype(BF16)
    up_grad = (hid_grad * act).astype(BF16)
    gate_grad_ref[...] = gate_grad
    up_grad_ref[...] = up_grad
    total = dot_nt(gate_grad, weight_ref[:, :part]) + dot_nt(up_grad, weight_ref[:, part : 2 * part])
    mine_ref[...] = total[:half]
    theirs_ref[...] = total[half:].astype(BF16)


def transition_grads_kernel(rows_ref, hidden_ref, grad_ref, gate_grad_ref, up_grad_ref, out_ref):
    part = gate_grad_ref.shape[1]
    rows = rows_ref[...]
    out_ref[:, :part] = dot_tn(rows, gate_grad_ref[...]).astype(BF16)
    out_ref[:, part : 2 * part] = dot_tn(rows, up_grad_ref[...]).astype(BF16)
    out_ref[:, 2 * part :] = dot_tn(hidden_ref[...], grad_ref[...]).astype(BF16)


def attention_back_kernel(
    heads,
    lengths_ref,
    own_ref,
    other_ref,
    mod_ref,
    first_out_ref,
    second_grad_ref,
    branch_ref,
    res_ref,
    qkv_ref,
    prob_ref,
    out_w_ref,
    qkv_w_ref,
    branch_grad_ref,
    qkv_grad_ref,
    scores_grad_ref,
    res_grad_ref,
    pre_ref,
    attended_grad,
    first_grad,
):
    chains, length, width = res_ref.shape
    factor = 1.0 / math.sqrt(width // heads)
    mask = head_mask(heads, length, width)
    for c in range(chains):
        rows = slice(c * length, (c + 1) * length)
        keep = keep_of(lengths_ref, c, length)
        upstream = own_ref[rows] + other_ref[rows].astype(F32)
        normed, inverse = norm_parts(first_out_ref[rows])
        pre_ref[c : c + 1, 3 * width : 4 * width] = jnp.sum(upstream * normed, 0, keepdims=True)
        pre_ref[c : c + 1, 4 * width : 5 * width] = jnp.sum(upstream, 0, keepdims=True)
        scale = mod_ref[c : c + 1, 3 * width : 4 * width]
        grad = second_grad_ref[rows] + norm_back(normed, inverse, upstream * (1.0 + scale))
        first_grad[rows] = grad
        gate = mod_ref[c : c + 1, 2 * width : 3 * width]
        kept = keep * grad
        branch_grad_ref[rows] = (gate * kept).astype(BF16)
        pre_ref[c : c + 1, 2 * width : 3 * width] = (
            jnp.sum(branch_ref[rows] * kept, 0, keepdims=True) * gate * (1.0 - gate)
        )
    attended_grad[...] = dot_nt(branch_grad_ref[...], out_w_ref[...]).astype(BF16)
    for c in range(chains):
        rows = slice(c * length, (c + 1) * length)
        queries = spread_heads(qkv_ref[rows, :width], mask, heads)
        keys = qkv_ref[rows, width : 2 * width]
        value_rows = qkv_ref[rows, 2 * width :]
        upstream = spread_heads(attended_grad[rows], mask, heads)
        prob = prob_ref[c]
        prob_grad = dot_nt(upstream, value_rows)
        scores_grad = (
            prob * (prob_grad - jnp.sum(prob_grad * prob, -1, keepdims=True))
        ).astype(BF16)
        scores_grad_ref[c] = scores_grad
        query_grad = fold_heads(dot(scores_grad, keys), mask, heads) * factor
        key_grad = dot_tn(scores_grad, queries) * factor
        value_grad = dot_tn(prob.astype(BF16), upstream)
        qkv_grad_ref[rows, :width] = query_grad.astype(BF16)
        qkv_grad_ref[rows, width : 2 * width] = key_grad.astype(BF16)
        qkv_grad_ref[rows, 2 * width :] = value_grad.astype(BF16)
    first_in_grad = dot_nt(qkv_grad_ref[...], qkv_w_ref[...])
    for c in range(chains):
        rows = slice(c * length, (c + 1) * length)
        upstream = first_in_grad[rows]
        normed, inverse = norm_parts(res_ref[c].astype(F32))
        pre_ref[c : c + 1, :width] = jnp.sum(upstream * normed, 0, keepdims=True)
        pre_ref[c : c + 1, width : 2 * width] = jnp.sum(upstream, 0, keepdims=True)
        scale = mod_ref[c : c + 1, :width]
        res_grad_ref[rows] = first_grad[rows] + norm_back(
            normed, inverse, upstream * (1.0 + scale)
        )


def weight_grad_kernel(in_ref, grad_ref, out_ref):
    out_ref[...] = dot_tn(in_ref[...], grad_ref[...]).astype(BF16)


def pair_last_kernel(
    pairs_ref, one_grad_ref, scores_grad_ref, gain_ref, weight_ref, out_ref, g_weight_ref, g_gain_ref
):
    normed, inverse = norm_parts(pairs_ref[...].astype(F32))
    gain = gain_ref[...]
    low = (normed * gain).astype(BF16)
    scores_grad = scores_grad_ref[...]
    upstream = dot_tn(scores_grad, weight_ref[...])
    out_ref[...] = one_grad_ref[...] + norm_back(normed, inverse, upstream * gain)

    @pl.when(pl.program_id(0) == 0)
    def _():
        g_weight_ref[...] = jnp.zeros_like(g_weight_ref)
        g_gain_ref[...] = jnp.zeros_like(g_gain_ref)

    g_weight_ref[...] += dot(scores_grad, low)
    g_gain_ref[...] += jnp.sum(upstream * normed, 0, keepdims=True)


def on_device(
    n_dp,
    n_f,
    residues,
    pairs,
    lengths,
    time_bins,
    cath_labels,
    residue_cotangent,
    pair_cotangent,
    time_table,
    cath_table,
    attn_modulation,
    attn_gate,
    qkv_weight,
    bias_gain,
    bias_weight,
    out_weight,
    ffn_modulation,
    ffn_gate,
    gate_up,
    down_weight,
    outer_gain,
    outer_weight,
    outer_out,
    pair_gain,
    pair_gate_up,
    pair_down,
):
    place = Place(n_dp, n_f)
    d, f = place.d, place.f
    chains, length, width = residues.shape
    rows = chains * length
    heads = bias_weight.shape[1]
    pair_width = outer_out.shape[1]
    pair_rows = chains * length * length
    time_rows, cath_rows = time_table.shape[0], cath_table.shape[0]
    mod_rows = attn_modulation.shape[0]
    hid_rows = down_weight.shape[0]
    hid_part = hid_rows // 4

    my_gate_up = pl.pallas_call(
        functools.partial(split_kernel, hid_rows, hid_part),
        name="split_gate_up",
        grid=(1,),
        in_specs=[SMEM, whole(gate_up.shape)],
        out_specs=whole((mod_rows, gate_up.shape[1] // 4)),
        out_shape=struct((mod_rows, gate_up.shape[1] // 4), BF16),
        compiler_params=params(),
    )(d.reshape(1).astype(jnp.int32), gate_up)
    my_down = pick(down_weight.reshape(4, hid_part, width), d, 0)
    ffn_weight = lax.all_gather(
        jnp.concatenate([my_gate_up, my_down], 1), "fsdp", axis=0, tiled=True
    )

    small = jnp.concatenate(
        [
            time_bins.astype(F32),
            cath_labels.astype(F32),
            bias_gain.astype(F32),
            pair_gain.astype(F32),
            outer_gain.astype(F32),
            bias_weight.astype(F32).reshape(-1),
        ]
    )
    small = place.sum_f(
        lax.dynamic_update_index_in_dim(jnp.zeros((n_f, small.shape[0]), F32), small, f, 0)
    )
    at = 0

    def take(size):
        nonlocal at
        part = small[:, at : at + size]
        at += size
        return part

    bins = take(chains).reshape(-1).astype(jnp.int32)
    labels = take(chains).reshape(-1).astype(jnp.int32)
    bias_gain_row = take(bias_gain.shape[0]).reshape(1, pair_width)
    pair_gain_row = take(pair_gain.shape[0]).reshape(1, pair_width)
    outer_gain_row = take(outer_gain.shape[0]).reshape(1, width)
    bias_w = take(bias_weight.size).reshape(pair_width, heads)
    bias_w_t = jnp.pad(bias_w.T, ((0, 16 - heads), (0, 0))).astype(BF16)

    quarter = mod_rows // 4
    qkv_q = pick(qkv_weight.reshape(4, quarter, qkv_weight.shape[1]), d, 0)
    qkv_full = place.gather_quarters(qkv_q).reshape(width, qkv_weight.shape[1])

    others = (out_weight, outer_weight, outer_out, pair_gate_up, pair_down)
    quarters = [pick(w.reshape(4, w.shape[0] // 4, w.shape[1]), d, 0) for w in others]
    packed = jnp.concatenate([to_blocks(q) for q in quarters], 0)
    held = place.gather_quarters(packed)
    unpacked, start = [], 0
    for q in quarters:
        count = q.shape[0] * q.shape[1] // 256
        block = from_blocks(held[:, :, start : start + count], *q.shape)
        unpacked.append(block.reshape(-1, q.shape[1]))
        start += count
    out_full, outer_w_full, outer_out_full, pair_gate_up_full, pair_down_full = unpacked

    time_hot = (
        (bins[:, None] - f * time_rows) == jnp.arange(time_rows)[None, :]
    ).astype(BF16)
    cath_hot = (
        (labels[:, None] - f * cath_rows) == jnp.arange(cath_rows)[None, :]
    ).astype(BF16)
    condition = place.sum_f(dot(time_hot, time_table) + dot(cath_hot, cath_table))
    cond_cols = lax.dynamic_slice_in_dim(condition.astype(BF16), f * mod_rows, mod_rows, 1)
    mods = jnp.concatenate(
        [
            dot(cond_cols, w)
            for w in (attn_modulation, attn_gate, ffn_modulation, ffn_gate)
        ],
        1,
    ).astype(BF16)
    mods = mods.reshape(n_f, chains, 6 * width)
    bit = n_f // 2
    while bit >= 1:
        mods = place.halve(
            mods.reshape((2, bit) + mods.shape[1:]),
            0,
            (f // bit) % 2,
            functools.partial(swap, axis="fsdp", size=n_f, bit=bit),
        )
        bit //= 2
    mods = mods.reshape(chains, 6 * width).astype(F32)
    gated = jnp.arange(6 * width)[None, :] // width
    mods = jnp.where((gated == 2) | (gated == 5), jax.nn.sigmoid(mods), mods)

    n_group = n_f * chains
    back_small = jnp.concatenate(
        [bins.astype(F32)[:, None], labels.astype(F32)[:, None], cond_cols.astype(F32)], 1
    )
    back_small = place.gather_bits_d(back_small).reshape(n_dp * n_group, -1)
    bins_all = back_small[:, 0].astype(jnp.int32)
    labels_all = back_small[:, 1].astype(jnp.int32)
    cond_all = back_small[:, 2:].astype(BF16)

    pairs_flat = pairs.reshape(pair_rows, pair_width)
    block = 512
    bias = pl.pallas_call(
        bias_kernel,
        name="pair_bias",
        grid=(pair_rows // block,),
        in_specs=[
            pl.BlockSpec((block, pair_width), lambda i: (i, 0)),
            whole((1, pair_width)),
            whole((16, pair_width)),
        ],
        out_specs=pl.BlockSpec((16, block), lambda i: (0, i)),
        out_shape=struct((16, pair_rows), F32),
        compiler_params=params(),
    )(pairs_flat, bias_gain_row, bias_w_t)
    bias = bias[:heads].reshape(heads, chains, length, length)
    bias = jnp.transpose(bias, (1, 0, 2, 3)).reshape(chains, heads * length, length)
    first_in, qkv, prob, attended, first_branch, first_out, second_in = call_whole(
        functools.partial(attention_kernel, heads),
        "attention",
        [
            struct((rows, width), BF16),
            struct((rows, 3 * width), BF16),
            struct((chains, heads * length, length), F32),
            struct((rows, width), BF16),
            struct((rows, width), F32),
            struct((rows, width), F32),
            struct((rows, width), BF16),
        ],
        lengths,
        residues,
        mods,
        qkv_full,
        out_full,
        bias,
    )

    rows_all = place.rows_gather(second_in)
    part = ffn_weight.shape[1] - width
    part //= 2
    gate, up, hidden, mine, theirs = call_whole(
        transition_kernel,
        "transition",
        [
            struct((4 * rows, part), F32),
            struct((4 * rows, part), F32),
            struct((4 * rows, part), BF16),
            struct((2 * rows, width), F32),
            struct((2 * rows, width), BF16),
        ],
        rows_all,
        ffn_weight,
    )
    branch_own, branch_other = place.rows_reduce(mine, theirs)
    second_branch, second_out, res_out, outer_in, sides = call_whole(
        outer_kernel,
        "outer_sides",
        [
            struct((rows, width), F32),
            struct((rows, width), F32),
            struct((rows, width), BF16),
            struct((rows, width), BF16),
            struct((rows, 2 * pair_width), F32),
        ],
        lengths,
        first_out,
        branch_own,
        branch_other,
        mods,
        outer_gain_row,
        outer_w_full,
    )

    sides = sides.reshape(chains, length, 2 * pair_width)
    count = 8
    pair_hidden = pair_down_full.shape[0]
    pair_block = pl.BlockSpec((1, count, length, pair_width), lambda c, b: (c, b, 0, 0))
    (
        pair_out,
        pair_grad,
        left_grad,
        right_grad,
        g_pair_gate_up,
        g_pair_down_t,
        g_outer_out,
        g_pair_gain,
    ) = pl.pallas_call(
        pair_kernel,
        name="pairs",
        grid=(chains, length // count),
        in_specs=[
            SMEM,
            pl.BlockSpec((1, count, pair_width), lambda c, b: (c, b, 0)),
            pl.BlockSpec((1, length, pair_width), lambda c, b: (c, 0, 1)),
            pair_block,
            pair_block,
            whole((1, pair_width)),
            whole(outer_out_full.shape),
            whole(pair_gate_up_full.shape),
            whole(pair_down_full.shape),
        ],
        out_specs=[
            pair_block,
            pair_block,
            pl.BlockSpec((1, count, pair_width), lambda c, b: (c, b, 0)),
            pl.BlockSpec((1, length, pair_width), lambda c, b: (c, 0, 0)),
            whole(pair_gate_up_full.shape),
            whole((pair_width, pair_hidden)),
            whole(outer_out_full.shape),
            whole((1, pair_width)),
        ],
        out_shape=[
            struct(pairs.shape, BF16),
            struct(pairs.shape, F32),
            struct((chains, length, pair_width), F32),
            struct((chains, length, pair_width), F32),
            struct(pair_gate_up_full.shape, BF16),
            struct((pair_width, pair_hidden), BF16),
            struct(outer_out_full.shape, BF16),
            struct((1, pair_width), F32),
        ],
        scratch_shapes=[
            pltpu.VMEM(pair_gate_up_full.shape, F32),
            pltpu.VMEM((pair_width, pair_hidden), F32),
            pltpu.VMEM(outer_out_full.shape, F32),
            pltpu.VMEM((1, pair_width), F32),
        ],
        compiler_params=params(),
    )(
        lengths,
        sides,
        sides,
        pairs,
        pair_cotangent,
        pair_gain_row,
        outer_out_full,
        pair_gate_up_full,
        pair_down_full,
    )

    g_outer_w, g_outer_gain, second_grad, branch_two_grad, second_pre = call_whole(
        outer_back_kernel,
        "outer_sides_back",
        [
            struct((width, 2 * pair_width), BF16),
            struct((1, width), F32),
            struct((rows, width), F32),
            struct((rows, width), BF16),
            struct((chains, width), F32),
        ],
        lengths,
        left_grad.reshape(rows, pair_width),
        right_grad.reshape(rows, pair_width),
        outer_in,
        outer_w_full,
        outer_gain_row,
        second_out,
        residue_cotangent.reshape(rows, width),
        second_branch,
        mods,
    )

    def by_owner(grad):
        w = grad.shape[1]
        blocks = grad.reshape(n_f, grad.shape[0] // n_f, w // 256, 256)
        return jnp.swapaxes(blocks, 1, 2).reshape(n_f, -1, 256)

    def gain_rows(grad):
        own = grad.reshape(n_f, 1, -1).astype(BF16)
        return jnp.pad(own, ((0, 0), (0, 3), (0, 256 - own.shape[2])))

    pair_terms = [
        by_owner(g_pair_gate_up),
        by_owner(g_pair_down_t.T),
        by_owner(g_outer_out),
        by_owner(g_outer_w),
        gain_rows(g_pair_gain),
        gain_rows(g_outer_gain),
    ]
    pair_sums = place.reduce_all(jnp.concatenate(pair_terms, 1)).astype(F32)
    at = 0

    def take_rows(shape):
        nonlocal at
        n = shape[0] * shape[1] // 256
        piece = from_blocks(pair_sums[at : at + n], *shape)
        at += n
        return piece

    out_pair_gate_up = take_rows(pair_gate_up.shape)
    out_pair_down = take_rows(pair_down.shape)
    out_outer_out = take_rows(outer_out.shape)
    out_outer_w = take_rows(outer_weight.shape)
    out_pair_gain = pair_sums[at, : pair_gain.shape[0]]
    out_outer_gain = pair_sums[at + 4, : outer_gain.shape[0]]

    grads_all = place.rows_gather(branch_two_grad)
    gate_grad, up_grad, mine, theirs = call_whole(
        transition_back_kernel,
        "transition_back",
        [
            struct((4 * rows, part), BF16),
            struct((4 * rows, part), BF16),
            struct((2 * rows, width), F32),
            struct((2 * rows, width), BF16),
        ],
        grads_all,
        gate,
        up,
        ffn_weight,
    )
    own, other = place.rows_reduce(mine, theirs)
    (g_ffn,) = call_whole(
        transition_grads_kernel,
        "transition_grads",
        [struct((width, 2 * part + width), BF16)],
        rows_all,
        hidden,
        grads_all,
        gate_grad,
        up_grad,
    )

    branch_one_grad, qkv_grad, scores_grad, res_grad, pre = pl.pallas_call(
        functools.partial(attention_back_kernel, heads),
        name="attention_back",
        grid=(1,),
        in_specs=[SMEM]
        + [
            whole(a.shape)
            for a in (
                own,
                other,
                mods,
                first_out,
                second_grad,
                first_branch,
                residues,
                qkv,
                prob,
                out_full,
                qkv_full,
            )
        ],
        out_specs=[
            whole((rows, width)),
            whole((rows, 3 * width)),
            whole((chains, heads * length, length)),
            whole((rows, width)),
            whole((chains, 5 * width)),
        ],
        out_shape=[
            struct((rows, width), BF16),
            struct((rows, 3 * width), BF16),
            struct((chains, heads * length, length), BF16),
            struct((rows, width), F32),
            struct((chains, 5 * width), F32),
        ],
        scratch_shapes=[pltpu.VMEM((rows, width), BF16), pltpu.VMEM((rows, width), F32)],
        compiler_params=params(),
    )(
        lengths,
        own,
        other,
        mods,
        first_out,
        second_grad,
        first_branch,
        residues,
        qkv,
        prob,
        out_full,
        qkv_full,
    )
    (g_qkv,) = call_whole(
        weight_grad_kernel, "qkv_grads", [struct((width, 3 * width), BF16)], first_in, qkv_grad
    )
    (g_out,) = call_whole(
        weight_grad_kernel, "out_grads", [struct((width, width), BF16)], attended, branch_one_grad
    )

    pre = jnp.concatenate([pre, second_pre], 1).astype(BF16)
    pre_group = place.gather_bits_f(pre).reshape(n_group, 6 * width)
    mod_weights = (attn_modulation, attn_gate, ffn_modulation, ffn_gate)
    spans, at_col = [], 0
    for w in mod_weights:
        spans.append(slice(at_col, at_col + w.shape[1]))
        at_col += w.shape[1]
    cond_grad = sum(dot_nt(pre_group[:, s], w) for s, w in zip(spans, mod_weights))
    cond_grad = place.gather_bits_f(cond_grad.astype(BF16))
    cond_grad = jnp.transpose(cond_grad, (1, 0, 2)).reshape(n_group, width)
    cond_grad = place.gather_bits_d(cond_grad).reshape(n_dp * n_group, width)
    pre_all = place.gather_bits_d(pre_group).reshape(n_dp * n_group, 6 * width)
    g_mods = dot_tn(cond_all, pre_all)
    time_all = (
        (bins_all[:, None] - f * time_rows) == jnp.arange(time_rows)[None, :]
    ).astype(BF16)
    cath_all = (
        (labels_all[:, None] - f * cath_rows) == jnp.arange(cath_rows)[None, :]
    ).astype(BF16)
    out_time = dot_tn(time_all, cond_grad)
    out_cath = dot_tn(cath_all, cond_grad)

    attn_sums = place.reduce_all(
        jnp.concatenate([g_qkv, g_out], 1).reshape(n_f, mod_rows, 4 * width)
    ).astype(F32)
    out_qkv = attn_sums[:, : 3 * width]
    out_out = attn_sums[:, 3 * width :]

    ffn_sums = place.spread_d(place.reduce_f(g_ffn.reshape(n_f, mod_rows, 2 * part + width)))
    (out_gate_up,) = call_whole(
        functools.partial(join_kernel, hid_rows, hid_part),
        "join_gate_up",
        [struct(gate_up.shape, F32)],
        ffn_sums[:, :, : 2 * part],
    )
    out_down = ffn_sums[:, :, 2 * part :].astype(F32).reshape(hid_rows, width)

    scores_t = jnp.transpose(
        scores_grad.reshape(chains, heads, length, length), (1, 0, 2, 3)
    ).reshape(heads, pair_rows)
    scores_t = jnp.pad(scores_t, ((0, 16 - heads), (0, 0)))
    pairs_grad, g_bias_w, g_bias_gain = pl.pallas_call(
        pair_last_kernel,
        name="pairs_last",
        grid=(pair_rows // block,),
        in_specs=[
            pl.BlockSpec((block, pair_width), lambda i: (i, 0)),
            pl.BlockSpec((block, pair_width), lambda i: (i, 0)),
            pl.BlockSpec((16, block), lambda i: (0, i)),
            whole((1, pair_width)),
            whole((16, pair_width)),
        ],
        out_specs=[
            pl.BlockSpec((block, pair_width), lambda i: (i, 0)),
            whole((16, pair_width)),
            whole((1, pair_width)),
        ],
        out_shape=[
            struct((pair_rows, pair_width), F32),
            struct((16, pair_width), F32),
            struct((1, pair_width), F32),
        ],
        compiler_params=params(),
    )(pairs_flat, pair_grad.reshape(pair_rows, pair_width), scores_t, bias_gain_row, bias_w_t)

    bias_terms = jnp.concatenate([g_bias_w[:heads], g_bias_gain], 0)
    for axis, size in (("dp", n_dp), ("fsdp", n_f)):
        bit = 1
        while bit < size:
            bias_terms = bias_terms + swap(bias_terms, axis, size, bit)
            bit *= 2
    bias_rows = bias_weight.shape[0]
    mine = lax.dynamic_slice_in_dim(bias_terms, f * bias_rows, bias_rows, 1)
    out_bias_w = mine[:heads].T
    out_bias_gain = mine[heads]

    return (
        res_out.reshape(residues.shape),
        pair_out,
        res_grad.reshape(residues.shape),
        pairs_grad.reshape(pairs.shape),
        out_time,
        out_cath,
        g_mods[:, spans[0]],
        g_mods[:, spans[1]],
        out_qkv,
        out_bias_gain,
        out_bias_w,
        out_out,
        g_mods[:, spans[2]],
        g_mods[:, spans[3]],
        out_gate_up,
        out_down,
        out_outer_gain,
        out_outer_w,
        out_outer_out,
        out_pair_gain,
        out_pair_gate_up,
        out_pair_down,
    )


def solution(mesh):
    chains3 = P(("dp", "fsdp"), None, None)
    chains4 = P(("dp", "fsdp"), None, None, None)
    chains1 = P(("dp", "fsdp"))
    table = P("fsdp", None)
    line = P("fsdp")
    weights = (
        table,
        table,
        table,
        table,
        table,
        line,
        table,
        table,
        table,
        table,
        table,
        table,
        line,
        table,
        table,
        line,
        table,
        table,
    )
    return jax.shard_map(
        functools.partial(on_device, mesh.shape["dp"], mesh.shape["fsdp"]),
        mesh=mesh,
        in_specs=(chains3, chains4, chains1, chains1, chains1, chains3, chains4) + weights,
        out_specs=(chains3, chains4, chains3, chains4) + weights,
        check_vma=False,
    )
```

```python
import functools
import math

import jax
import jax.numpy as jnp
from jax import lax
from jax.experimental import pallas as pl
from jax.experimental.pallas import tpu as pltpu
from jax.sharding import PartitionSpec as P

EPSILON = 1e-05
F32 = jnp.float32
BF16 = jnp.bfloat16
VMEM_LIMIT = 56 * 1024 * 1024


def norm_parts(values):
    center = values - jnp.mean(values, -1, keepdims=True)
    inverse = lax.rsqrt(jnp.mean(center * center, -1, keepdims=True) + EPSILON)
    return center * inverse, inverse


def norm_back(normed, inverse, upstream):
    return inverse * (
        upstream
        - jnp.mean(upstream, -1, keepdims=True)
        - normed * jnp.mean(upstream * normed, -1, keepdims=True)
    )


def dot(left, right):
    return jnp.dot(left, right, preferred_element_type=F32)


def dot_nt(left, right):
    return lax.dot_general(left, right, (((1,), (1,)), ((), ())), preferred_element_type=F32)


def dot_tn(left, right):
    return lax.dot_general(left, right, (((0,), (0,)), ((), ())), preferred_element_type=F32)


def params():
    return pltpu.CompilerParams(vmem_limit_bytes=VMEM_LIMIT)


def cost(micros):
    return pl.CostEstimate(flops=int(micros * 1e9), bytes_accessed=0, transcendentals=0)


def whole(shape):
    return pl.BlockSpec(shape, lambda *_: (0,) * len(shape))


SMEM = pl.BlockSpec(memory_space=pltpu.SMEM)


def call_whole(kernel, name, micros, outs, *operands, blocks=None, scratch=()):
    blocks = blocks or {}
    specs = [
        blocks.get(i, SMEM if a.dtype == jnp.int32 else whole(a.shape))
        for i, a in enumerate(operands)
    ]
    return pl.pallas_call(
        kernel,
        grid=(1,),
        name=name,
        in_specs=specs,
        out_specs=[whole(o.shape) for o in outs],
        out_shape=outs,
        scratch_shapes=list(scratch),
        cost_estimate=cost(micros),
        compiler_params=params(),
    )(*operands)


def struct(shape, dtype):
    return jax.ShapeDtypeStruct(shape, dtype)


def swap(values, axis, size, bit):
    return lax.ppermute(values, axis, [(i, i ^ bit) for i in range(size)])


def pick(values, index, axis):
    return lax.dynamic_index_in_dim(values, index, axis, keepdims=False)


def ordered(bit, own, other, axis):
    first = jnp.where(bit == 0, own, other)
    second = jnp.where(bit == 0, other, own)
    return jnp.stack([first, second], axis)


class Place:
    def __init__(self, n_dp, n_f):
        self.n_dp, self.n_f, self.ring = n_dp, n_f, n_f // 2
        self.d = lax.axis_index("dp")
        self.f = lax.axis_index("fsdp")
        self.core, self.x = self.d % 2, self.d // 2
        self.y, self.r = self.f % 2, self.f // 2
        self.ints = jnp.stack([self.d, self.f]).astype(jnp.int32)

    def swap_core(self, values):
        return swap(values, "dp", self.n_dp, 1)

    def swap_x(self, values):
        return swap(values, "dp", self.n_dp, 2)

    def swap_y(self, values):
        return swap(values, "fsdp", self.n_f, 1)

    def shift_ring(self, values):
        return lax.ppermute(
            values, "fsdp", [(i, (i + 2) % self.n_f) for i in range(self.n_f)]
        )

    def to_each_f(self, values):
        return lax.all_to_all(values, "fsdp", split_axis=0, concat_axis=0, tiled=True)

    def to_all_f(self, values):
        return self.to_each_f(jnp.broadcast_to(values[None], (self.n_f,) + values.shape))


    def gather_f(self, shard):
        ring = self.ring
        pieces, moving = [], shard
        for k in range(ring):
            moves = [(self.swap_y, moving)]
            if k < ring - 1:
                moves.append((self.shift_ring, moving))
            got = yield moves
            pieces += [moving, got[0]]
            if k < ring - 1:
                moving = got[1]
        return self.assemble(pieces, 2)

    def gather_all(self, shard):
        ring = self.ring
        rows, width = shard.shape
        halves = lax.dynamic_slice_in_dim(shard, self.core * (width // 2), width // 2, 1)
        halves = halves.reshape(2, rows // 2, width // 2)
        moving, last, pieces = pick(halves, self.x, 0), None, []
        for k in range(ring + 1):
            moves = []
            if k < ring:
                moves.append((self.swap_y, moving))
            if k < ring - 1:
                moves.append((self.shift_ring, moving))
            if k > 0:
                moves.append((self.swap_x, last[1] if k == 1 else jnp.stack(last)))
            got = yield moves
            if k > 0:
                pieces += last
                pieces += [pick(halves, 1 - self.x, 0), got[-1]] if k == 1 else [got[-1]]
            if k < ring:
                last = [moving, got[0]]
            if k < ring - 1:
                moving = got[1]
        held = self.assemble(pieces, 4).reshape(self.n_f * rows, width // 2)
        (other,) = yield [(self.swap_core, held)]
        return held, other

    def assemble(self, pieces, per_step):
        block = pieces[0].shape
        lead = (self.ring, 2) if per_step == 2 else (self.ring, 2, 2)
        (held,) = call_whole(
            functools.partial(assemble_kernel, self.ring, per_step),
            "assemble",
            3.0,
            [struct(lead + block, pieces[0].dtype)],
            self.ints,
            *pieces,
        )
        return held.reshape((self.n_f,) + lead[2:] + block)

    def add(self, keep, got):
        return (keep.astype(F32) + got.astype(F32)).astype(BF16)

    def chunks(self, values):
        give, keep = [], []
        values = values.reshape((self.ring, 2) + values.shape[1:])
        for k in range(self.ring):
            chunk = pick(values, (self.r - 1 - k) % self.ring, 0)
            give.append(pick(chunk, 1 - self.y, 0))
            keep.append(pick(chunk, self.y, 0))
        return give, keep

    def reduce_f(self, give, keep):
        moving = None
        for k in range(self.ring):
            moves = [(self.swap_y, give[k])]
            if k > 0:
                moves.append((self.shift_ring, moving))
            got = yield moves
            total = keep[k].astype(F32)
            for other in got:
                total = total + other.astype(F32)
            moving = total.astype(BF16)
        return (yield from self.spread_d(moving))

    def reduce_x(self, mine, across):
        ring = self.ring
        got = yield [
            (self.swap_x, self.add(pick(mine, 1 - self.x, 1), pick(across, 1 - self.x, 1)))
        ]
        values = (
            pick(mine, self.x, 1).astype(F32)
            + pick(across, self.x, 1).astype(F32)
            + got[0].astype(F32)
        ).astype(BF16)
        values = values.reshape((ring, 2) + values.shape[1:])
        got = yield [(self.swap_y, pick(values, 1 - self.y, 1))]
        values = self.add(pick(values, self.y, 1), got[0])
        moving = pick(values, (self.r - 1) % ring, 0)
        for k in range(1, ring):
            got = yield [(self.shift_ring, moving)]
            moving = self.add(pick(values, (self.r - 1 - k) % ring, 0), got[0])
        return (yield from self.spread_d(moving))

    def spread_d(self, values):
        other, across = yield [(self.swap_x, values), (self.swap_core, values)]
        (both,) = yield [(self.swap_core, other)]
        return values, across, other, both

    def sum_everywhere(self, values):
        for axis, size in (("dp", self.n_dp), ("fsdp", self.n_f)):
            bit = 1
            while bit < size:
                (other,) = yield [(functools.partial(swap, axis=axis, size=size, bit=bit), values)]
                values = values + other
                bit *= 2
        return values


class Chain:
    def __init__(self, moves):
        self.moves, self.result, self.done = moves, None, False
        self.pending = self.advance(None)

    def advance(self, got):
        try:
            return self.moves.send(got)
        except StopIteration as stop:
            self.result, self.done = stop.value, True
            return []


class Slots:
    def __init__(self):
        self.chains, self.token = [], None

    def add(self, moves):
        chain = Chain(moves)
        self.chains.append(chain)
        return chain

    def step(self, *extra):
        moves = list(extra)
        for chain in self.chains:
            moves += chain.pending
        values = tuple(value for _, value in moves)
        if self.token is not None:
            values = lax.optimization_barrier((values, self.token))[0]
        got = [move(value) for (move, _), value in zip(moves, values)]
        got = lax.optimization_barrier(tuple(got))
        self.token = got[0]
        at = len(extra)
        for chain in self.chains:
            count = len(chain.pending)
            chain.pending = chain.advance(list(got[at : at + count]))
            at += count
        self.chains = [chain for chain in self.chains if not chain.done]
        return got[: len(extra)]

    def finish(self, *chains):
        while not all(chain.done for chain in chains):
            self.step()
        return [chain.result for chain in chains]


def choose_matrix(group, part, member):
    row = lax.broadcasted_iota(jnp.int32, (1536, 1), 0)
    col = lax.broadcasted_iota(jnp.int32, (1, 384), 1)
    want = (col // part) * group + member * part + col % part
    return jnp.where(row == want, 1.0, 0.0).astype(BF16)


def assemble_kernel(ring, per_step, place_ref, *refs):
    pieces, out_ref = list(refs[:-1]), refs[-1]
    x, y, r = place_ref[0] // 2, place_ref[1] % 2, place_ref[1] // 2
    for k in range(ring):
        at = lax.rem(r - k + ring, ring)
        own, other = pieces.pop(0), pieces.pop(0)
        if per_step == 2:
            out_ref[at, y] = own[...]
            out_ref[at, 1 - y] = other[...]
            continue
        out_ref[at, y, x] = own[...]
        out_ref[at, 1 - y, x] = other[...]
        if k == 0:
            out_ref[at, y, 1 - x] = pieces.pop(0)[...]
            out_ref[at, 1 - y, 1 - x] = pieces.pop(0)[...]
        else:
            both = pieces.pop(0)
            out_ref[at, y, 1 - x] = both[0]
            out_ref[at, 1 - y, 1 - x] = both[1]


def emit_chunks(place_ref, values_ref, give_refs, keep_refs):
    ring = len(give_refs)
    y, r = place_ref[1] % 2, place_ref[1] // 2
    for k in range(ring):
        at = 2 * lax.rem(r - 1 - k + 2 * ring, ring)
        give_refs[k][...] = values_ref[at + 1 - y]
        keep_refs[k][...] = values_ref[at + y]


def split_kernel(group, part, place_ref, full_ref, out_ref):
    choose = choose_matrix(group, part, place_ref[0])
    for chunk in range(full_ref.shape[1] // 1536):
        out_ref[:, chunk * 384 : chunk * 384 + 384] = dot(
            full_ref[:, chunk * 1536 : chunk * 1536 + 1536], choose
        ).astype(BF16)


def finish_kernel(group, part, place_ref, *refs):
    ffn, attn, pair = refs[0:4], refs[4:8], refs[8:12]
    gate_up_ref, down_ref, qkv_ref, out_ref, outer_w_ref = refs[12:17]
    pair_gate_up_ref, outer_out_ref, pair_down_ref = refs[17:20]
    ffn_all, attn_all, pair_all = refs[20:23]
    d = place_ref[0]
    for pieces, held in ((ffn, ffn_all), (attn, attn_all), (pair, pair_all)):
        for distance in range(4):
            member = d + (1 - 2 * (d % 2)) * (distance % 2)
            member = member + (2 - 4 * (d // 2)) * (distance // 2)
            held[member] = pieces[distance][...]
    width = out_ref.shape[1]
    side = outer_w_ref.shape[1] // 4
    count = down_ref.shape[0] // 4
    quarter = gate_up_ref.shape[1] // 4
    for m in range(4):
        if m < 3:
            qkv_ref[:, m * width : (m + 1) * width] = attn_all[m][:, :width].astype(F32)
        else:
            out_ref[...] = attn_all[m][:, :width].astype(F32)
        outer_w_ref[:, m * side : (m + 1) * side] = attn_all[m][:, width:].astype(F32)
        down_ref[m * count : (m + 1) * count] = ffn_all[m][:, quarter:].astype(F32)
        choose = choose_matrix(group, part, m)
        for chunk in range(quarter // 384):
            span = slice(chunk * 1536, chunk * 1536 + 1536)
            term = dot_nt(ffn_all[m][:, chunk * 384 : chunk * 384 + 384], choose)
            if m == 0:
                gate_up_ref[:, span] = term
            else:
                gate_up_ref[:, span] += term
    half = pair_all.shape[1]
    hidden2, pair_width = pair_gate_up_ref.shape[1], outer_out_ref.shape[1]
    for x in range(2):
        rows = slice(x * half, (x + 1) * half)
        wide = jnp.concatenate([pair_all[2 * x], pair_all[2 * x + 1]], 1).astype(F32)
        pair_gate_up_ref[rows] = wide[:, :hidden2]
        outer_out_ref[rows] = wide[:, hidden2 : hidden2 + pair_width]
        for block in range(4):
            start = hidden2 + (1 + block) * pair_width
            place = 2 * half * block + x * half
            pair_down_ref[place : place + half] = wide[:, start : start + pair_width]


def bias_kernel(pairs_ref, gain_ref, weight_ref, out_ref):
    normed, _ = norm_parts(pairs_ref[...].astype(F32))
    low = (normed * gain_ref[...]).astype(BF16)
    out_ref[...] = dot_nt(weight_ref[...], low)


def head_mask(heads, length, width):
    row = lax.broadcasted_iota(jnp.int32, (heads * length, 1), 0) // length
    col = lax.broadcasted_iota(jnp.int32, (1, width), 1) // (width // heads)
    return row == col


def spread_heads(rows, mask, heads):
    return jnp.where(mask, jnp.concatenate([rows] * heads, 0), jnp.zeros((), rows.dtype))


def fold_heads(wide, mask, heads):
    kept = jnp.where(mask, wide, 0.0)
    return jnp.sum(kept.reshape(heads, wide.shape[0] // heads, wide.shape[1]), 0)


def keep_of(lengths_ref, chain, length):
    row = lax.broadcasted_iota(jnp.int32, (length, 1), 0)
    return (row < lengths_ref[chain]).astype(F32)


def attention_kernel(
    heads,
    lengths_ref,
    place_ref,
    res_ref,
    mod_ref,
    own_w_ref,
    other_w_ref,
    bias_ref,
    first_in_ref,
    qkv_ref,
    prob_ref,
    attended_ref,
    branch_ref,
    first_out_ref,
    second_in_ref,
    by_half,
):
    chains, length, width = res_ref.shape
    core = place_ref[0] % 2
    factor = 1.0 / math.sqrt(width // heads)
    mask = head_mask(heads, length, width)
    for c in range(chains):
        rows = slice(c * length, (c + 1) * length)
        normed, _ = norm_parts(res_ref[c].astype(F32))
        scale = mod_ref[c : c + 1, :width]
        shift = mod_ref[c : c + 1, width : 2 * width]
        first_in_ref[rows] = (normed * (1.0 + scale) + shift).astype(BF16)
    by_half[core] = dot(first_in_ref[...], own_w_ref[...])
    by_half[1 - core] = dot(first_in_ref[...], other_w_ref[...])
    qkv_ref[:, : 2 * width] = by_half[0].astype(BF16)
    qkv_ref[:, 2 * width :] = by_half[1][:, :width].astype(BF16)
    for c in range(chains):
        rows = slice(c * length, (c + 1) * length)
        queries = spread_heads(qkv_ref[rows, :width], mask, heads)
        keys = qkv_ref[rows, width : 2 * width]
        value_rows = qkv_ref[rows, 2 * width :]
        scores = dot_nt(queries, keys) * factor + bias_ref[c]
        column = lax.broadcasted_iota(jnp.int32, scores.shape, 1)
        scores = jnp.where(column < lengths_ref[c], scores, -1000000000.0)
        exps = jnp.exp(scores - jnp.max(scores, -1, keepdims=True))
        prob = exps / jnp.sum(exps, -1, keepdims=True)
        prob_ref[c] = prob
        wide = dot(prob.astype(BF16), value_rows)
        attended_ref[rows] = fold_heads(wide, mask, heads).astype(BF16)
    by_half[core, :, :width] = dot(attended_ref[...], own_w_ref[:, width:])
    by_half[1 - core, :, :width] = dot(attended_ref[...], other_w_ref[:, width:])
    branch_ref[...] = by_half[1, :, :width]
    for c in range(chains):
        rows = slice(c * length, (c + 1) * length)
        keep = keep_of(lengths_ref, c, length)
        gate = mod_ref[c : c + 1, 2 * width : 3 * width]
        first_out = res_ref[c].astype(F32) + keep * gate * branch_ref[rows]
        first_out_ref[rows] = first_out
        normed, _ = norm_parts(first_out)
        scale = mod_ref[c : c + 1, 3 * width : 4 * width]
        shift = mod_ref[c : c + 1, 4 * width : 5 * width]
        second_in_ref[rows] = (normed * (1.0 + scale) + shift).astype(BF16)


def emit_members(place_ref, blocks, keep_ref, give_ref):
    for m, block in enumerate(blocks):

        @pl.when(place_ref[0] // 2 == m // 2)
        def _(m=m, block=block):
            keep_ref[m % 2] = block

        @pl.when(place_ref[0] // 2 != m // 2)
        def _(m=m, block=block):
            give_ref[m % 2] = block


def silu_parts(gate):
    logistic = jax.nn.sigmoid(gate)
    act = gate * logistic
    return act, logistic + act * (1.0 - logistic)


def transition_kernel(
    own_ref,
    other_ref,
    across_ref,
    weight_ref,
    rows_ref,
    gate_ref,
    up_ref,
    hidden_ref,
    mine_ref,
    theirs_ref,
):
    count, width = own_ref.shape
    part = gate_ref.shape[1]
    rows_ref[:count] = own_ref[...]
    rows_ref[count : 2 * count] = other_ref[...]
    rows_ref[2 * count :] = across_ref[...]
    rows = rows_ref[...]
    gate = dot(rows, weight_ref[:, :part])
    up = dot(rows, weight_ref[:, part : 2 * part])
    gate_ref[...] = gate
    up_ref[...] = up
    hidden = (gate * jax.nn.sigmoid(gate) * up).astype(BF16)
    hidden_ref[...] = hidden
    down = weight_ref[:, 2 * part :]
    mine_ref[...] = dot(hidden[: 2 * count], down)
    theirs_ref[...] = dot(hidden[2 * count :], down).astype(BF16)


def outer_kernel(
    lengths_ref,
    first_out_ref,
    branch_own_ref,
    branch_other_ref,
    mod_ref,
    gain_ref,
    weight_ref,
    branch_ref,
    second_out_ref,
    res_out_ref,
    outer_in_ref,
    sides_ref,
):
    chains, width = mod_ref.shape[0], first_out_ref.shape[1]
    length = first_out_ref.shape[0] // chains
    branch = branch_own_ref[...] + branch_other_ref[...].astype(F32)
    branch_ref[...] = branch
    for c in range(chains):
        rows = slice(c * length, (c + 1) * length)
        keep = keep_of(lengths_ref, c, length)
        gate = mod_ref[c : c + 1, 5 * width : 6 * width]
        second_out_ref[rows] = first_out_ref[rows] + keep * gate * branch[rows]
    second_out = second_out_ref[...]
    res_out_ref[...] = second_out.astype(BF16)
    normed, _ = norm_parts(second_out)
    outer_in_ref[...] = (normed * gain_ref[...]).astype(BF16)
    sides_ref[...] = dot(outer_in_ref[...], weight_ref[...])


def pair_kernel(
    owners,
    lengths_ref,
    place_ref,
    left_ref,
    right_ref,
    pairs_ref,
    cot_ref,
    gain_ref,
    outer_w_ref,
    gate_up_ref,
    down_ref,
    pair_out_ref,
    pair_grad_ref,
    left_grad_ref,
    right_grad_ref,
    keep_ref,
    give_ref,
    g_gain_ref,
    acc_gate_up,
    acc_down,
    acc_outer,
    acc_gain,
):
    chain, block = pl.program_id(0), pl.program_id(1)
    _, count, length, width = pairs_ref.shape
    rows = count * length
    hidden = down_ref.shape[0]
    size = lengths_ref[chain]

    @pl.when((chain == 0) & (block == 0))
    def _():
        acc_gate_up[...] = jnp.zeros_like(acc_gate_up)
        acc_down[...] = jnp.zeros_like(acc_down)
        acc_outer[...] = jnp.zeros_like(acc_outer)
        acc_gain[...] = jnp.zeros_like(acc_gain)

    @pl.when(block == 0)
    def _():
        right_grad_ref[...] = jnp.zeros_like(right_grad_ref)

    @pl.when(block * count >= size)
    def _():
        pair_out_ref[...] = pairs_ref[...]
        pair_grad_ref[...] = cot_ref[...].astype(F32)
        left_grad_ref[...] = jnp.zeros_like(left_grad_ref)

    @pl.when(block * count < size)
    def _():
        row_i = lax.broadcasted_iota(jnp.int32, (count, length, width), 0) + block * count
        row_j = lax.broadcasted_iota(jnp.int32, (count, length, width), 1)
        kept = ((row_i < size) & (row_j < size)).reshape(rows, width)
        left = left_ref[0]
        right = right_ref[0]
        outer = (left[:, None, :] * right[None, :, :]).reshape(rows, width).astype(BF16)
        term = dot(outer, outer_w_ref[...])
        pair_one = pairs_ref[0].reshape(rows, width).astype(F32) + jnp.where(kept, term, 0.0)
        normed, inverse = norm_parts(pair_one)
        gain = gain_ref[...]
        low = (normed * gain).astype(BF16)
        both = dot(low, gate_up_ref[...])
        gate, up = both[:, :hidden], both[:, hidden:]
        act, slope = silu_parts(gate)
        hid = (act * up).astype(BF16)
        pair_two = pair_one + jnp.where(kept, dot(hid, down_ref[...]), 0.0)
        pair_out_ref[0] = pair_two.astype(BF16).reshape(count, length, width)
        cot = cot_ref[0].reshape(rows, width)
        branch_grad = jnp.where(kept, cot, jnp.zeros((), BF16))
        acc_down[...] += dot_tn(branch_grad, hid)
        hid_grad = dot_nt(branch_grad, down_ref[...])
        gate_grad = (hid_grad * up * slope).astype(BF16)
        up_grad = (hid_grad * act).astype(BF16)
        acc_gate_up[:, :hidden] += dot_tn(low, gate_grad)
        acc_gate_up[:, hidden:] += dot_tn(low, up_grad)
        low_grad = dot_nt(gate_grad, gate_up_ref[:, :hidden]) + dot_nt(
            up_grad, gate_up_ref[:, hidden:]
        )
        acc_gain[...] += jnp.sum(low_grad * normed, 0, keepdims=True)
        one_grad = cot.astype(F32) + norm_back(normed, inverse, low_grad * gain)
        pair_grad_ref[0] = one_grad.reshape(count, length, width)
        outer_grad = jnp.where(kept, one_grad, 0.0).astype(BF16)
        acc_outer[...] += dot_tn(outer, outer_grad)
        prod = dot_nt(outer_grad, outer_w_ref[...]).reshape(count, length, width)
        left_grad_ref[0] = jnp.sum(prod * right[None], 1)
        right_grad_ref[0] += jnp.sum(prod * left[:, None, :], 0)

    @pl.when((chain == pl.num_programs(0) - 1) & (block == pl.num_programs(1) - 1))
    def _():
        down = acc_down[...].T.astype(BF16)
        down = down.reshape(owners, 4, hidden // (4 * owners), width)
        down = [down[:, i].reshape(hidden // 4, width) for i in range(4)]
        wide = [acc_gate_up[...].astype(BF16), acc_outer[...].astype(BF16)] + down
        wide = jnp.concatenate(wide, 1)
        half = wide.shape[1] // 2

        @pl.when(place_ref[0] % 2 == 0)
        def _():
            keep_ref[...] = wide[:, :half]
            give_ref[...] = wide[:, half:]

        @pl.when(place_ref[0] % 2 == 1)
        def _():
            keep_ref[...] = wide[:, half:]
            give_ref[...] = wide[:, :half]

        g_gain_ref[...] = acc_gain[...]


def outer_back_kernel(
    lengths_ref,
    place_ref,
    left_grad_ref,
    right_grad_ref,
    weight_ref,
    gain_ref,
    second_out_ref,
    cot_ref,
    branch_ref,
    mod_ref,
    keep_ref,
    give_ref,
    g_gain_ref,
    second_grad_ref,
    branch_grad_ref,
    gate_pre_ref,
):
    chains, width = mod_ref.shape[0], second_out_ref.shape[1]
    length = second_out_ref.shape[0] // chains
    sides = jnp.concatenate([left_grad_ref[...], right_grad_ref[...]], 1).astype(BF16)
    upstream = dot_nt(sides, weight_ref[...])
    normed, inverse = norm_parts(second_out_ref[...])
    g_gain_ref[...] = jnp.sum(upstream * normed, 0, keepdims=True)
    second_grad_ref[...] = cot_ref[...].astype(F32) + norm_back(
        normed, inverse, upstream * gain_ref[...]
    )
    for c in range(chains):
        rows = slice(c * length, (c + 1) * length)
        keep = keep_of(lengths_ref, c, length)
        gate = mod_ref[c : c + 1, 5 * width : 6 * width]
        grad = keep * second_grad_ref[rows]
        branch_grad_ref[rows] = (gate * grad).astype(BF16)
        gate_pre_ref[c : c + 1] = (
            jnp.sum(branch_ref[rows] * grad, 0, keepdims=True) * gate * (1.0 - gate)
        )
    span = sides.shape[1] // 4
    emit_members(place_ref, [sides[:, m * span : (m + 1) * span] for m in range(4)], keep_ref, give_ref)


def transition_back_kernel(
    own_ref,
    other_ref,
    across_ref,
    gate_ref,
    up_ref,
    weight_ref,
    grads_ref,
    gate_grad_ref,
    up_grad_ref,
    mine_ref,
    theirs_ref,
):
    count = own_ref.shape[0]
    part = gate_ref.shape[1]
    grads_ref[:count] = own_ref[...]
    grads_ref[count : 2 * count] = other_ref[...]
    grads_ref[2 * count :] = across_ref[...]
    hid_grad = dot_nt(grads_ref[...], weight_ref[:, 2 * part :])
    act, slope = silu_parts(gate_ref[...])
    gate_grad = (hid_grad * up_ref[...] * slope).astype(BF16)
    up_grad = (hid_grad * act).astype(BF16)
    gate_grad_ref[...] = gate_grad
    up_grad_ref[...] = up_grad
    total = dot_nt(gate_grad, weight_ref[:, :part]) + dot_nt(
        up_grad, weight_ref[:, part : 2 * part]
    )
    mine_ref[...] = total[: 2 * count]
    theirs_ref[...] = total[2 * count :].astype(BF16)


def transition_grads_kernel(
    place_ref, rows_ref, hidden_ref, grads_ref, gate_grad_ref, up_grad_ref, *refs
):
    *out_refs, total = refs
    part = gate_grad_ref.shape[1]
    blocks = total.shape[:2] + (part,)
    rows = rows_ref[...]
    total[:, :, :part] = dot_tn(rows, gate_grad_ref[...]).astype(BF16).reshape(blocks)
    total[:, :, part : 2 * part] = dot_tn(rows, up_grad_ref[...]).astype(BF16).reshape(blocks)
    total[:, :, 2 * part :] = dot_tn(hidden_ref[...], grads_ref[...]).astype(BF16).reshape(blocks)
    emit_chunks(place_ref, total, out_refs[: len(out_refs) // 2], out_refs[len(out_refs) // 2 :])


def attention_back_kernel(
    heads,
    lengths_ref,
    place_ref,
    own_ref,
    other_ref,
    mod_ref,
    first_out_ref,
    second_grad_ref,
    branch_ref,
    res_ref,
    qkv_ref,
    prob_ref,
    own_w_ref,
    other_w_ref,
    keep_ref,
    give_ref,
    scores_grad_ref,
    res_grad_ref,
    pre_ref,
    attended_grad,
    first_grad,
    branch_grad_ref,
    qkv_grad_ref,
    by_half,
):
    chains, length, width = res_ref.shape
    core = place_ref[0] % 2
    factor = 1.0 / math.sqrt(width // heads)
    mask = head_mask(heads, length, width)
    for c in range(chains):
        rows = slice(c * length, (c + 1) * length)
        keep = keep_of(lengths_ref, c, length)
        upstream = own_ref[rows] + other_ref[rows].astype(F32)
        normed, inverse = norm_parts(first_out_ref[rows])
        pre_ref[c : c + 1, 3 * width : 4 * width] = jnp.sum(upstream * normed, 0, keepdims=True)
        pre_ref[c : c + 1, 4 * width : 5 * width] = jnp.sum(upstream, 0, keepdims=True)
        scale = mod_ref[c : c + 1, 3 * width : 4 * width]
        grad = second_grad_ref[rows] + norm_back(normed, inverse, upstream * (1.0 + scale))
        first_grad[rows] = grad
        gate = mod_ref[c : c + 1, 2 * width : 3 * width]
        kept = keep * grad
        branch_grad_ref[rows] = (gate * kept).astype(BF16)
        pre_ref[c : c + 1, 2 * width : 3 * width] = (
            jnp.sum(branch_ref[rows] * kept, 0, keepdims=True) * gate * (1.0 - gate)
        )
    by_half[core] = dot_nt(branch_grad_ref[...], own_w_ref[:, width:]).astype(BF16)
    by_half[1 - core] = dot_nt(branch_grad_ref[...], other_w_ref[:, width:]).astype(BF16)
    attended_grad[...] = by_half[1]
    for c in range(chains):
        rows = slice(c * length, (c + 1) * length)
        queries = spread_heads(qkv_ref[rows, :width], mask, heads)
        keys = qkv_ref[rows, width : 2 * width]
        value_rows = qkv_ref[rows, 2 * width :]
        upstream = spread_heads(attended_grad[rows], mask, heads)
        prob = prob_ref[c]
        prob_grad = dot_nt(upstream, value_rows)
        scores_grad = (
            prob * (prob_grad - jnp.sum(prob_grad * prob, -1, keepdims=True))
        ).astype(BF16)
        scores_grad_ref[c] = scores_grad
        query_grad = fold_heads(dot(scores_grad, keys), mask, heads) * factor
        key_grad = dot_tn(scores_grad, queries) * factor
        value_grad = dot_tn(prob.astype(BF16), upstream)
        qkv_grad_ref[0, rows, :width] = query_grad.astype(BF16)
        qkv_grad_ref[0, rows, width:] = key_grad.astype(BF16)
        qkv_grad_ref[1, rows, :width] = value_grad.astype(BF16)
    blocks = [
        qkv_grad_ref[0, :, :width],
        qkv_grad_ref[0, :, width:],
        qkv_grad_ref[1, :, :width],
        branch_grad_ref[...],
    ]
    emit_members(place_ref, blocks, keep_ref, give_ref)
    qkv_grad_ref[1, :, width:] = jnp.zeros((chains * length, width), BF16)
    first_in_grad = dot_nt(qkv_grad_ref[core], own_w_ref[...]) + dot_nt(
        qkv_grad_ref[1 - core], other_w_ref[...]
    )
    for c in range(chains):
        rows = slice(c * length, (c + 1) * length)
        upstream = first_in_grad[rows]
        normed, inverse = norm_parts(res_ref[c].astype(F32))
        pre_ref[c : c + 1, :width] = jnp.sum(upstream * normed, 0, keepdims=True)
        pre_ref[c : c + 1, width : 2 * width] = jnp.sum(upstream, 0, keepdims=True)
        scale = mod_ref[c : c + 1, :width]
        res_grad_ref[rows] = first_grad[rows] + norm_back(
            normed, inverse, upstream * (1.0 + scale)
        )


def attention_grads_kernel(
    place_ref,
    keep_in,
    got_in,
    across_in,
    keep_grad,
    got_grad,
    across_grad,
    outer_own,
    outer_other,
    outer_across,
    keep_side,
    got_side,
    across_side,
    *refs,
):
    *out_refs, total = refs
    core = place_ref[0] % 2
    width = outer_own.shape[1]
    lead = total.shape[:2]
    inputs = jnp.concatenate([keep_in[core], got_in[core], across_in[0], across_in[1]], 0)
    grads = jnp.concatenate([keep_grad[core], got_grad[core], across_grad[0], across_grad[1]], 0)
    total[:, :, :width] = dot_tn(inputs, grads).astype(BF16).reshape(lead + (width,))
    inputs = jnp.concatenate([outer_own[...], outer_other[...], outer_across[...]], 0)
    grads = jnp.concatenate([keep_side[core], got_side[core], across_side[0], across_side[1]], 0)
    term = dot_tn(inputs, grads).astype(BF16)
    total[:, :, width:] = term.reshape(lead + (term.shape[1],))
    emit_chunks(place_ref, total, out_refs[: len(out_refs) // 2], out_refs[len(out_refs) // 2 :])


def whole_chunks_kernel(kernel, place_ref, *refs):
    kernel(place_ref, *refs)


def pair_last_kernel(
    pairs_ref, one_grad_ref, scores_grad_ref, gain_ref, weight_ref, out_ref, g_weight_ref, g_gain_ref
):
    normed, inverse = norm_parts(pairs_ref[...].astype(F32))
    gain = gain_ref[...]
    low = (normed * gain).astype(BF16)
    scores_grad = scores_grad_ref[...]
    upstream = dot_tn(scores_grad, weight_ref[...])
    out_ref[...] = one_grad_ref[...] + norm_back(normed, inverse, upstream * gain)

    @pl.when(pl.program_id(0) == 0)
    def _():
        g_weight_ref[...] = jnp.zeros_like(g_weight_ref)
        g_gain_ref[...] = jnp.zeros_like(g_gain_ref)

    g_weight_ref[...] += dot(scores_grad, low)
    g_gain_ref[...] += jnp.sum(upstream * normed, 0, keepdims=True)


def on_device(
    n_dp,
    n_f,
    residues,
    pairs,
    lengths,
    time_bins,
    cath_labels,
    residue_cotangent,
    pair_cotangent,
    time_table,
    cath_table,
    attn_modulation,
    attn_gate,
    qkv_weight,
    bias_gain,
    bias_weight,
    out_weight,
    ffn_modulation,
    ffn_gate,
    gate_up,
    down_weight,
    outer_gain,
    outer_weight,
    outer_out,
    pair_gain,
    pair_gate_up,
    pair_down,
):
    place = Place(n_dp, n_f)
    d, f = place.d, place.f
    chains, length, width = residues.shape
    rows = chains * length
    heads = bias_weight.shape[1]
    pair_width = outer_out.shape[1]
    pair_rows = chains * length * length
    time_rows, cath_rows = time_table.shape[0], cath_table.shape[0]
    mod_rows = attn_modulation.shape[0]
    hid_rows = down_weight.shape[0]
    hid_part = hid_rows // 4
    part = hid_part * n_f
    place_ints = place.ints

    slots = Slots()

    lanes = pair_gate_up.shape[0]
    attn_weights = slots.add(place.gather_all(jnp.concatenate([qkv_weight, out_weight], 1)))

    (my_gate_up,) = call_whole(
        functools.partial(split_kernel, hid_rows, hid_part),
        "split_gate_up",
        2.0,
        [struct((mod_rows, gate_up.shape[1] // 4), BF16)],
        place_ints,
        gate_up,
    )
    my_down = pick(down_weight.reshape(4, hid_part, width), d, 0)

    small = jnp.concatenate(
        [
            time_bins.astype(F32),
            cath_labels.astype(F32),
            bias_gain.astype(F32),
            pair_gain.astype(F32),
            outer_gain.astype(F32),
            bias_weight.astype(F32).reshape(-1),
        ]
    )
    (small,) = slots.step((place.to_all_f, small))
    at = 0

    def take(size):
        nonlocal at
        piece = small[:, at : at + size]
        at += size
        return piece

    ffn_weights = slots.add(place.gather_f(jnp.concatenate([my_gate_up, my_down], 1)))
    bins = take(chains).reshape(-1).astype(jnp.int32)
    labels = take(chains).reshape(-1).astype(jnp.int32)
    bias_gain_row = take(bias_gain.shape[0]).reshape(1, pair_width)
    pair_gain_row = take(pair_gain.shape[0]).reshape(1, pair_width)
    outer_gain_row = take(outer_gain.shape[0]).reshape(1, width)
    bias_w = take(bias_weight.size).reshape(pair_width, heads)
    bias_w_t = jnp.pad(bias_w.T, ((0, 16 - heads), (0, 0))).astype(BF16)

    n_group = n_f * chains
    time_hot = (
        (bins[:, None] - f * time_rows) == jnp.arange(time_rows)[None, :]
    ).astype(BF16)
    cath_hot = (
        (labels[:, None] - f * cath_rows) == jnp.arange(cath_rows)[None, :]
    ).astype(BF16)
    condition = (dot(time_hot, time_table) + dot(cath_hot, cath_table)).astype(BF16)
    condition = jnp.swapaxes(condition.reshape(n_group, n_f, mod_rows), 0, 1)
    (condition,) = slots.step((place.to_each_f, condition))
    cond_cols = jnp.sum(condition.astype(F32), 0).astype(BF16)
    mod_weights = jnp.concatenate([attn_modulation, attn_gate, ffn_modulation, ffn_gate], 1)
    mods = dot(cond_cols, mod_weights).reshape(n_f, chains, 6 * width)
    first_mods, other_mods = mods[..., : 2 * width], mods[..., 2 * width :]
    (first_mods,) = slots.step((place.to_each_f, first_mods))
    def side_by_side(weight):
        rows_of, width_of = weight.shape
        parts = weight.reshape(rows_of // lanes, lanes, width_of)
        return [parts[i] for i in range(rows_of // lanes)]

    pair_weights = slots.add(
        place.gather_all(
            jnp.concatenate(
                [pair_gate_up] + side_by_side(outer_weight) + [outer_out] + side_by_side(pair_down), 1
            )
        )
    )
    (other_mods,) = slots.step((place.to_each_f, other_mods))
    mods = jnp.concatenate([jnp.sum(first_mods, 0), jnp.sum(other_mods, 0)], 1)
    gated = jnp.arange(6 * width)[None, :] // width
    mods = jnp.where((gated == 2) | (gated == 5), jax.nn.sigmoid(mods), mods)

    ((own_attn, other_attn),) = slots.finish(attn_weights)

    pairs_flat = pairs.reshape(pair_rows, pair_width)
    block = 512
    bias = pl.pallas_call(
        bias_kernel,
        name="pair_bias",
        grid=(pair_rows // block,),
        in_specs=[
            pl.BlockSpec((block, pair_width), lambda i: (i, 0)),
            whole((1, pair_width)),
            whole((16, pair_width)),
        ],
        out_specs=pl.BlockSpec((16, block), lambda i: (0, i)),
        out_shape=struct((16, pair_rows), F32),
        cost_estimate=cost(6.0),
        compiler_params=params(),
    )(pairs_flat, bias_gain_row, bias_w_t)
    bias = bias[:heads].reshape(heads, chains, length, length)
    bias = jnp.transpose(bias, (1, 0, 2, 3)).reshape(chains, heads * length, length)
    first_in, qkv, prob, attended, first_branch, first_out, second_in = call_whole(
        functools.partial(attention_kernel, heads),
        "attention",
        6.0,
        [
            struct((rows, width), BF16),
            struct((rows, 3 * width), BF16),
            struct((chains, heads * length, length), F32),
            struct((rows, width), BF16),
            struct((rows, width), F32),
            struct((rows, width), F32),
            struct((rows, width), BF16),
        ],
        lengths,
        place_ints,
        residues,
        mods,
        own_attn,
        other_attn,
        bias,
        scratch=[pltpu.VMEM((2, rows, 2 * width), F32)],
    )

    slots.step()
    (other_rows,) = slots.step((place.swap_x, second_in))
    (across_rows,) = slots.step((place.swap_core, jnp.concatenate([second_in, other_rows])))
    (ffn_weight,) = slots.finish(ffn_weights)
    ffn_weight = ffn_weight.reshape(width, -1)
    rows_all, gate, up, hidden, mine, theirs = call_whole(
        transition_kernel,
        "transition",
        5.0,
        [
            struct((4 * rows, width), BF16),
            struct((4 * rows, part), F32),
            struct((4 * rows, part), F32),
            struct((4 * rows, part), BF16),
            struct((2 * rows, width), F32),
            struct((2 * rows, width), BF16),
        ],
        second_in,
        other_rows,
        across_rows,
        ffn_weight,
    )
    (across,) = slots.step((place.swap_core, theirs))
    branch_own = mine + across.astype(F32)
    (branch_other,) = slots.step((place.swap_x, branch_own[rows:].astype(BF16)))
    ((own_pair, other_pair),) = slots.finish(pair_weights)
    low_pair = jnp.where(place.core == 0, own_pair, other_pair)
    high_pair = jnp.where(place.core == 0, other_pair, own_pair)
    pair_all = jnp.concatenate([low_pair, high_pair], 1)
    start = pair_gate_up.shape[1]

    def take_cols(shape):
        nonlocal start
        wide = shape[0] * shape[1] // pair_all.shape[0]
        piece = pair_all[:, start : start + wide].reshape(n_f, lanes, wide // shape[1], shape[1])
        start += wide
        return jnp.swapaxes(piece, 1, 2).reshape(shape)

    outer_w_full = take_cols((width, 2 * pair_width))
    outer_out_full = take_cols((pair_width, pair_width))
    pair_down_full = take_cols((pair_down.shape[0] * n_f, pair_width))
    first_half = {2: whole((rows, width))}
    second_branch, second_out, res_out, outer_in, sides = call_whole(
        outer_kernel,
        "outer_sides",
        3.0,
        [
            struct((rows, width), F32),
            struct((rows, width), F32),
            struct((rows, width), BF16),
            struct((rows, width), BF16),
            struct((rows, 2 * pair_width), F32),
        ],
        lengths,
        first_out,
        branch_own,
        branch_other,
        mods,
        outer_gain_row,
        outer_w_full,
        blocks=first_half,
    )

    back_small = jnp.concatenate(
        [bins.astype(F32)[:, None], labels.astype(F32)[:, None], cond_cols.astype(F32)], 1
    )
    keep_in = jnp.stack([first_in, jnp.where(place.x == 1, attended, first_in)])
    give_in = jnp.stack([first_in, jnp.where(place.x == 0, attended, first_in)])
    got_in, other_small, outer_other = slots.step(
        (place.swap_x, give_in), (place.swap_x, back_small), (place.swap_x, outer_in)
    )
    back_small = ordered(place.x, back_small, other_small, 0)

    def toward_core(keep, got):
        return jnp.stack([pick(keep, 1 - place.core, 0), pick(got, 1 - place.core, 0)])


    sides = sides.reshape(chains, length, 2 * pair_width)
    count = 8
    pair_hidden = pair_down_full.shape[0]
    wide_half = (3 * pair_hidden + pair_width) // 2
    pair_block = pl.BlockSpec((1, count, length, pair_width), lambda c, b: (c, b, 0, 0))
    (
        pair_out,
        pair_grad,
        left_grad,
        right_grad,
        keep_pair,
        give_pair,
        g_pair_gain,
    ) = pl.pallas_call(
        functools.partial(pair_kernel, n_f),
        name="pairs",
        grid=(chains, length // count),
        in_specs=[
            SMEM,
            SMEM,
            pl.BlockSpec((1, count, pair_width), lambda c, b: (c, b, 0)),
            pl.BlockSpec((1, length, pair_width), lambda c, b: (c, 0, 1)),
            pair_block,
            pair_block,
            whole((1, pair_width)),
            whole(outer_out_full.shape),
            whole((pair_width, 2 * pair_hidden)),
            whole(pair_down_full.shape),
        ],
        out_specs=[
            pair_block,
            pair_block,
            pl.BlockSpec((1, count, pair_width), lambda c, b: (c, b, 0)),
            pl.BlockSpec((1, length, pair_width), lambda c, b: (c, 0, 0)),
            whole((pair_width, wide_half)),
            whole((pair_width, wide_half)),
            whole((1, pair_width)),
        ],
        out_shape=[
            struct(pairs.shape, BF16),
            struct(pairs.shape, F32),
            struct((chains, length, pair_width), F32),
            struct((chains, length, pair_width), F32),
            struct((pair_width, wide_half), BF16),
            struct((pair_width, wide_half), BF16),
            struct((1, pair_width), F32),
        ],
        scratch_shapes=[
            pltpu.VMEM((pair_width, 2 * pair_hidden), F32),
            pltpu.VMEM((pair_width, pair_hidden), F32),
            pltpu.VMEM((pair_width, pair_width), F32),
            pltpu.VMEM((1, pair_width), F32),
        ],
        cost_estimate=cost(35.0),
        compiler_params=params(),
    )(
        lengths,
        place_ints,
        sides,
        sides,
        pairs,
        pair_cotangent,
        pair_gain_row,
        outer_out_full,
        pair_all,
        pair_down_full,
    )

    keep_side, give_side, g_outer_gain, second_grad, branch_two_grad, second_pre = call_whole(
        outer_back_kernel,
        "outer_sides_back",
        3.0,
        [
            struct((2, rows, pair_width // 2), BF16),
            struct((2, rows, pair_width // 2), BF16),
            struct((1, width), F32),
            struct((rows, width), F32),
            struct((rows, width), BF16),
            struct((chains, width), F32),
        ],
        lengths,
        place_ints,
        left_grad.reshape(rows, pair_width),
        right_grad.reshape(rows, pair_width),
        outer_w_full,
        outer_gain_row,
        second_out,
        residue_cotangent.reshape(rows, width),
        second_branch,
        mods,
    )

    other_grads, got_side, across_in, other_small, outer_across, across_pair = slots.step(
        (place.swap_x, branch_two_grad),
        (place.swap_x, give_side),
        (place.swap_core, toward_core(keep_in, got_in)),
        (place.swap_core, back_small),
        (place.swap_core, jnp.concatenate([outer_in, outer_other])),
        (place.swap_core, give_pair),
    )
    back_small = ordered(place.core, back_small, other_small, 1).reshape(n_dp * n_group, -1)
    bins_all = back_small[:, 0].astype(jnp.int32)
    labels_all = back_small[:, 1].astype(jnp.int32)
    cond_all = back_small[:, 2:].astype(BF16)
    across_grads, across_side = slots.step(
        (place.swap_core, jnp.concatenate([branch_two_grad, other_grads])),
        (place.swap_core, toward_core(keep_side, got_side)),
    )
    grads_all, gate_grad, up_grad, mine, theirs = call_whole(
        transition_back_kernel,
        "transition_back",
        6.0,
        [
            struct((4 * rows, width), BF16),
            struct((4 * rows, part), BF16),
            struct((4 * rows, part), BF16),
            struct((2 * rows, width), F32),
            struct((2 * rows, width), BF16),
        ],
        branch_two_grad,
        other_grads,
        across_grads,
        gate,
        up,
        ffn_weight,
    )
    (across,) = slots.step((place.swap_core, theirs))
    own = mine + across.astype(F32)

    def chunk_call(kernel, name, micros, shape, *operands):
        if shape[0] % 16 == 0:
            chunks = call_whole(
                kernel,
                name,
                micros,
                [struct(shape, BF16)] * (2 * place.ring),
                place_ints,
                *operands,
                scratch=[pltpu.VMEM((n_f,) + shape, BF16)],
            )
            return chunks[: place.ring], chunks[place.ring :]
        (total,) = call_whole(
            functools.partial(whole_chunks_kernel, kernel),
            name,
            micros,
            [struct((1, n_f * shape[0], shape[1]), BF16)],
            place_ints,
            *operands,
        )
        return place.chunks(total.reshape((n_f,) + shape))

    ffn_chunks = chunk_call(
        transition_grads_kernel,
        "transition_grads",
        5.0,
        (mod_rows, 2 * part + width),
        rows_all,
        hidden,
        grads_all,
        gate_grad,
        up_grad,
    )
    (other,) = slots.step((place.swap_x, own[rows:].astype(BF16)))
    ffn_sums = slots.add(place.reduce_f(*ffn_chunks))
    pair_shape = (n_f, 2, lanes // 2, wide_half)
    pair_sums = slots.add(
        place.reduce_x(keep_pair.reshape(pair_shape), across_pair.reshape(pair_shape))
    )

    keep_grad, give_grad, scores_grad, res_grad, pre = call_whole(
        functools.partial(attention_back_kernel, heads),
        "attention_back",
        9.0,
        [
            struct((2, rows, width), BF16),
            struct((2, rows, width), BF16),
            struct((chains, heads * length, length), BF16),
            struct((rows, width), F32),
            struct((chains, 5 * width), F32),
        ],
        lengths,
        place_ints,
        own,
        other,
        mods,
        first_out,
        second_grad,
        first_branch,
        residues,
        qkv,
        prob,
        own_attn,
        other_attn,
        blocks=first_half,
        scratch=[
            pltpu.VMEM((rows, width), BF16),
            pltpu.VMEM((rows, width), F32),
            pltpu.VMEM((rows, width), BF16),
            pltpu.VMEM((2, rows, 2 * width), BF16),
            pltpu.VMEM((2, rows, width), BF16),
        ],
    )
    slots.step()

    pre = jnp.concatenate([pre, second_pre], 1).astype(BF16)
    got_grad, pre_group = slots.step((place.swap_x, give_grad), (place.to_all_f, pre))
    scores_t = jnp.transpose(
        scores_grad.reshape(chains, heads, length, length), (1, 0, 2, 3)
    ).reshape(heads, pair_rows)
    scores_t = jnp.pad(scores_t, ((0, 16 - heads), (0, 0)))
    pairs_grad, g_bias_w, g_bias_gain = pl.pallas_call(
        pair_last_kernel,
        name="pairs_last",
        grid=(pair_rows // block,),
        in_specs=[
            pl.BlockSpec((block, pair_width), lambda i: (i, 0)),
            pl.BlockSpec((block, pair_width), lambda i: (i, 0)),
            pl.BlockSpec((16, block), lambda i: (0, i)),
            whole((1, pair_width)),
            whole((16, pair_width)),
        ],
        out_specs=[
            pl.BlockSpec((block, pair_width), lambda i: (i, 0)),
            whole((16, pair_width)),
            whole((1, pair_width)),
        ],
        out_shape=[
            struct((pair_rows, pair_width), F32),
            struct((16, pair_width), F32),
            struct((1, pair_width), F32),
        ],
        cost_estimate=cost(9.0),
        compiler_params=params(),
    )(pairs_flat, pair_grad.reshape(pair_rows, pair_width), scores_t, bias_gain_row, bias_w_t)

    small_terms = jnp.concatenate(
        [g_bias_w[:heads], g_bias_gain, g_pair_gain, g_outer_gain.reshape(-1, pair_width)], 0
    )
    small_terms = slots.add(place.sum_everywhere(small_terms))
    pre_group = pre_group.reshape(n_group, 6 * width)
    cond_grad = dot_nt(pre_group, mod_weights)
    across_grad, cond_grad, pre_other = slots.step(
        (place.swap_core, toward_core(keep_grad, got_grad)),
        (place.to_all_f, cond_grad.astype(BF16)),
        (place.swap_x, pre_group),
    )
    attn_chunks = chunk_call(
        attention_grads_kernel,
        "attention_grads",
        4.0,
        (mod_rows, width + pair_width // 2),
        keep_in,
        got_in,
        across_in,
        keep_grad,
        got_grad,
        across_grad,
        outer_in,
        outer_other,
        outer_across,
        keep_side,
        got_side,
        across_side,
    )
    attn_sums = slots.add(place.reduce_f(*attn_chunks))
    pre_all = ordered(place.x, pre_group, pre_other, 0)
    cond_grad = jnp.swapaxes(cond_grad, 0, 1).reshape(n_group, width)
    pre_other, cond_other = slots.step((place.swap_core, pre_all), (place.swap_x, cond_grad))
    pre_all = ordered(place.core, pre_all, pre_other, 1).reshape(n_dp * n_group, 6 * width)
    cond_grad = ordered(place.x, cond_grad, cond_other, 0)
    (cond_other,) = slots.step((place.swap_core, cond_grad))
    cond_grad = ordered(place.core, cond_grad, cond_other, 1).reshape(n_dp * n_group, width)
    g_mods = dot_tn(cond_all, pre_all)
    time_all = (
        (bins_all[:, None] - f * time_rows) == jnp.arange(time_rows)[None, :]
    ).astype(BF16)
    cath_all = (
        (labels_all[:, None] - f * cath_rows) == jnp.arange(cath_rows)[None, :]
    ).astype(BF16)
    out_time = dot_tn(time_all, cond_grad)
    out_cath = dot_tn(cath_all, cond_grad)

    attn_sums, ffn_sums, pair_sums, small_terms = slots.finish(
        attn_sums, ffn_sums, pair_sums, small_terms
    )
    (
        out_gate_up,
        out_down,
        out_qkv,
        out_out,
        out_outer_w,
        out_pair_gate_up,
        out_outer_out,
        out_pair_down,
    ) = call_whole(
        functools.partial(finish_kernel, hid_rows, hid_part),
        "finish",
        8.0,
        [
            struct(w.shape, F32)
            for w in (
                gate_up,
                down_weight,
                qkv_weight,
                out_weight,
                outer_weight,
                pair_gate_up,
                outer_out,
                pair_down,
            )
        ],
        place_ints,
        *ffn_sums,
        *attn_sums,
        *pair_sums,
        scratch=[pltpu.VMEM((4,) + sums[0].shape, BF16) for sums in (ffn_sums, attn_sums, pair_sums)],
    )
    bias_rows = bias_weight.shape[0]
    small_own = lax.dynamic_slice_in_dim(small_terms, f * bias_rows, bias_rows, 1)
    out_bias_w = small_own[:heads].T
    out_bias_gain = small_own[heads]
    out_pair_gain = small_own[heads + 1]
    out_outer_gain = lax.dynamic_slice_in_dim(
        small_terms[heads + 2 :].reshape(-1), f * mod_rows, mod_rows, 0
    )

    return (
        res_out.reshape(residues.shape),
        pair_out,
        res_grad.reshape(residues.shape),
        pairs_grad.reshape(pairs.shape),
        out_time,
        out_cath,
        g_mods[:, : 2 * width],
        g_mods[:, 2 * width : 3 * width],
        out_qkv,
        out_bias_gain,
        out_bias_w,
        out_out,
        g_mods[:, 3 * width : 5 * width],
        g_mods[:, 5 * width :],
        out_gate_up,
        out_down,
        out_outer_gain,
        out_outer_w,
        out_outer_out,
        out_pair_gain,
        out_pair_gate_up,
        out_pair_down,
    )


def solution(mesh):
    chains3 = P(("dp", "fsdp"), None, None)
    chains4 = P(("dp", "fsdp"), None, None, None)
    chains1 = P(("dp", "fsdp"))
    table = P("fsdp", None)
    line = P("fsdp")
    weights = (
        table,
        table,
        table,
        table,
        table,
        line,
        table,
        table,
        table,
        table,
        table,
        table,
        line,
        table,
        table,
        line,
        table,
        table,
    )
    return jax.shard_map(
        functools.partial(on_device, mesh.shape["dp"], mesh.shape["fsdp"]),
        mesh=mesh,
        in_specs=(chains3, chains4, chains1, chains1, chains1, chains3, chains4) + weights,
        out_specs=(chains3, chains4, chains3, chains4) + weights,
        check_vma=False,
    )
```

```python
import functools
import math

import jax
import jax.numpy as jnp
from jax import lax
from jax.experimental import pallas as pl
from jax.experimental.pallas import tpu as pltpu
from jax.sharding import PartitionSpec as P

EPSILON = 1e-05
F32 = jnp.float32
BF16 = jnp.bfloat16
VMEM_LIMIT = 56 * 1024 * 1024


def norm_parts(values):
    center = values - jnp.mean(values, -1, keepdims=True)
    inverse = lax.rsqrt(jnp.mean(center * center, -1, keepdims=True) + EPSILON)
    return center * inverse, inverse


def norm_back(normed, inverse, upstream):
    return inverse * (
        upstream
        - jnp.mean(upstream, -1, keepdims=True)
        - normed * jnp.mean(upstream * normed, -1, keepdims=True)
    )


def dot(left, right):
    return jnp.dot(left, right, preferred_element_type=F32)


def dot_nt(left, right):
    return lax.dot_general(left, right, (((1,), (1,)), ((), ())), preferred_element_type=F32)


def dot_tn(left, right):
    return lax.dot_general(left, right, (((0,), (0,)), ((), ())), preferred_element_type=F32)


def params():
    return pltpu.CompilerParams(vmem_limit_bytes=VMEM_LIMIT)


def cost(micros):
    return pl.CostEstimate(flops=int(micros * 1e9), bytes_accessed=0, transcendentals=0)


def whole(shape):
    return pl.BlockSpec(shape, lambda *_: (0,) * len(shape))


SMEM = pl.BlockSpec(memory_space=pltpu.SMEM)


def call_whole(kernel, name, micros, outs, *operands, blocks=None, scratch=()):
    blocks = blocks or {}
    specs = [
        blocks.get(i, SMEM if a.dtype == jnp.int32 else whole(a.shape))
        for i, a in enumerate(operands)
    ]
    return pl.pallas_call(
        kernel,
        grid=(1,),
        name=name,
        in_specs=specs,
        out_specs=[whole(o.shape) for o in outs],
        out_shape=outs,
        scratch_shapes=list(scratch),
        cost_estimate=cost(micros),
        compiler_params=params(),
    )(*operands)


def struct(shape, dtype):
    return jax.ShapeDtypeStruct(shape, dtype)


def swap(values, axis, size, bit):
    return lax.ppermute(values, axis, [(i, i ^ bit) for i in range(size)])


def pick(values, index, axis):
    return lax.dynamic_index_in_dim(values, index, axis, keepdims=False)


def ordered(bit, own, other, axis):
    first = jnp.where(bit == 0, own, other)
    second = jnp.where(bit == 0, other, own)
    return jnp.stack([first, second], axis)


class Place:
    def __init__(self, n_dp, n_f):
        self.n_dp, self.n_f, self.ring = n_dp, n_f, n_f // 2
        self.d = lax.axis_index("dp")
        self.f = lax.axis_index("fsdp")
        self.core, self.x = self.d % 2, self.d // 2
        self.y, self.r = self.f % 2, self.f // 2
        self.ints = jnp.stack([self.d, self.f]).astype(jnp.int32)

    def swap_core(self, values):
        return swap(values, "dp", self.n_dp, 1)

    def swap_x(self, values):
        return swap(values, "dp", self.n_dp, 2)

    def swap_y(self, values):
        return swap(values, "fsdp", self.n_f, 1)

    def shift_ring(self, values):
        return lax.ppermute(
            values, "fsdp", [(i, (i + 2) % self.n_f) for i in range(self.n_f)]
        )

    def to_each_f(self, values):
        return lax.all_to_all(values, "fsdp", split_axis=0, concat_axis=0, tiled=True)

    def to_all_f(self, values):
        return self.to_each_f(jnp.broadcast_to(values[None], (self.n_f,) + values.shape))


    def gather(self, piece, shared, x_own, on_all_f):
        ring = self.ring
        moving, last, pieces, from_x = piece, None, [], []
        for k in range(ring + 1):
            moves, beside = [], ()
            if k < ring:
                moves.append((self.swap_y, moving))
            if k < ring - 1:
                moves.append((self.shift_ring, moving))
            if k == ring and on_all_f:
                beside = on_all_f(pieces)
            if k > 0:
                both = [p[:shared] for p in last]
                moves.append((self.swap_x, both[1] if k == 1 else jnp.stack(both)))
            got = yield moves, beside
            if k > 0:
                from_x.append(got[-1])
            if k < ring:
                last = [moving, got[0]]
                pieces += last
            if k < ring - 1:
                moving = got[1]
        return pieces, [x_own] + from_x

    def gather_cores(self, pieces, from_x, rows, urgent):
        held = self.assemble(pieces, 0, rows, from_x)
        if not urgent:
            yield [], (held,)
        (other,) = yield [(self.swap_core, held)]
        return held, other

    def gather_shared(self, piece, x_own, rows, urgent, on_all_f=None):
        shared = x_own.shape[0]
        pieces, from_x = yield from self.gather(piece, shared, x_own, on_all_f)
        return (yield from self.gather_cores(pieces, from_x, rows, urgent))

    def assemble(self, pieces, first, rows, from_x=()):
        width = pieces[0].shape[1]
        last = from_x[0].shape[0] if from_x else pieces[0].shape[0]
        blocks = (last - first) // rows
        if rows % 16 == 0:
            lead = (2,) if from_x else ()
            take = pl.BlockSpec((last, width), lambda *_: (0, 0))
            (held,) = call_whole(
                functools.partial(assemble_kernel, self.ring, first, rows, blocks, bool(from_x)),
                "assemble",
                3.0,
                [struct(lead + (self.n_f, rows, blocks * width), pieces[0].dtype)],
                self.ints,
                *pieces,
                *from_x,
                blocks={1 + i: take for i in range(len(pieces))},
            )
            return held
        order = (self.r - jnp.arange(self.ring)) % self.ring

        def placed(pairs):
            steps = jnp.stack([ordered(self.y, own, other, 0) for own, other in pairs])
            steps = jnp.take(steps, order, 0)[:, :, first:last]
            steps = steps.reshape(self.n_f, blocks, rows, width)
            return jnp.swapaxes(steps, 1, 2).reshape(self.n_f, rows, blocks * width)

        held = placed(list(zip(pieces[0::2], pieces[1::2])))
        if not from_x:
            return held
        pairs = [(from_x[0], from_x[1])] + [(both[0], both[1]) for both in from_x[2:]]
        return jnp.stack([held, placed(pairs)])

    def add(self, keep, got):
        return (keep.astype(F32) + got.astype(F32)).astype(BF16)

    def chunks(self, values):
        give, keep = [], []
        values = values.reshape((self.ring, 2) + values.shape[1:])
        for k in range(self.ring):
            chunk = pick(values, (self.r - 1 - k) % self.ring, 0)
            give.append(pick(chunk, 1 - self.y, 0))
            keep.append(pick(chunk, self.y, 0))
        return tuple(give + keep)

    def reduce_f(self, give, keep):
        moving = None
        for k in range(self.ring):
            moves = [(self.swap_y, give[k])]
            if k > 0:
                moves.append((self.shift_ring, moving))
            got = yield moves
            total = keep[k].astype(F32)
            for other in got:
                total = total + other.astype(F32)
            moving = total.astype(BF16)
        return (yield from self.spread_d(moving))

    def chunks_by_distance(self, values):
        values = values.reshape((self.ring, 2) + values.shape[1:])
        order = (self.r + jnp.arange(self.ring)) % self.ring
        return tuple(jnp.take(pick(values, i, 1), order, 0) for i in (1 - self.y, self.y))

    def reduce_direct(self, give, keep):
        ring = self.ring
        (got,) = yield [(self.swap_y, give)]
        total, *parts = [self.add(keep[k], got[k]) for k in range(ring)]

        def shift(values, distance):
            pairs = [(i, (i + 2 * distance) % self.n_f) for i in range(self.n_f)]
            return lax.ppermute(values, "fsdp", pairs)

        got = yield [
            (functools.partial(shift, distance=k + 1), part) for k, part in enumerate(parts)
        ]
        total = total.astype(F32)
        for other in got:
            total = total + other.astype(F32)
        return (yield from self.spread_d(total.astype(BF16)))

    def parts_ring(self, mine, across):
        order = [(self.r - 1 - k) % self.ring for k in range(self.ring)]
        return tuple(self.add(pick(mine, at, 0), pick(across, at, 0)) for at in order)

    def reduce_pair(self, *chunks):
        moving = chunks[0]
        for k, chunk in enumerate(chunks[1:]):
            if k == 2:
                yield []
                yield []
                yield []
            got = yield [(self.shift_ring, moving)]
            moving = self.add(chunk, got[0])
        got = yield [(self.swap_y, pick(moving, 1 - self.y, 0))]
        moving = self.add(pick(moving, self.y, 0), got[0])
        got = yield [(self.swap_x, moving)]
        moving = self.add(moving, got[0])
        got = yield [(self.swap_core, moving)]
        return moving, got[0]

    def spread_d(self, values):
        (other,) = yield [(self.swap_x, values)]
        (across,) = yield [(self.swap_core, jnp.stack([values, other]))]
        return values, other, across


class Chain:
    def __init__(self, moves):
        self.moves, self.result, self.done = moves, None, False
        self.pending, self.beside = [], ()
        self.advance(None)

    def advance(self, got):
        try:
            asked = self.moves.send(got)
            self.pending, self.beside = asked if isinstance(asked, tuple) else (asked, ())
        except StopIteration as stop:
            self.result, self.done = stop.value, True
            self.pending, self.beside = [], ()


class Slots:
    def __init__(self):
        self.chains, self.token = [], None

    def add(self, moves):
        chain = Chain(moves)
        self.chains.append(chain)
        return chain

    def step(self, *extra, beside=()):
        moves, all_beside = list(extra), list(beside)
        for chain in self.chains:
            moves += chain.pending
            all_beside += chain.beside
        if not moves:
            return tuple(beside)
        values = tuple(value for _, value in moves)
        if self.token is not None:
            values = lax.optimization_barrier((values, self.token))[0]
        got = [move(value) for (move, _), value in zip(moves, values)]
        got, all_beside = lax.optimization_barrier((tuple(got), tuple(all_beside)))
        self.token = got[0]
        at = len(extra)
        for chain in self.chains:
            count = len(chain.pending)
            chain.advance(list(got[at : at + count]))
            at += count
        self.chains = [chain for chain in self.chains if not chain.done]
        return got[: len(extra)] + all_beside[: len(beside)]

    def finish(self, *chains):
        while not all(chain.done for chain in chains):
            self.step()
        return [chain.result for chain in chains]


def assemble_kernel(ring, first, rows, blocks, shared, place_ref, *refs):
    *pieces, out_ref = refs
    y, r = place_ref[1] % 2, place_ref[1] // 2
    width = pieces[0].shape[-1]
    pairs = [(pieces[2 * k], (), pieces[2 * k + 1], ()) for k in range(ring)]
    planes = [pairs]
    if shared:
        x_own, x_first, *both = pieces[2 * ring :]
        planes.append([(x_own, (), x_first, ())] + [(ref, (0,), ref, (1,)) for ref in both])
    for plane, pairs in enumerate(planes):
        lead = (plane,) if shared else ()
        for k, (own, own_at, other, other_at) in enumerate(pairs):
            at = 2 * lax.rem(r - k + ring, ring)
            for b in range(blocks):
                cols = slice(b * width, (b + 1) * width)
                span = slice(first + b * rows, first + (b + 1) * rows)
                out_ref[lead + (at + y, slice(None), cols)] = own[own_at + (span,)]
                out_ref[lead + (at + 1 - y, slice(None), cols)] = other[other_at + (span,)]


def member_other(d):
    return d + 2 - 4 * (d // 2), 1 - 2 * (d % 2)


def pack_kernel(
    group,
    part,
    place_ref,
    gate_up_ref,
    down_ref,
    pair_gate_up_ref,
    outer_w_ref,
    outer_out_ref,
    pair_down_ref,
    own_ref,
    x_ref,
    wide,
):
    d = place_ref[0]
    lanes = wide.shape[0]
    at = 0
    for ref in (pair_gate_up_ref, outer_w_ref, outer_out_ref, pair_down_ref):
        for i in range(ref.shape[0] // lanes):
            wide[:, at : at + ref.shape[1]] = ref[i * lanes : (i + 1) * lanes]
            at += ref.shape[1]
    wide[:, at:] = jnp.zeros((lanes, wide.shape[1] - at), BF16)
    span = wide.shape[1] // 4
    for member, out_ref in ((d, own_ref), (member_other(d)[0], x_ref)):
        mine = wide[:, pl.ds(pl.multiple_of(member * span, 128), span)]
        for b in range(span // 256):
            out_ref[b * lanes : (b + 1) * lanes] = mine[:, b * 256 : (b + 1) * 256]
    first = span // 256 * lanes
    rows = gate_up_ref.shape[0]
    groups = gate_up_ref.shape[1] // group
    for m in range(4):

        @pl.when(d == m)
        def _(m=m):
            cols = [
                gate_up_ref[:, g * group + m * part : g * group + (m + 1) * part].astype(F32)
                for g in range(groups)
            ]
            mine = jnp.concatenate(cols, 1).astype(BF16)
            mine = jnp.concatenate([mine, down_ref[m * part : (m + 1) * part]], 1)
            for b in range(mine.shape[1] // 256):
                at = first + b * rows
                own_ref[at : at + rows] = mine[:, b * 256 : (b + 1) * 256]


def unpack_kernel(place_ref, own_ref, other_ref, *refs):
    *out_refs, wide = refs
    d = place_ref[0]
    x, toward = member_other(d)
    span = own_ref.shape[3]
    for ref, i, member in (
        (own_ref, 0, d),
        (own_ref, 1, x),
        (other_ref, 0, d + toward),
        (other_ref, 1, x + toward),
    ):
        wide[:, :, pl.ds(pl.multiple_of(member * span, 128), span)] = ref[i]
    at = 0
    for ref in out_refs:
        width = ref.shape[3]
        for i in range(ref.shape[1]):
            ref[:, i] = wide[:, :, at : at + width]
            at += width


def put_members(place_ref, pieces, held):
    d = place_ref[0]
    x, toward = member_other(d)
    held[d] = pieces[0][...]
    held[x] = pieces[1][...]
    held[d + toward] = pieces[2][0]
    held[x + toward] = pieces[2][1]


def finish_kernel(part, place_ref, *refs):
    gate_up_ref, down_ref, qkv_ref, out_ref, outer_w_ref = refs[8:13]
    pair_gate_up_ref, outer_out_ref, pair_down_ref, held, attn_held, pair_held = refs[13:]
    put_members(place_ref, refs[:3], held)
    put_members(place_ref, refs[3:6], attn_held)
    core = place_ref[0] % 2
    pair_held[core] = refs[6][...]
    pair_held[1 - core] = refs[7][...]
    count = down_ref.shape[0] // 4
    quarter = gate_up_ref.shape[1] // 4
    width = out_ref.shape[1]
    side = outer_w_ref.shape[1] // 4
    for m in range(4):
        down_ref[m * count : (m + 1) * count] = held[m][:, quarter:].astype(F32)
        if m < 3:
            qkv_ref[:, m * width : (m + 1) * width] = attn_held[m][:, :width].astype(F32)
        else:
            out_ref[...] = attn_held[m][:, :width].astype(F32)
        outer_w_ref[:, m * side : (m + 1) * side] = attn_held[m][:, width:].astype(F32)
    for start in range(0, quarter, part):
        both = [held[m][:, start : start + part].astype(F32) for m in range(4)]
        gate_up_ref[:, 4 * start : 4 * (start + part)] = jnp.concatenate(both, 1)
    lanes = pair_held.shape[1]
    hidden2, pair_width = pair_gate_up_ref.shape[1], outer_out_ref.shape[1]
    wide = jnp.concatenate([pair_held[0], pair_held[1]], 1).astype(F32)
    pair_gate_up_ref[...] = wide[:, :hidden2]
    outer_out_ref[...] = wide[:, hidden2 : hidden2 + pair_width]
    for block in range(4):
        start = hidden2 + (1 + block) * pair_width
        pair_down_ref[block * lanes : (block + 1) * lanes] = wide[:, start : start + pair_width]


def bias_kernel(pairs_ref, gain_ref, weight_ref, out_ref):
    normed, _ = norm_parts(pairs_ref[...].astype(F32))
    low = (normed * gain_ref[...]).astype(BF16)
    out_ref[...] = dot_nt(weight_ref[...], low)


def head_mask(heads, length, width):
    row = lax.broadcasted_iota(jnp.int32, (heads * length, 1), 0) // length
    col = lax.broadcasted_iota(jnp.int32, (1, width), 1) // (width // heads)
    return row == col


def spread_heads(rows, mask, heads):
    return jnp.where(mask, jnp.concatenate([rows] * heads, 0), jnp.zeros((), rows.dtype))


def fold_heads(wide, mask, heads):
    kept = jnp.where(mask, wide, 0.0)
    return jnp.sum(kept.reshape(heads, wide.shape[0] // heads, wide.shape[1]), 0)


def keep_of(lengths_ref, chain, length):
    row = lax.broadcasted_iota(jnp.int32, (length, 1), 0)
    return (row < lengths_ref[chain]).astype(F32)


def members_of(place_ref, own_ref, other_ref):
    d = place_ref[0]
    x, toward = member_other(d)
    return (
        (lambda: own_ref[0], d),
        (lambda: own_ref[1], x),
        (lambda: other_ref[0], d + toward),
        (lambda: other_ref[1], x + toward),
    )


def attention_kernel(
    heads,
    lengths_ref,
    place_ref,
    res_ref,
    mod_ref,
    own_w_ref,
    other_w_ref,
    bias_ref,
    first_in_ref,
    qkv_ref,
    prob_ref,
    attended_ref,
    branch_ref,
    first_out_ref,
    second_in_ref,
    by_member,
):
    chains, length, width = res_ref.shape
    factor = 1.0 / math.sqrt(width // heads)
    mask = head_mask(heads, length, width)
    for c in range(chains):
        rows = slice(c * length, (c + 1) * length)
        normed, _ = norm_parts(res_ref[c].astype(F32))
        scale = mod_ref[c : c + 1, :width]
        shift = mod_ref[c : c + 1, width : 2 * width]
        first_in_ref[rows] = (normed * (1.0 + scale) + shift).astype(BF16)
    for weight, member in members_of(place_ref, own_w_ref, other_w_ref):
        by_member[member] = dot(first_in_ref[...], weight()).astype(BF16)
    for m in range(3):
        qkv_ref[:, m * width : (m + 1) * width] = by_member[m]
    for c in range(chains):
        rows = slice(c * length, (c + 1) * length)
        queries = spread_heads(qkv_ref[rows, :width], mask, heads)
        keys = qkv_ref[rows, width : 2 * width]
        value_rows = qkv_ref[rows, 2 * width :]
        scores = dot_nt(queries, keys) * factor + bias_ref[c]
        column = lax.broadcasted_iota(jnp.int32, scores.shape, 1)
        scores = jnp.where(column < lengths_ref[c], scores, -1000000000.0)
        exps = jnp.exp(scores - jnp.max(scores, -1, keepdims=True))
        prob = exps / jnp.sum(exps, -1, keepdims=True)
        prob_ref[c] = prob
        wide = dot(prob.astype(BF16), value_rows)
        attended_ref[rows] = fold_heads(wide, mask, heads).astype(BF16)
    for weight, member in members_of(place_ref, own_w_ref, other_w_ref):

        @pl.when(member == 3)
        def _(weight=weight):
            branch_ref[...] = dot(attended_ref[...], weight())

    for c in range(chains):
        rows = slice(c * length, (c + 1) * length)
        keep = keep_of(lengths_ref, c, length)
        gate = mod_ref[c : c + 1, 2 * width : 3 * width]
        first_out = res_ref[c].astype(F32) + keep * gate * branch_ref[rows]
        first_out_ref[rows] = first_out
        normed, _ = norm_parts(first_out)
        scale = mod_ref[c : c + 1, 3 * width : 4 * width]
        shift = mod_ref[c : c + 1, 4 * width : 5 * width]
        second_in_ref[rows] = (normed * (1.0 + scale) + shift).astype(BF16)


def emit_members(place_ref, blocks, keep_ref, give_ref):
    for m, block in enumerate(blocks):

        @pl.when(place_ref[0] // 2 == m // 2)
        def _(m=m, block=block):
            keep_ref[m % 2] = block

        @pl.when(place_ref[0] // 2 != m // 2)
        def _(m=m, block=block):
            give_ref[m % 2] = block


def silu_parts(gate):
    logistic = jax.nn.sigmoid(gate)
    act = gate * logistic
    return act, logistic + act * (1.0 - logistic)


def transition_kernel(
    own_ref,
    other_ref,
    across_ref,
    across_other_ref,
    weight_ref,
    rows_ref,
    gate_ref,
    up_ref,
    hidden_ref,
    mine_ref,
    theirs_ref,
):
    count, width = own_ref.shape
    part = gate_ref.shape[1]
    for i, ref in enumerate((own_ref, other_ref, across_ref, across_other_ref)):
        rows_ref[i * count : (i + 1) * count] = ref[...]
    rows = rows_ref[...]
    gate = dot(rows, weight_ref[:, :part])
    up = dot(rows, weight_ref[:, part : 2 * part])
    gate_ref[...] = gate.astype(BF16)
    up_ref[...] = up.astype(BF16)
    hidden = (gate * jax.nn.sigmoid(gate) * up).astype(BF16)
    hidden_ref[...] = hidden
    down = weight_ref[:, 2 * part :]
    mine_ref[...] = dot(hidden[: 2 * count], down)
    theirs_ref[...] = dot(hidden[2 * count :], down).astype(BF16)


def outer_kernel(
    lengths_ref,
    first_out_ref,
    branch_own_ref,
    branch_across_ref,
    branch_other_ref,
    mod_ref,
    gain_ref,
    weight_ref,
    branch_ref,
    second_out_ref,
    res_out_ref,
    outer_in_ref,
    sides_ref,
):
    chains, width = mod_ref.shape[0], first_out_ref.shape[1]
    length = first_out_ref.shape[0] // chains
    branch = branch_own_ref[...] + branch_across_ref[...].astype(F32)
    branch = branch + branch_other_ref[...].astype(F32)
    branch_ref[...] = branch
    for c in range(chains):
        rows = slice(c * length, (c + 1) * length)
        keep = keep_of(lengths_ref, c, length)
        gate = mod_ref[c : c + 1, 5 * width : 6 * width]
        second_out_ref[rows] = first_out_ref[rows] + keep * gate * branch[rows]
    second_out = second_out_ref[...]
    res_out_ref[...] = second_out.astype(BF16)
    normed, _ = norm_parts(second_out)
    outer_in_ref[...] = (normed * gain_ref[...]).astype(BF16)
    sides_ref[...] = dot(outer_in_ref[...], weight_ref[...])


def pair_kernel(
    owners,
    lengths_ref,
    place_ref,
    left_ref,
    right_ref,
    pairs_ref,
    cot_ref,
    gain_ref,
    outer_w_ref,
    gate_up_ref,
    down_ref,
    pair_out_ref,
    pair_grad_ref,
    left_grad_ref,
    right_grad_ref,
    keep_ref,
    give_ref,
    g_gain_ref,
    acc_gate_up,
    acc_down,
    acc_outer,
    acc_gain,
):
    chain, block = pl.program_id(0), pl.program_id(1)
    _, count, length, width = pairs_ref.shape
    rows = count * length
    hidden = down_ref.shape[0]
    size = lengths_ref[chain]

    @pl.when((chain == 0) & (block == 0))
    def _():
        acc_gate_up[...] = jnp.zeros_like(acc_gate_up)
        acc_down[...] = jnp.zeros_like(acc_down)
        acc_outer[...] = jnp.zeros_like(acc_outer)
        acc_gain[...] = jnp.zeros_like(acc_gain)

    @pl.when(block == 0)
    def _():
        right_grad_ref[...] = jnp.zeros_like(right_grad_ref)

    @pl.when(block * count >= size)
    def _():
        pair_out_ref[...] = pairs_ref[...]
        pair_grad_ref[...] = cot_ref[...]
        left_grad_ref[...] = jnp.zeros_like(left_grad_ref)

    @pl.when(block * count < size)
    def _():
        row_i = lax.broadcasted_iota(jnp.int32, (count, length, width), 0) + block * count
        row_j = lax.broadcasted_iota(jnp.int32, (count, length, width), 1)
        kept = ((row_i < size) & (row_j < size)).reshape(rows, width)
        left = left_ref[0]
        right = right_ref[0]
        outer = (left[:, None, :] * right[None, :, :]).reshape(rows, width).astype(BF16)
        term = dot(outer, outer_w_ref[...])
        pair_one = pairs_ref[0].reshape(rows, width).astype(F32) + jnp.where(kept, term, 0.0)
        normed, inverse = norm_parts(pair_one)
        gain = gain_ref[...]
        low = (normed * gain).astype(BF16)
        both = dot(low, gate_up_ref[...]).astype(BF16)
        gate, up = both[:, :hidden], both[:, hidden:]
        act, slope = silu_parts(gate)
        hid = act * up
        pair_two = pair_one + jnp.where(kept, dot(hid, down_ref[...]), 0.0)
        pair_out_ref[0] = pair_two.astype(BF16).reshape(count, length, width)
        cot = cot_ref[0].reshape(rows, width)
        branch_grad = jnp.where(kept, cot, jnp.zeros((), BF16))
        acc_down[...] += dot_tn(branch_grad, hid)
        hid_grad = dot_nt(branch_grad, down_ref[...]).astype(BF16)
        gate_grad = hid_grad * (up * slope)
        up_grad = hid_grad * act
        acc_gate_up[:, :hidden] += dot_tn(low, gate_grad)
        acc_gate_up[:, hidden:] += dot_tn(low, up_grad)
        low_grad = dot_nt(gate_grad, gate_up_ref[:, :hidden]) + dot_nt(
            up_grad, gate_up_ref[:, hidden:]
        )
        acc_gain[...] += jnp.sum(low_grad * normed, 0, keepdims=True)
        one_grad = cot.astype(F32) + norm_back(normed, inverse, low_grad * gain)
        pair_grad_ref[0] = one_grad.astype(BF16).reshape(count, length, width)
        outer_grad = jnp.where(kept, one_grad, 0.0).astype(BF16)
        acc_outer[...] += dot_tn(outer, outer_grad)
        prod = dot_nt(outer_grad, outer_w_ref[...]).reshape(count, length, width)
        left_grad_ref[0] = jnp.sum(prod * right[None], 1)
        right_grad_ref[0] += jnp.sum(prod * left[:, None, :], 0)

    @pl.when((chain == pl.num_programs(0) - 1) & (block == pl.num_programs(1) - 1))
    def _():
        down = acc_down[...].T.astype(BF16)
        down = down.reshape(owners, 4, hidden // (4 * owners), width)
        down = [down[:, i].reshape(hidden // 4, width) for i in range(4)]
        wide = [acc_gate_up[...].astype(BF16), acc_outer[...].astype(BF16)] + down
        wide = jnp.concatenate(wide, 1)
        half = wide.shape[1] // 2

        @pl.when(place_ref[0] % 2 == 0)
        def _():
            keep_ref[...] = wide[:, :half]
            give_ref[...] = wide[:, half:]

        @pl.when(place_ref[0] % 2 == 1)
        def _():
            keep_ref[...] = wide[:, half:]
            give_ref[...] = wide[:, :half]

        g_gain_ref[...] = acc_gain[...]


def outer_back_kernel(
    lengths_ref,
    place_ref,
    left_grad_ref,
    right_grad_ref,
    weight_ref,
    gain_ref,
    second_out_ref,
    cot_ref,
    branch_ref,
    mod_ref,
    keep_ref,
    give_ref,
    g_gain_ref,
    second_grad_ref,
    gate_pre_ref,
):
    chains, width = mod_ref.shape[0], second_out_ref.shape[1]
    length = second_out_ref.shape[0] // chains
    sides = jnp.concatenate([left_grad_ref[...], right_grad_ref[...]], 1).astype(BF16)
    upstream = dot_nt(sides, weight_ref[...])
    normed, inverse = norm_parts(second_out_ref[...])
    g_gain_ref[...] = jnp.sum(upstream * normed, 0, keepdims=True)
    second_grad_ref[...] = cot_ref[...].astype(F32) + norm_back(
        normed, inverse, upstream * gain_ref[...]
    )
    for c in range(chains):
        rows = slice(c * length, (c + 1) * length)
        keep = keep_of(lengths_ref, c, length)
        gate = mod_ref[c : c + 1, 5 * width : 6 * width]
        grad = keep * second_grad_ref[rows]
        branch_grad = (gate * grad).astype(BF16)
        keep_ref[rows, :width] = branch_grad
        give_ref[rows, :width] = branch_grad
        gate_pre_ref[c : c + 1] = (
            jnp.sum(branch_ref[rows] * grad, 0, keepdims=True) * gate * (1.0 - gate)
        )
    half = sides.shape[1] // 2
    for x in range(2):

        @pl.when(place_ref[0] // 2 == x)
        def _(x=x):
            keep_ref[:, width:] = sides[:, x * half : (x + 1) * half]
            give_ref[:, width:] = sides[:, (1 - x) * half : (2 - x) * half]


def transition_back_kernel(
    own_ref,
    other_ref,
    across_ref,
    across_other_ref,
    gate_ref,
    up_ref,
    weight_ref,
    grads_ref,
    gate_grad_ref,
    up_grad_ref,
    mine_ref,
    theirs_ref,
):
    count = own_ref.shape[0]
    part = gate_ref.shape[1]
    for i, ref in enumerate((own_ref, other_ref, across_ref, across_other_ref)):
        grads_ref[i * count : (i + 1) * count] = ref[...]
    hid_grad = dot_nt(grads_ref[...], weight_ref[:, 2 * part :])
    act, slope = silu_parts(gate_ref[...].astype(F32))
    gate_grad = (hid_grad * up_ref[...].astype(F32) * slope).astype(BF16)
    up_grad = (hid_grad * act).astype(BF16)
    gate_grad_ref[...] = gate_grad
    up_grad_ref[...] = up_grad
    total = dot_nt(gate_grad, weight_ref[:, :part]) + dot_nt(
        up_grad, weight_ref[:, part : 2 * part]
    )
    mine_ref[...] = total[: 2 * count]
    theirs_ref[...] = total[2 * count :].astype(BF16)


def transition_grads_kernel(
    place_ref, rows_ref, hidden_ref, grads_ref, gate_grad_ref, up_grad_ref, *refs
):
    *out_refs, total = refs
    part = gate_grad_ref.shape[1]
    blocks = total.shape[:2] + (part,)
    rows = rows_ref[...]
    total[:, :, :part] = dot_tn(rows, gate_grad_ref[...]).astype(BF16).reshape(blocks)
    total[:, :, part : 2 * part] = dot_tn(rows, up_grad_ref[...]).astype(BF16).reshape(blocks)
    total[:, :, 2 * part :] = dot_tn(hidden_ref[...], grads_ref[...]).astype(BF16).reshape(blocks)
    ring = len(out_refs) // 2
    y, r = place_ref[1] % 2, place_ref[1] // 2
    for k in range(ring):
        at = 2 * lax.rem(r - 1 - k + 2 * ring, ring)
        out_refs[k][...] = total[at + 1 - y]
        out_refs[ring + k][...] = total[at + y]


def attention_back_kernel(
    heads,
    lengths_ref,
    place_ref,
    own_ref,
    across_ref,
    other_ref,
    mod_ref,
    first_out_ref,
    second_grad_ref,
    branch_ref,
    res_ref,
    qkv_ref,
    prob_ref,
    own_w_ref,
    other_w_ref,
    keep_ref,
    give_ref,
    scores_grad_ref,
    res_grad_ref,
    pre_ref,
    attended_grad,
    first_grad,
    branch_grad_ref,
    by_member,
):
    chains, length, width = res_ref.shape
    factor = 1.0 / math.sqrt(width // heads)
    mask = head_mask(heads, length, width)
    for c in range(chains):
        rows = slice(c * length, (c + 1) * length)
        keep = keep_of(lengths_ref, c, length)
        upstream = own_ref[rows] + across_ref[rows].astype(F32) + other_ref[rows].astype(F32)
        normed, inverse = norm_parts(first_out_ref[rows])
        pre_ref[c : c + 1, 3 * width : 4 * width] = jnp.sum(upstream * normed, 0, keepdims=True)
        pre_ref[c : c + 1, 4 * width : 5 * width] = jnp.sum(upstream, 0, keepdims=True)
        scale = mod_ref[c : c + 1, 3 * width : 4 * width]
        grad = second_grad_ref[rows] + norm_back(normed, inverse, upstream * (1.0 + scale))
        first_grad[rows] = grad
        gate = mod_ref[c : c + 1, 2 * width : 3 * width]
        kept = keep * grad
        branch_grad_ref[rows] = (gate * kept).astype(BF16)
        pre_ref[c : c + 1, 2 * width : 3 * width] = (
            jnp.sum(branch_ref[rows] * kept, 0, keepdims=True) * gate * (1.0 - gate)
        )
    for weight, member in members_of(place_ref, own_w_ref, other_w_ref):

        @pl.when(member == 3)
        def _(weight=weight):
            attended_grad[...] = dot_nt(branch_grad_ref[...], weight()).astype(BF16)

    for c in range(chains):
        rows = slice(c * length, (c + 1) * length)
        queries = spread_heads(qkv_ref[rows, :width], mask, heads)
        keys = qkv_ref[rows, width : 2 * width]
        value_rows = qkv_ref[rows, 2 * width :]
        upstream = spread_heads(attended_grad[rows], mask, heads)
        prob = prob_ref[c]
        prob_grad = dot_nt(upstream, value_rows)
        scores_grad = (
            prob * (prob_grad - jnp.sum(prob_grad * prob, -1, keepdims=True))
        ).astype(BF16)
        scores_grad_ref[c] = scores_grad
        query_grad = fold_heads(dot(scores_grad, keys), mask, heads) * factor
        key_grad = dot_tn(scores_grad, queries) * factor
        value_grad = dot_tn(prob.astype(BF16), upstream)
        by_member[0, rows] = query_grad.astype(BF16)
        by_member[1, rows] = key_grad.astype(BF16)
        by_member[2, rows] = value_grad.astype(BF16)
    blocks = [by_member[0], by_member[1], by_member[2], branch_grad_ref[...]]
    emit_members(place_ref, blocks, keep_ref, give_ref)
    by_member[3] = jnp.zeros((chains * length, width), BF16)
    first_in_grad = sum(
        dot_nt(by_member[member], weight())
        for weight, member in members_of(place_ref, own_w_ref, other_w_ref)
    )
    for c in range(chains):
        rows = slice(c * length, (c + 1) * length)
        upstream = first_in_grad[rows]
        normed, inverse = norm_parts(res_ref[c].astype(F32))
        pre_ref[c : c + 1, :width] = jnp.sum(upstream * normed, 0, keepdims=True)
        pre_ref[c : c + 1, width : 2 * width] = jnp.sum(upstream, 0, keepdims=True)
        scale = mod_ref[c : c + 1, :width]
        res_grad_ref[rows] = first_grad[rows] + norm_back(
            normed, inverse, upstream * (1.0 + scale)
        )


def attention_grads_kernel(
    place_ref,
    keep_in,
    got_in,
    keep_grad,
    got_grad,
    across_in,
    across_grad,
    outer_own,
    outer_other,
    outer_across,
    outer_both,
    side_own,
    side_other,
    side_across,
    side_both,
    *refs,
):
    *out_refs, total = refs
    core = place_ref[0] % 2
    width = outer_own.shape[1]
    lead = total.shape[:2]
    inputs = jnp.concatenate([keep_in[core], got_in[core], across_in[0], across_in[1]], 0)
    grads = jnp.concatenate([keep_grad[core], got_grad[core], across_grad[0], across_grad[1]], 0)
    total[:, :, :width] = dot_tn(inputs, grads).astype(BF16).reshape(lead + (width,))
    outer = (outer_own, outer_other, outer_across, outer_both)
    inputs = jnp.concatenate([ref[...] for ref in outer], 0)
    side = total.shape[2] - width
    cols = pl.ds(pl.multiple_of(width + core * side, 128), side)
    sides = (side_own, side_other, side_across, side_both)
    grads = jnp.concatenate([ref[:, cols] for ref in sides], 0)
    term = dot_tn(inputs, grads).astype(BF16)
    total[:, :, width:] = term.reshape(lead + (term.shape[1],))
    if out_refs:
        give_ref, keep_ref = out_refs
        ring = give_ref.shape[0]
        y, r = place_ref[1] % 2, place_ref[1] // 2
        for k in range(ring):
            at = 2 * lax.rem(r + k, ring)
            give_ref[k] = total[at + 1 - y]
            keep_ref[k] = total[at + y]


def pair_last_kernel(
    pairs_ref, one_grad_ref, scores_grad_ref, gain_ref, weight_ref, out_ref, g_weight_ref, g_gain_ref
):
    normed, inverse = norm_parts(pairs_ref[...].astype(F32))
    gain = gain_ref[...]
    low = (normed * gain).astype(BF16)
    scores_grad = scores_grad_ref[...]
    upstream = dot_tn(scores_grad, weight_ref[...])
    out_ref[...] = one_grad_ref[...].astype(F32) + norm_back(normed, inverse, upstream * gain)

    @pl.when(pl.program_id(0) == 0)
    def _():
        g_weight_ref[...] = jnp.zeros_like(g_weight_ref)
        g_gain_ref[...] = jnp.zeros_like(g_gain_ref)

    g_weight_ref[...] += dot(scores_grad, low)
    g_gain_ref[...] += jnp.sum(upstream * normed, 0, keepdims=True)


def on_device(
    n_dp,
    n_f,
    residues,
    pairs,
    lengths,
    time_bins,
    cath_labels,
    residue_cotangent,
    pair_cotangent,
    time_table,
    cath_table,
    attn_modulation,
    attn_gate,
    qkv_weight,
    bias_gain,
    bias_weight,
    out_weight,
    ffn_modulation,
    ffn_gate,
    gate_up,
    down_weight,
    outer_gain,
    outer_weight,
    outer_out,
    pair_gain,
    pair_gate_up,
    pair_down,
):
    place = Place(n_dp, n_f)
    d, f = place.d, place.f
    chains, length, width = residues.shape
    rows = chains * length
    heads = bias_weight.shape[1]
    pair_width = outer_out.shape[1]
    pair_rows = chains * length * length
    time_rows, cath_rows = time_table.shape[0], cath_table.shape[0]
    mod_rows = attn_modulation.shape[0]
    hid_rows = down_weight.shape[0]
    hid_part = hid_rows // 4
    part = hid_part * n_f
    place_ints = place.ints

    slots = Slots()

    lanes = pair_gate_up.shape[0]
    x_member = d + 2 - 4 * place.x
    attn_own, attn_x = [
        jnp.where(
            member == 3,
            out_weight,
            lax.dynamic_slice_in_dim(qkv_weight, jnp.minimum(member, 2) * width, width, 1),
        )
        for member in (d, x_member)
    ]
    attn_weights = slots.add(place.gather_shared(attn_own, attn_x, mod_rows, True))

    pair_list = (pair_gate_up, outer_weight, outer_out, pair_down)
    pair_cols = sum(w.size for w in pair_list) // lanes
    pair_cols = -(-pair_cols // 1024) * 256
    shared = pair_cols // 256 * lanes
    others_rows = shared + (2 * part + width) // 256 * mod_rows
    if mod_rows % 16 == 0 and lanes % 16 == 0:
        others_own, others_x = call_whole(
            functools.partial(pack_kernel, hid_rows, hid_part),
            "pack",
            3.0,
            [struct((others_rows, 256), BF16), struct((shared, 256), BF16)],
            place_ints,
            gate_up,
            down_weight,
            *pair_list,
            scratch=[pltpu.VMEM((lanes, 4 * pair_cols), BF16)],
        )
    else:

        def by_blocks(values):
            rows_of = values.shape[0]
            blocks = jnp.swapaxes(values.reshape(rows_of, -1, 256), 0, 1)
            return blocks.reshape(-1, 256)

        wide = [w.reshape(-1, lanes, w.shape[1]) for w in pair_list]
        wide = jnp.concatenate([w[i] for w in wide for i in range(w.shape[0])], 1)
        wide = jnp.pad(wide, ((0, 0), (0, 4 * pair_cols - wide.shape[1])))
        others_own, others_x = [
            by_blocks(lax.dynamic_slice_in_dim(wide, member * pair_cols, pair_cols, 1))
            for member in (d, x_member)
        ]
        mine = pick(gate_up.reshape(mod_rows, -1, 4, hid_part), d, 2).reshape(mod_rows, -1)
        mine = jnp.concatenate([mine, pick(down_weight.reshape(4, hid_part, width), d, 0)], 1)
        others_own = jnp.concatenate([others_own, by_blocks(mine)], 0)

    labels = jnp.stack([time_bins, cath_labels])
    labels, others_own, others_x = slots.step(
        (place.to_all_f, labels), beside=(others_own, others_x)
    )
    bins, labels = labels[:, 0].reshape(-1), labels[:, 1].reshape(-1)

    n_group = n_f * chains
    time_hot = (
        (bins[:, None] - f * time_rows) == jnp.arange(time_rows)[None, :]
    ).astype(BF16)
    cath_hot = (
        (labels[:, None] - f * cath_rows) == jnp.arange(cath_rows)[None, :]
    ).astype(BF16)
    condition = (dot(time_hot, time_table) + dot(cath_hot, cath_table)).astype(BF16)
    condition = jnp.swapaxes(condition.reshape(n_group, n_f, mod_rows), 0, 1)
    small_list = (bias_gain, pair_gain, outer_gain, bias_weight)
    small = jnp.concatenate([w.reshape(-1) for w in small_list])
    small_rows = -(-small.shape[0] // mod_rows)
    small = jnp.pad(small, (0, small_rows * mod_rows - small.shape[0]))
    small = jnp.broadcast_to(small.reshape(1, small_rows, mod_rows), (n_f, small_rows, mod_rows))
    (condition,) = slots.step((place.to_each_f, jnp.concatenate([condition, small], 1)))
    small = condition[:, n_group:].reshape(n_f, -1)
    cond_cols = jnp.sum(condition[:, :n_group].astype(F32), 0).astype(BF16)
    at = 0

    def take(weight):
        nonlocal at
        piece = small[:, at : at + weight.size].reshape((-1,) + weight.shape[1:])
        at += weight.size
        return piece

    bias_gain_row, pair_gain_row, outer_gain_row = [
        take(w).astype(F32)[None] for w in (bias_gain, pair_gain, outer_gain)
    ]
    bias_w_t = jnp.pad(take(bias_weight).T, ((0, 16 - heads), (0, 0)))

    pairs_flat = pairs.reshape(pair_rows, pair_width)
    block = 512
    bias = pl.pallas_call(
        bias_kernel,
        name="pair_bias",
        grid=(pair_rows // block,),
        in_specs=[
            pl.BlockSpec((block, pair_width), lambda i: (i, 0)),
            whole((1, pair_width)),
            whole((16, pair_width)),
        ],
        out_specs=pl.BlockSpec((16, block), lambda i: (0, i)),
        out_shape=struct((16, pair_rows), F32),
        cost_estimate=cost(6.0),
        compiler_params=params(),
    )(pairs_flat, bias_gain_row, bias_w_t)

    mod_weights = jnp.concatenate([attn_modulation, attn_gate, ffn_modulation, ffn_gate], 1)
    mods = dot(cond_cols, mod_weights).reshape(n_f, chains, 6 * width)
    first_mods, other_mods = mods[..., : 2 * width], mods[..., 2 * width :]
    first_mods, bias = slots.step((place.to_each_f, first_mods), beside=(bias,))
    ffn_weight = []

    def on_all_f(pieces):
        ffn_weight.append(place.assemble(pieces, shared, mod_rows))
        return ffn_weight

    other_weights = slots.add(
        place.gather_shared(others_own, others_x, lanes, False, on_all_f)
    )
    (other_mods,) = slots.step((place.to_each_f, other_mods.astype(BF16)))
    other_mods = other_mods.astype(F32)
    bias = bias[:heads].reshape(heads, chains, length, length)
    bias = jnp.transpose(bias, (1, 0, 2, 3)).reshape(chains, heads * length, length)
    mods = jnp.concatenate([jnp.sum(first_mods, 0), jnp.sum(other_mods, 0)], 1)
    gated = jnp.arange(6 * width)[None, :] // width
    mods = jnp.where((gated == 2) | (gated == 5), jax.nn.sigmoid(mods), mods)

    ((own_attn, other_attn),) = slots.finish(attn_weights)
    own_attn, other_attn = [w.reshape(2, width, width) for w in (own_attn, other_attn)]

    attention_out = call_whole(
        functools.partial(attention_kernel, heads),
        "attention",
        6.0,
        [
            struct((rows, width), BF16),
            struct((rows, 3 * width), BF16),
            struct((chains, heads * length, length), F32),
            struct((rows, width), BF16),
            struct((rows, width), F32),
            struct((rows, width), F32),
            struct((rows, width), BF16),
        ],
        lengths,
        place_ints,
        residues,
        mods,
        own_attn,
        other_attn,
        bias,
        scratch=[pltpu.VMEM((4, rows, width), BF16)],
    )

    attention_out = slots.step(beside=attention_out)
    first_in, qkv, prob, attended, first_branch, first_out, second_in = attention_out
    other_rows, across_rows = slots.step((place.swap_x, second_in), (place.swap_core, second_in))
    (across_other_rows,) = slots.step((place.swap_core, other_rows))
    ffn_weight = ffn_weight[0].reshape(width, -1)
    transition_out = call_whole(
        transition_kernel,
        "transition",
        5.0,
        [
            struct((4 * rows, width), BF16),
            struct((4 * rows, part), BF16),
            struct((4 * rows, part), BF16),
            struct((4 * rows, part), BF16),
            struct((2 * rows, width), F32),
            struct((2 * rows, width), BF16),
        ],
        second_in,
        other_rows,
        across_rows,
        across_other_rows,
        ffn_weight,
    )
    back_small = jnp.concatenate(
        [bins.astype(F32)[:, None], labels.astype(F32)[:, None], cond_cols.astype(F32)], 1
    )
    other_small, *transition_out = slots.step((place.swap_x, back_small), beside=transition_out)
    rows_all, gate, up, hidden, mine, theirs = transition_out
    back_small = ordered(place.x, back_small, other_small, 0)
    across, other_small = slots.step((place.swap_core, theirs), (place.swap_core, back_small))
    back_small = ordered(place.core, back_small, other_small, 1).reshape(n_dp * n_group, -1)
    bins_all = back_small[:, 0].astype(jnp.int32)
    labels_all = back_small[:, 1].astype(jnp.int32)
    cond_all = back_small[:, 2:].astype(BF16)
    ((own_pair, other_pair),) = slots.finish(other_weights)
    pair_shapes = [(n_f, w.shape[0] // lanes, lanes, w.shape[1]) for w in pair_list]
    if lanes % 16 == 0:
        pair_full = call_whole(
            unpack_kernel,
            "unpack",
            3.0,
            [struct(shape, BF16) for shape in pair_shapes],
            place_ints,
            own_pair,
            other_pair,
            scratch=[pltpu.VMEM((n_f, lanes, 4 * pair_cols), BF16)],
        )
    else:
        pair_full, at = [], 0
        wide = jnp.stack([own_pair, other_pair])
        wide = jnp.where(place.core == 0, wide, wide[::-1])
        wide = jnp.where(place.x == 0, wide, wide[:, ::-1])
        wide = jnp.transpose(wide, (2, 3, 1, 0, 4)).reshape(n_f, lanes, -1)
        for shape in pair_shapes:
            cols = shape[1] * shape[3]
            piece = wide[:, :, at : at + cols].reshape(n_f, lanes, shape[1], shape[3])
            pair_full.append(jnp.swapaxes(piece, 1, 2))
            at += cols
    branch_other, *pair_full = slots.step(
        (place.swap_x, (mine[rows:] + across[rows:].astype(F32)).astype(BF16)), beside=pair_full
    )
    pair_gate_up_full, outer_w_full, outer_out_full, pair_down_full = [
        w.reshape(-1, w.shape[3]) for w in pair_full
    ]
    half_rows = whole((rows, width))
    second_branch, second_out, res_out, outer_in, sides = call_whole(
        outer_kernel,
        "outer_sides",
        3.0,
        [
            struct((rows, width), F32),
            struct((rows, width), F32),
            struct((rows, width), BF16),
            struct((rows, width), BF16),
            struct((rows, 2 * pair_width), F32),
        ],
        lengths,
        first_out,
        mine,
        across,
        branch_other,
        mods,
        outer_gain_row,
        outer_w_full,
        blocks={2: half_rows, 3: half_rows},
    )

    keep_in = jnp.stack([first_in, jnp.where(place.x == 1, attended, first_in)])
    give_in = jnp.stack([first_in, jnp.where(place.x == 0, attended, first_in)])
    sides = sides.reshape(chains, length, 2 * pair_width)
    count = 16
    pair_hidden = pair_down_full.shape[0]
    wide_half = (3 * pair_hidden + pair_width) // 2
    pair_block = pl.BlockSpec((1, count, length, pair_width), lambda c, b: (c, b, 0, 0))
    pairs_done = pl.pallas_call(
        functools.partial(pair_kernel, n_f),
        name="pairs",
        grid=(chains, length // count),
        in_specs=[
            SMEM,
            SMEM,
            pl.BlockSpec((1, count, pair_width), lambda c, b: (c, b, 0)),
            pl.BlockSpec((1, length, pair_width), lambda c, b: (c, 0, 1)),
            pair_block,
            pair_block,
            whole((1, pair_width)),
            whole(outer_out_full.shape),
            whole((pair_width, 2 * pair_hidden)),
            whole(pair_down_full.shape),
        ],
        out_specs=[
            pair_block,
            pair_block,
            pl.BlockSpec((1, count, pair_width), lambda c, b: (c, b, 0)),
            pl.BlockSpec((1, length, pair_width), lambda c, b: (c, 0, 0)),
            whole((pair_width, wide_half)),
            whole((pair_width, wide_half)),
            whole((1, pair_width)),
        ],
        out_shape=[
            struct(pairs.shape, BF16),
            struct(pairs.shape, BF16),
            struct((chains, length, pair_width), F32),
            struct((chains, length, pair_width), F32),
            struct((pair_width, wide_half), BF16),
            struct((pair_width, wide_half), BF16),
            struct((1, pair_width), F32),
        ],
        scratch_shapes=[
            pltpu.VMEM((pair_width, 2 * pair_hidden), F32),
            pltpu.VMEM((pair_width, pair_hidden), F32),
            pltpu.VMEM((pair_width, pair_width), F32),
            pltpu.VMEM((1, pair_width), F32),
        ],
        cost_estimate=cost(35.0),
        compiler_params=params(),
    )(
        lengths,
        place_ints,
        sides,
        sides,
        pairs,
        pair_cotangent,
        pair_gain_row,
        outer_out_full,
        pair_gate_up_full,
        pair_down_full,
    )

    pair_out, pair_grad, left_grad, right_grad, keep_pair, give_pair, g_pair_gain = pairs_done

    def toward_core(keep, got):
        return jnp.stack([pick(keep, 1 - place.core, 0), pick(got, 1 - place.core, 0)])


    grads_keep, grads_give, g_outer_gain, second_grad, second_pre = call_whole(
        outer_back_kernel,
        "outer_sides_back",
        3.0,
        [
            struct((rows, width + pair_width), BF16),
            struct((rows, width + pair_width), BF16),
            struct((1, width), F32),
            struct((rows, width), F32),
            struct((chains, width), F32),
        ],
        lengths,
        place_ints,
        left_grad.reshape(rows, pair_width),
        right_grad.reshape(rows, pair_width),
        outer_w_full,
        outer_gain_row,
        second_out,
        residue_cotangent.reshape(rows, width),
        second_branch,
        mods,
    )

    grads_other, across_pair, grads_across = slots.step(
        (place.swap_x, grads_give), (place.swap_core, give_pair), (place.swap_core, grads_keep)
    )
    pair_parts = place.parts_ring(
        *(a.reshape(place.ring, 2, lanes, wide_half) for a in (keep_pair, across_pair))
    )
    grads_both, *pair_parts = slots.step((place.swap_core, grads_other), beside=pair_parts)
    transition_back_out = call_whole(
        transition_back_kernel,
        "transition_back",
        6.0,
        [
            struct((4 * rows, width), BF16),
            struct((4 * rows, part), BF16),
            struct((4 * rows, part), BF16),
            struct((2 * rows, width), F32),
            struct((2 * rows, width), BF16),
        ],
        grads_keep,
        grads_other,
        grads_across,
        grads_both,
        gate,
        up,
        ffn_weight,
        blocks={i: half_rows for i in range(4)},
    )
    grads_all, gate_grad, up_grad, mine, theirs = transition_back_out
    (across,) = slots.step((place.swap_core, theirs))

    def chunk_call(kernel, name, micros, shape, outs, split, *operands):
        if shape[0] % 16 == 0:
            return call_whole(
                kernel,
                name,
                micros,
                [struct(o, BF16) for o in outs],
                place_ints,
                *operands,
                scratch=[pltpu.VMEM((n_f,) + shape, BF16)],
            )
        (total,) = call_whole(
            kernel,
            name,
            micros,
            [struct((1, n_f * shape[0], shape[1]), BF16)],
            place_ints,
            *operands,
        )
        return split(total.reshape((n_f,) + shape))

    shape = (mod_rows, 2 * part + width)
    ffn_chunks = chunk_call(
        transition_grads_kernel,
        "transition_grads",
        5.0,
        shape,
        [shape] * (2 * place.ring),
        place.chunks,
        rows_all,
        hidden,
        grads_all,
        gate_grad,
        up_grad,
    )
    pair_sums = slots.add(place.reduce_pair(*pair_parts))
    other, *ffn_chunks = slots.step(
        (place.swap_x, (mine[rows:] + across[rows:].astype(F32)).astype(BF16)), beside=ffn_chunks
    )
    ffn_sums = slots.add(place.reduce_f(ffn_chunks[: place.ring], ffn_chunks[place.ring :]))

    attention_back_out = call_whole(
        functools.partial(attention_back_kernel, heads),
        "attention_back",
        9.0,
        [
            struct((2, rows, width), BF16),
            struct((2, rows, width), BF16),
            struct((chains, heads * length, length), BF16),
            struct((rows, width), F32),
            struct((chains, 5 * width), F32),
        ],
        lengths,
        place_ints,
        mine,
        across,
        other,
        mods,
        first_out,
        second_grad,
        first_branch,
        residues,
        qkv,
        prob,
        own_attn,
        other_attn,
        blocks={2: half_rows, 3: half_rows},
        scratch=[
            pltpu.VMEM((rows, width), BF16),
            pltpu.VMEM((rows, width), F32),
            pltpu.VMEM((rows, width), BF16),
            pltpu.VMEM((4, rows, width), BF16),
        ],
    )
    got_in, outer_other, outer_across, *attention_back_out = slots.step(
        (place.swap_x, give_in),
        (place.swap_x, outer_in),
        (place.swap_core, outer_in),
        beside=attention_back_out,
    )
    keep_grad, give_grad, scores_grad, res_grad, pre = attention_back_out

    pre = jnp.concatenate([pre, second_pre], 1).astype(BF16)
    scores_t = jnp.transpose(
        scores_grad.reshape(chains, heads, length, length), (1, 0, 2, 3)
    ).reshape(heads, pair_rows)
    scores_t = jnp.pad(scores_t, ((0, 16 - heads), (0, 0)))
    pairs_grad, g_bias_w, g_bias_gain = pl.pallas_call(
        pair_last_kernel,
        name="pairs_last",
        grid=(pair_rows // block,),
        in_specs=[
            pl.BlockSpec((block, pair_width), lambda i: (i, 0)),
            pl.BlockSpec((block, pair_width), lambda i: (i, 0)),
            pl.BlockSpec((16, block), lambda i: (0, i)),
            whole((1, pair_width)),
            whole((16, pair_width)),
        ],
        out_specs=[
            pl.BlockSpec((block, pair_width), lambda i: (i, 0)),
            whole((16, pair_width)),
            whole((1, pair_width)),
        ],
        out_shape=[
            struct((pair_rows, pair_width), F32),
            struct((16, pair_width), F32),
            struct((1, pair_width), F32),
        ],
        cost_estimate=cost(9.0),
        compiler_params=params(),
    )(pairs_flat, pair_grad.reshape(pair_rows, pair_width), scores_t, bias_gain_row, bias_w_t)

    got_grad, across_in, pairs_grad, g_bias_w, g_bias_gain = slots.step(
        (place.swap_x, give_grad),
        (place.swap_core, toward_core(keep_in, got_in)),
        beside=(pairs_grad, g_bias_w, g_bias_gain),
    )
    across_grad, outer_both, pre_group = slots.step(
        (place.swap_core, toward_core(keep_grad, got_grad)),
        (place.swap_core, outer_other),
        (place.to_all_f, pre),
    )

    small_terms = jnp.concatenate(
        [g_bias_w[:heads], g_bias_gain, g_pair_gain, g_outer_gain.reshape(-1, pair_width)], 0
    )
    pre_group = pre_group.reshape(n_group, 6 * width)
    cond_grad = dot_nt(pre_group, mod_weights)
    small_shape, small_rows = small_terms.shape, -(-small_terms.size // mod_rows)
    small_terms = jnp.pad(
        small_terms.reshape(-1), (0, small_rows * mod_rows - small_terms.size)
    ).reshape(small_rows, mod_rows)
    packed = jnp.concatenate([cond_grad, small_terms], 0).astype(BF16)
    shape = (mod_rows, width + pair_width // 2)
    attn_chunks = chunk_call(
        attention_grads_kernel,
        "attention_grads",
        4.0,
        shape,
        [(place.ring,) + shape] * 2,
        place.chunks_by_distance,
        keep_in,
        got_in,
        keep_grad,
        got_grad,
        across_in,
        across_grad,
        outer_in,
        outer_other,
        outer_across,
        outer_both,
        grads_keep,
        grads_other,
        grads_across,
        grads_both,
    )
    packed, pre_other, *attn_chunks = slots.step(
        (place.to_all_f, packed), (place.swap_x, pre_group), beside=attn_chunks
    )
    attn_sums = slots.add(place.reduce_direct(*attn_chunks))
    pre_all = ordered(place.x, pre_group, pre_other, 0)
    packed = jnp.concatenate(
        [
            packed[:, :n_group].reshape(-1, mod_rows),
            jnp.sum(packed[:, n_group:].astype(F32), 0).astype(BF16),
        ],
        0,
    )
    cond_rows = n_f * n_group
    pre_other, packed_x = slots.step((place.swap_core, pre_all), (place.swap_x, packed))
    pre_all = ordered(place.core, pre_all, pre_other, 1).reshape(n_dp * n_group, 6 * width)
    packed = jnp.stack([packed, packed_x])
    packed_core, g_mods = slots.step(
        (place.swap_core, packed), beside=(dot_tn(cond_all, pre_all),)
    )
    packed = jnp.stack([packed, packed_core])
    small_terms = jnp.sum(packed[:, :, cond_rows:].astype(F32), (0, 1)).reshape(-1)
    small_terms = small_terms[: math.prod(small_shape)].reshape(small_shape)
    cond_grad = jnp.where(place.core == 0, packed, packed[::-1])[:, :, :cond_rows]
    cond_grad = jnp.where(place.x == 0, cond_grad, cond_grad[:, ::-1])
    cond_grad = cond_grad.reshape(2, 2, n_f, n_group, mod_rows)
    cond_grad = jnp.transpose(cond_grad, (1, 0, 3, 2, 4)).reshape(n_dp * n_group, width)
    time_all = (
        (bins_all[:, None] - f * time_rows) == jnp.arange(time_rows)[None, :]
    ).astype(BF16)
    cath_all = (
        (labels_all[:, None] - f * cath_rows) == jnp.arange(cath_rows)[None, :]
    ).astype(BF16)
    out_time = dot_tn(time_all, cond_grad)
    out_cath = dot_tn(cath_all, cond_grad)

    bias_rows = bias_weight.shape[0]
    small_own = lax.dynamic_slice_in_dim(small_terms, f * bias_rows, bias_rows, 1)
    outer_own = lax.dynamic_slice_in_dim(
        small_terms[heads + 2 :].reshape(-1), f * mod_rows, mod_rows, 0
    )
    small_outs = (out_time, out_cath, small_own[:heads].T, small_own[heads:], outer_own)
    out_time, out_cath, out_bias_w, small_own, out_outer_gain = slots.step(beside=small_outs)
    out_bias_gain, out_pair_gain = small_own[0], small_own[1]
    ffn_sums, attn_sums, pair_sums = slots.finish(ffn_sums, attn_sums, pair_sums)
    (
        out_gate_up,
        out_down,
        out_qkv,
        out_out,
        out_outer_w,
        out_pair_gate_up,
        out_outer_out,
        out_pair_down,
    ) = call_whole(
        functools.partial(finish_kernel, hid_part),
        "finish",
        6.0,
        [
            struct(w.shape, F32)
            for w in (
                gate_up,
                down_weight,
                qkv_weight,
                out_weight,
                outer_weight,
                pair_gate_up,
                outer_out,
                pair_down,
            )
        ],
        place_ints,
        *ffn_sums,
        *attn_sums,
        *pair_sums,
        scratch=[
            pltpu.VMEM((n,) + sums[0].shape, BF16)
            for n, sums in ((4, ffn_sums), (4, attn_sums), (2, pair_sums))
        ],
    )

    return (
        res_out.reshape(residues.shape),
        pair_out,
        res_grad.reshape(residues.shape),
        pairs_grad.reshape(pairs.shape),
        out_time,
        out_cath,
        g_mods[:, : 2 * width],
        g_mods[:, 2 * width : 3 * width],
        out_qkv,
        out_bias_gain,
        out_bias_w,
        out_out,
        g_mods[:, 3 * width : 5 * width],
        g_mods[:, 5 * width :],
        out_gate_up,
        out_down,
        out_outer_gain,
        out_outer_w,
        out_outer_out,
        out_pair_gain,
        out_pair_gate_up,
        out_pair_down,
    )


def solution(mesh):
    chains3 = P(("dp", "fsdp"), None, None)
    chains4 = P(("dp", "fsdp"), None, None, None)
    chains1 = P(("dp", "fsdp"))
    table = P("fsdp", None)
    line = P("fsdp")
    weights = (
        table,
        table,
        table,
        table,
        table,
        line,
        table,
        table,
        table,
        table,
        table,
        table,
        line,
        table,
        table,
        line,
        table,
        table,
    )
    return jax.shard_map(
        functools.partial(on_device, mesh.shape["dp"], mesh.shape["fsdp"]),
        mesh=mesh,
        in_specs=(chains3, chains4, chains1, chains1, chains1, chains3, chains4) + weights,
        out_specs=(chains3, chains4, chains3, chains4) + weights,
        check_vma=False,
    )
```

```python
import functools
import math

import jax
import jax.numpy as jnp
from jax import lax
from jax.experimental import pallas as pl
from jax.experimental.pallas import tpu as pltpu
from jax.sharding import PartitionSpec as P

EPSILON = 1e-05
F32 = jnp.float32
BF16 = jnp.bfloat16
VMEM_LIMIT = 56 * 1024 * 1024


def norm_parts(values):
    center = values - jnp.mean(values, -1, keepdims=True)
    inverse = lax.rsqrt(jnp.mean(center * center, -1, keepdims=True) + EPSILON)
    return center * inverse, inverse


def norm_back(normed, inverse, upstream):
    return inverse * (
        upstream
        - jnp.mean(upstream, -1, keepdims=True)
        - normed * jnp.mean(upstream * normed, -1, keepdims=True)
    )


def dot(left, right):
    return jnp.dot(left, right, preferred_element_type=F32)


def dot_nt(left, right):
    return lax.dot_general(left, right, (((1,), (1,)), ((), ())), preferred_element_type=F32)


def dot_tn(left, right):
    return lax.dot_general(left, right, (((0,), (0,)), ((), ())), preferred_element_type=F32)


def params():
    return pltpu.CompilerParams(vmem_limit_bytes=VMEM_LIMIT)


def cost(micros):
    return pl.CostEstimate(flops=int(micros * 1e9), bytes_accessed=0, transcendentals=0)


def whole(shape):
    return pl.BlockSpec(shape, lambda *_: (0,) * len(shape))


SMEM = pl.BlockSpec(memory_space=pltpu.SMEM)


def call_whole(kernel, name, micros, outs, *operands, blocks=None, scratch=()):
    blocks = blocks or {}
    specs = [
        blocks.get(i, SMEM if a.dtype == jnp.int32 else whole(a.shape))
        for i, a in enumerate(operands)
    ]
    return pl.pallas_call(
        kernel,
        grid=(1,),
        name=name,
        in_specs=specs,
        out_specs=[whole(o.shape) for o in outs],
        out_shape=outs,
        scratch_shapes=list(scratch),
        cost_estimate=cost(micros),
        compiler_params=params(),
    )(*operands)


def struct(shape, dtype):
    return jax.ShapeDtypeStruct(shape, dtype)


def swap(values, axis, size, bit):
    return lax.ppermute(values, axis, [(i, i ^ bit) for i in range(size)])


def pick(values, index, axis):
    return lax.dynamic_index_in_dim(values, index, axis, keepdims=False)


def ordered(bit, own, other, axis):
    first = jnp.where(bit == 0, own, other)
    second = jnp.where(bit == 0, other, own)
    return jnp.stack([first, second], axis)


class Place:
    def __init__(self, n_dp, n_f):
        self.n_dp, self.n_f, self.ring = n_dp, n_f, n_f // 2
        self.d = lax.axis_index("dp")
        self.f = lax.axis_index("fsdp")
        self.core, self.x = self.d % 2, self.d // 2
        self.y, self.r = self.f % 2, self.f // 2
        self.ints = jnp.stack([self.d, self.f]).astype(jnp.int32)

    def swap_core(self, values):
        return swap(values, "dp", self.n_dp, 1)

    def swap_x(self, values):
        return swap(values, "dp", self.n_dp, 2)

    def swap_y(self, values):
        return swap(values, "fsdp", self.n_f, 1)

    def shift_ring(self, values):
        return lax.ppermute(
            values, "fsdp", [(i, (i + 2) % self.n_f) for i in range(self.n_f)]
        )

    def to_each_f(self, values):
        return lax.all_to_all(values, "fsdp", split_axis=0, concat_axis=0, tiled=True)

    def to_all_f(self, values):
        return self.to_each_f(jnp.broadcast_to(values[None], (self.n_f,) + values.shape))


    def gather(self, piece, shared, x_own, on_all_f):
        ring = self.ring
        moving, last, pieces, from_x = piece, None, [], []
        for k in range(ring + 1):
            moves, beside = [], ()
            if k < ring:
                moves.append((self.swap_y, moving))
            if k < ring - 1:
                moves.append((self.shift_ring, moving))
            if k == ring and on_all_f:
                beside = on_all_f(pieces)
            if k > 0:
                both = [p[:shared] for p in last]
                moves.append((self.swap_x, both[1] if k == 1 else jnp.stack(both)))
            got = yield moves, beside
            if k > 0:
                from_x.append(got[-1])
            if k < ring:
                last = [moving, got[0]]
                pieces += last
            if k < ring - 1:
                moving = got[1]
        return pieces, [x_own] + from_x

    def gather_cores(self, pieces, from_x, rows, urgent):
        held = self.assemble(pieces, 0, rows, from_x)
        if not urgent:
            yield [], (held,)
        (other,) = yield [(self.swap_core, held)]
        return held, other

    def gather_shared(self, piece, x_own, rows, urgent, on_all_f=None):
        shared = x_own.shape[0]
        pieces, from_x = yield from self.gather(piece, shared, x_own, on_all_f)
        return (yield from self.gather_cores(pieces, from_x, rows, urgent))

    def assemble(self, pieces, first, rows, from_x=()):
        width = pieces[0].shape[1]
        last = from_x[0].shape[0] if from_x else pieces[0].shape[0]
        blocks = (last - first) // rows
        if rows % 16 == 0:
            lead = (2,) if from_x else ()
            take = pl.BlockSpec((last, width), lambda *_: (0, 0))
            (held,) = call_whole(
                functools.partial(assemble_kernel, self.ring, first, rows, blocks, bool(from_x)),
                "assemble",
                3.0,
                [struct(lead + (self.n_f, rows, blocks * width), pieces[0].dtype)],
                self.ints,
                *pieces,
                *from_x,
                blocks={1 + i: take for i in range(len(pieces))},
            )
            return held
        order = (self.r - jnp.arange(self.ring)) % self.ring

        def placed(pairs):
            steps = jnp.stack([ordered(self.y, own, other, 0) for own, other in pairs])
            steps = jnp.take(steps, order, 0)[:, :, first:last]
            steps = steps.reshape(self.n_f, blocks, rows, width)
            return jnp.swapaxes(steps, 1, 2).reshape(self.n_f, rows, blocks * width)

        held = placed(list(zip(pieces[0::2], pieces[1::2])))
        if not from_x:
            return held
        pairs = [(from_x[0], from_x[1])] + [(both[0], both[1]) for both in from_x[2:]]
        return jnp.stack([held, placed(pairs)])

    def add(self, keep, got):
        return (keep.astype(F32) + got.astype(F32)).astype(BF16)

    def chunks(self, values):
        give, keep = [], []
        values = values.reshape((self.ring, 2) + values.shape[1:])
        for k in range(self.ring):
            chunk = pick(values, (self.r - 1 - k) % self.ring, 0)
            give.append(pick(chunk, 1 - self.y, 0))
            keep.append(pick(chunk, self.y, 0))
        return tuple(give + keep)

    def reduce_f(self, give, keep):
        moving = None
        for k in range(self.ring):
            moves = [(self.swap_y, give[k])]
            if k > 0:
                moves.append((self.shift_ring, moving))
            got = yield moves
            total = keep[k].astype(F32)
            for other in got:
                total = total + other.astype(F32)
            moving = total.astype(BF16)
        return (yield from self.spread_d(moving))

    def chunks_by_distance(self, values):
        values = values.reshape((self.ring, 2) + values.shape[1:])
        order = (self.r + jnp.arange(self.ring)) % self.ring
        return tuple(jnp.take(pick(values, i, 1), order, 0) for i in (1 - self.y, self.y))

    def reduce_direct(self, give, keep):
        ring = self.ring
        (got,) = yield [(self.swap_y, give)]
        total, *parts = [self.add(keep[k], got[k]) for k in range(ring)]

        def shift(values, distance):
            pairs = [(i, (i + 2 * distance) % self.n_f) for i in range(self.n_f)]
            return lax.ppermute(values, "fsdp", pairs)

        got = yield [
            (functools.partial(shift, distance=k + 1), part) for k, part in enumerate(parts)
        ]
        total = total.astype(F32)
        for other in got:
            total = total + other.astype(F32)
        return (yield from self.spread_d(total.astype(BF16)))

    def parts_ring(self, mine, across):
        order = [(self.r - 1 - k) % self.ring for k in range(self.ring)]
        return tuple(self.add(pick(mine, at, 0), pick(across, at, 0)) for at in order)

    def reduce_pair(self, *chunks):
        moving = chunks[0]
        for k, chunk in enumerate(chunks[1:]):
            if k == 2:
                yield []
                yield []
                yield []
            got = yield [(self.shift_ring, moving)]
            moving = self.add(chunk, got[0])
        got = yield [(self.swap_y, pick(moving, 1 - self.y, 0))]
        moving = self.add(pick(moving, self.y, 0), got[0])
        got = yield [(self.swap_x, moving)]
        moving = self.add(moving, got[0])
        got = yield [(self.swap_core, moving)]
        return moving, got[0]

    def spread_d(self, values):
        (other,) = yield [(self.swap_x, values)]
        (across,) = yield [(self.swap_core, jnp.stack([values, other]))]
        return values, other, across


class Chain:
    def __init__(self, moves):
        self.moves, self.result, self.done = moves, None, False
        self.pending, self.beside = [], ()
        self.advance(None)

    def advance(self, got):
        try:
            asked = self.moves.send(got)
            self.pending, self.beside = asked if isinstance(asked, tuple) else (asked, ())
        except StopIteration as stop:
            self.result, self.done = stop.value, True
            self.pending, self.beside = [], ()


class Slots:
    def __init__(self):
        self.chains, self.token = [], None

    def add(self, moves):
        chain = Chain(moves)
        self.chains.append(chain)
        return chain

    def step(self, *extra, beside=()):
        moves, all_beside = [], list(beside)
        for chain in self.chains:
            moves += chain.pending
            all_beside += chain.beside
        moves += extra
        if not moves:
            return tuple(beside)
        values = tuple(value for _, value in moves)
        if self.token is not None:
            values = lax.optimization_barrier((values, self.token))[0]
        got = [move(value) for (move, _), value in zip(moves, values)]
        got, all_beside = lax.optimization_barrier((tuple(got), tuple(all_beside)))
        self.token = got[0]
        at = 0
        for chain in self.chains:
            count = len(chain.pending)
            chain.advance(list(got[at : at + count]))
            at += count
        self.chains = [chain for chain in self.chains if not chain.done]
        return got[at:] + all_beside[: len(beside)]

    def finish(self, *chains):
        while not all(chain.done for chain in chains):
            self.step()
        return [chain.result for chain in chains]


def assemble_kernel(ring, first, rows, blocks, shared, place_ref, *refs):
    *pieces, out_ref = refs
    y, r = place_ref[1] % 2, place_ref[1] // 2
    width = pieces[0].shape[-1]
    pairs = [(pieces[2 * k], (), pieces[2 * k + 1], ()) for k in range(ring)]
    planes = [pairs]
    if shared:
        x_own, x_first, *both = pieces[2 * ring :]
        planes.append([(x_own, (), x_first, ())] + [(ref, (0,), ref, (1,)) for ref in both])
    for plane, pairs in enumerate(planes):
        lead = (plane,) if shared else ()
        for k, (own, own_at, other, other_at) in enumerate(pairs):
            at = 2 * lax.rem(r - k + ring, ring)
            for b in range(blocks):
                cols = slice(b * width, (b + 1) * width)
                span = slice(first + b * rows, first + (b + 1) * rows)
                out_ref[lead + (at + y, slice(None), cols)] = own[own_at + (span,)]
                out_ref[lead + (at + 1 - y, slice(None), cols)] = other[other_at + (span,)]


def member_other(d):
    return d + 2 - 4 * (d // 2), 1 - 2 * (d % 2)


def pack_kernel(
    group,
    part,
    place_ref,
    gate_up_ref,
    down_ref,
    pair_gate_up_ref,
    outer_w_ref,
    outer_out_ref,
    pair_down_ref,
    own_ref,
    x_ref,
    wide,
):
    d = place_ref[0]
    lanes = wide.shape[0]
    at = 0
    for ref in (pair_gate_up_ref, outer_w_ref, outer_out_ref, pair_down_ref):
        for i in range(ref.shape[0] // lanes):
            wide[:, at : at + ref.shape[1]] = ref[i * lanes : (i + 1) * lanes]
            at += ref.shape[1]
    wide[:, at:] = jnp.zeros((lanes, wide.shape[1] - at), BF16)
    span = wide.shape[1] // 4
    for member, out_ref in ((d, own_ref), (member_other(d)[0], x_ref)):
        mine = wide[:, pl.ds(pl.multiple_of(member * span, 128), span)]
        for b in range(span // 256):
            out_ref[b * lanes : (b + 1) * lanes] = mine[:, b * 256 : (b + 1) * 256]
    first = span // 256 * lanes
    rows = gate_up_ref.shape[0]
    groups = gate_up_ref.shape[1] // group
    for m in range(4):

        @pl.when(d == m)
        def _(m=m):
            cols = [
                gate_up_ref[:, g * group + m * part : g * group + (m + 1) * part].astype(F32)
                for g in range(groups)
            ]
            mine = jnp.concatenate(cols, 1).astype(BF16)
            mine = jnp.concatenate([mine, down_ref[m * part : (m + 1) * part]], 1)
            for b in range(mine.shape[1] // 256):
                at = first + b * rows
                own_ref[at : at + rows] = mine[:, b * 256 : (b + 1) * 256]


def unpack_kernel(place_ref, own_ref, other_ref, *refs):
    *out_refs, wide = refs
    d = place_ref[0]
    x, toward = member_other(d)
    span = own_ref.shape[3]
    for ref, i, member in (
        (own_ref, 0, d),
        (own_ref, 1, x),
        (other_ref, 0, d + toward),
        (other_ref, 1, x + toward),
    ):
        wide[:, :, pl.ds(pl.multiple_of(member * span, 128), span)] = ref[i]
    at = 0
    for ref in out_refs:
        width = ref.shape[3]
        for i in range(ref.shape[1]):
            ref[:, i] = wide[:, :, at : at + width]
            at += width


def put_members(place_ref, pieces, held):
    d = place_ref[0]
    x, toward = member_other(d)
    held[d] = pieces[0][...]
    held[x] = pieces[1][...]
    held[d + toward] = pieces[2][0]
    held[x + toward] = pieces[2][1]


def finish_kernel(part, place_ref, *refs):
    gate_up_ref, down_ref, qkv_ref, out_ref, outer_w_ref = refs[8:13]
    pair_gate_up_ref, outer_out_ref, pair_down_ref, held, attn_held, pair_held = refs[13:]
    put_members(place_ref, refs[:3], held)
    put_members(place_ref, refs[3:6], attn_held)
    core = place_ref[0] % 2
    pair_held[core] = refs[6][...]
    pair_held[1 - core] = refs[7][...]
    count = down_ref.shape[0] // 4
    quarter = gate_up_ref.shape[1] // 4
    width = out_ref.shape[1]
    side = outer_w_ref.shape[1] // 4
    for m in range(4):
        down_ref[m * count : (m + 1) * count] = held[m][:, quarter:].astype(F32)
        if m < 3:
            qkv_ref[:, m * width : (m + 1) * width] = attn_held[m][:, :width].astype(F32)
        else:
            out_ref[...] = attn_held[m][:, :width].astype(F32)
        outer_w_ref[:, m * side : (m + 1) * side] = attn_held[m][:, width:].astype(F32)
    for start in range(0, quarter, part):
        both = [held[m][:, start : start + part].astype(F32) for m in range(4)]
        gate_up_ref[:, 4 * start : 4 * (start + part)] = jnp.concatenate(both, 1)
    lanes = pair_held.shape[1]
    hidden2, pair_width = pair_gate_up_ref.shape[1], outer_out_ref.shape[1]
    wide = jnp.concatenate([pair_held[0], pair_held[1]], 1).astype(F32)
    pair_gate_up_ref[...] = wide[:, :hidden2]
    outer_out_ref[...] = wide[:, hidden2 : hidden2 + pair_width]
    for block in range(4):
        start = hidden2 + (1 + block) * pair_width
        pair_down_ref[block * lanes : (block + 1) * lanes] = wide[:, start : start + pair_width]


def bias_kernel(pairs_ref, gain_ref, weight_ref, out_ref):
    normed, _ = norm_parts(pairs_ref[...].astype(F32))
    low = (normed * gain_ref[...]).astype(BF16)
    out_ref[...] = dot_nt(weight_ref[...], low)


def head_mask(heads, length, width):
    row = lax.broadcasted_iota(jnp.int32, (heads * length, 1), 0) // length
    col = lax.broadcasted_iota(jnp.int32, (1, width), 1) // (width // heads)
    return row == col


def spread_heads(rows, mask, heads):
    return jnp.where(mask, jnp.concatenate([rows] * heads, 0), jnp.zeros((), rows.dtype))


def fold_heads(wide, mask, heads):
    kept = jnp.where(mask, wide, 0.0)
    return jnp.sum(kept.reshape(heads, wide.shape[0] // heads, wide.shape[1]), 0)


def keep_of(lengths_ref, chain, length):
    row = lax.broadcasted_iota(jnp.int32, (length, 1), 0)
    return (row < lengths_ref[chain]).astype(F32)


def members_of(place_ref, own_ref, other_ref):
    d = place_ref[0]
    x, toward = member_other(d)
    return (
        (lambda: own_ref[0], d),
        (lambda: own_ref[1], x),
        (lambda: other_ref[0], d + toward),
        (lambda: other_ref[1], x + toward),
    )


def attention_kernel(
    heads,
    lengths_ref,
    place_ref,
    res_ref,
    mod_ref,
    own_w_ref,
    other_w_ref,
    bias_ref,
    first_in_ref,
    qkv_ref,
    prob_ref,
    attended_ref,
    branch_ref,
    first_out_ref,
    second_in_ref,
    by_member,
):
    chains, length, width = res_ref.shape
    factor = 1.0 / math.sqrt(width // heads)
    mask = head_mask(heads, length, width)
    for c in range(chains):
        rows = slice(c * length, (c + 1) * length)
        normed, _ = norm_parts(res_ref[c].astype(F32))
        scale = mod_ref[c : c + 1, :width]
        shift = mod_ref[c : c + 1, width : 2 * width]
        first_in_ref[rows] = (normed * (1.0 + scale) + shift).astype(BF16)
    for weight, member in members_of(place_ref, own_w_ref, other_w_ref):
        by_member[member] = dot(first_in_ref[...], weight()).astype(BF16)
    for m in range(3):
        qkv_ref[:, m * width : (m + 1) * width] = by_member[m]
    for c in range(chains):
        rows = slice(c * length, (c + 1) * length)
        queries = spread_heads(qkv_ref[rows, :width], mask, heads)
        keys = qkv_ref[rows, width : 2 * width]
        value_rows = qkv_ref[rows, 2 * width :]
        scores = dot_nt(queries, keys) * factor + bias_ref[c]
        column = lax.broadcasted_iota(jnp.int32, scores.shape, 1)
        scores = jnp.where(column < lengths_ref[c], scores, -1000000000.0)
        exps = jnp.exp(scores - jnp.max(scores, -1, keepdims=True))
        prob = exps / jnp.sum(exps, -1, keepdims=True)
        prob_ref[c] = prob
        wide = dot(prob.astype(BF16), value_rows)
        attended_ref[rows] = fold_heads(wide, mask, heads).astype(BF16)
    for weight, member in members_of(place_ref, own_w_ref, other_w_ref):

        @pl.when(member == 3)
        def _(weight=weight):
            branch_ref[...] = dot(attended_ref[...], weight())

    for c in range(chains):
        rows = slice(c * length, (c + 1) * length)
        keep = keep_of(lengths_ref, c, length)
        gate = mod_ref[c : c + 1, 2 * width : 3 * width]
        first_out = res_ref[c].astype(F32) + keep * gate * branch_ref[rows]
        first_out_ref[rows] = first_out
        normed, _ = norm_parts(first_out)
        scale = mod_ref[c : c + 1, 3 * width : 4 * width]
        shift = mod_ref[c : c + 1, 4 * width : 5 * width]
        second_in_ref[rows] = (normed * (1.0 + scale) + shift).astype(BF16)


def emit_members(place_ref, blocks, keep_ref, give_ref):
    for m, block in enumerate(blocks):

        @pl.when(place_ref[0] // 2 == m // 2)
        def _(m=m, block=block):
            keep_ref[m % 2] = block

        @pl.when(place_ref[0] // 2 != m // 2)
        def _(m=m, block=block):
            give_ref[m % 2] = block


def silu_parts(gate):
    logistic = jax.nn.sigmoid(gate)
    act = gate * logistic
    return act, logistic + act * (1.0 - logistic)


def transition_kernel(
    own_ref,
    other_ref,
    across_ref,
    across_other_ref,
    weight_ref,
    rows_ref,
    gate_ref,
    up_ref,
    hidden_ref,
    mine_ref,
    theirs_ref,
):
    count, width = own_ref.shape
    part = gate_ref.shape[1]
    for i, ref in enumerate((own_ref, other_ref, across_ref, across_other_ref)):
        rows_ref[i * count : (i + 1) * count] = ref[...]
    rows = rows_ref[...]
    gate = dot(rows, weight_ref[:, :part])
    up = dot(rows, weight_ref[:, part : 2 * part])
    gate_ref[...] = gate.astype(BF16)
    up_ref[...] = up.astype(BF16)
    hidden = (gate * jax.nn.sigmoid(gate) * up).astype(BF16)
    hidden_ref[...] = hidden
    down = weight_ref[:, 2 * part :]
    mine_ref[...] = dot(hidden[: 2 * count], down)
    theirs_ref[...] = dot(hidden[2 * count :], down).astype(BF16)


def outer_kernel(
    lengths_ref,
    first_out_ref,
    branch_own_ref,
    branch_across_ref,
    branch_other_ref,
    mod_ref,
    gain_ref,
    weight_ref,
    branch_ref,
    second_out_ref,
    res_out_ref,
    outer_in_ref,
    sides_ref,
):
    chains, width = mod_ref.shape[0], first_out_ref.shape[1]
    length = first_out_ref.shape[0] // chains
    branch = branch_own_ref[...] + branch_across_ref[...].astype(F32)
    branch = branch + branch_other_ref[...].astype(F32)
    branch_ref[...] = branch
    for c in range(chains):
        rows = slice(c * length, (c + 1) * length)
        keep = keep_of(lengths_ref, c, length)
        gate = mod_ref[c : c + 1, 5 * width : 6 * width]
        second_out_ref[rows] = first_out_ref[rows] + keep * gate * branch[rows]
    second_out = second_out_ref[...]
    res_out_ref[...] = second_out.astype(BF16)
    normed, _ = norm_parts(second_out)
    outer_in_ref[...] = (normed * gain_ref[...]).astype(BF16)
    sides_ref[...] = dot(outer_in_ref[...], weight_ref[...])


def pair_kernel(
    owners,
    lengths_ref,
    place_ref,
    left_ref,
    right_ref,
    pairs_ref,
    cot_ref,
    gain_ref,
    outer_w_ref,
    gate_up_ref,
    down_ref,
    pair_out_ref,
    pair_grad_ref,
    left_grad_ref,
    right_grad_ref,
    keep_ref,
    give_ref,
    g_gain_ref,
    acc_gate_up,
    acc_down,
    acc_outer,
    acc_gain,
):
    chain, block = pl.program_id(0), pl.program_id(1)
    _, count, length, width = pairs_ref.shape
    rows = count * length
    hidden = down_ref.shape[0]
    size = lengths_ref[chain]

    @pl.when((chain == 0) & (block == 0))
    def _():
        acc_gate_up[...] = jnp.zeros_like(acc_gate_up)
        acc_down[...] = jnp.zeros_like(acc_down)
        acc_outer[...] = jnp.zeros_like(acc_outer)
        acc_gain[...] = jnp.zeros_like(acc_gain)

    @pl.when(block == 0)
    def _():
        right_grad_ref[...] = jnp.zeros_like(right_grad_ref)

    @pl.when(block * count >= size)
    def _():
        pair_out_ref[...] = pairs_ref[...]
        pair_grad_ref[...] = cot_ref[...]
        left_grad_ref[...] = jnp.zeros_like(left_grad_ref)

    @pl.when(block * count < size)
    def _():
        row_i = lax.broadcasted_iota(jnp.int32, (count, length, width), 0) + block * count
        row_j = lax.broadcasted_iota(jnp.int32, (count, length, width), 1)
        kept = ((row_i < size) & (row_j < size)).reshape(rows, width)
        left = left_ref[0]
        right = right_ref[0]
        outer = (left[:, None, :] * right[None, :, :]).reshape(rows, width).astype(BF16)
        term = dot(outer, outer_w_ref[...])
        pair_one = pairs_ref[0].reshape(rows, width).astype(F32) + jnp.where(kept, term, 0.0)
        normed, inverse = norm_parts(pair_one)
        gain = gain_ref[...]
        low = (normed * gain).astype(BF16)
        both = dot(low, gate_up_ref[...]).astype(BF16)
        gate, up = both[:, :hidden], both[:, hidden:]
        act, slope = silu_parts(gate)
        hid = act * up
        pair_two = pair_one + jnp.where(kept, dot(hid, down_ref[...]), 0.0)
        pair_out_ref[0] = pair_two.astype(BF16).reshape(count, length, width)
        cot = cot_ref[0].reshape(rows, width)
        branch_grad = jnp.where(kept, cot, jnp.zeros((), BF16))
        acc_down[...] += dot_tn(branch_grad, hid)
        hid_grad = dot_nt(branch_grad, down_ref[...]).astype(BF16)
        gate_grad = hid_grad * (up * slope)
        up_grad = hid_grad * act
        acc_gate_up[:, :hidden] += dot_tn(low, gate_grad)
        acc_gate_up[:, hidden:] += dot_tn(low, up_grad)
        low_grad = dot_nt(gate_grad, gate_up_ref[:, :hidden]) + dot_nt(
            up_grad, gate_up_ref[:, hidden:]
        )
        acc_gain[...] += jnp.sum(low_grad * normed, 0, keepdims=True)
        one_grad = cot.astype(F32) + norm_back(normed, inverse, low_grad * gain)
        pair_grad_ref[0] = one_grad.astype(BF16).reshape(count, length, width)
        outer_grad = jnp.where(kept, one_grad, 0.0).astype(BF16)
        acc_outer[...] += dot_tn(outer, outer_grad)
        prod = dot_nt(outer_grad, outer_w_ref[...]).reshape(count, length, width)
        left_grad_ref[0] = jnp.sum(prod * right[None], 1)
        right_grad_ref[0] += jnp.sum(prod * left[:, None, :], 0)

    @pl.when((chain == pl.num_programs(0) - 1) & (block == pl.num_programs(1) - 1))
    def _():
        down = acc_down[...].T.astype(BF16)
        down = down.reshape(owners, 4, hidden // (4 * owners), width)
        down = [down[:, i].reshape(hidden // 4, width) for i in range(4)]
        wide = [acc_gate_up[...].astype(BF16), acc_outer[...].astype(BF16)] + down
        wide = jnp.concatenate(wide, 1)
        half = wide.shape[1] // 2

        @pl.when(place_ref[0] % 2 == 0)
        def _():
            keep_ref[...] = wide[:, :half]
            give_ref[...] = wide[:, half:]

        @pl.when(place_ref[0] % 2 == 1)
        def _():
            keep_ref[...] = wide[:, half:]
            give_ref[...] = wide[:, :half]

        g_gain_ref[...] = acc_gain[...]


def outer_back_kernel(
    lengths_ref,
    place_ref,
    left_grad_ref,
    right_grad_ref,
    weight_ref,
    gain_ref,
    second_out_ref,
    cot_ref,
    branch_ref,
    mod_ref,
    keep_ref,
    give_ref,
    g_gain_ref,
    second_grad_ref,
    gate_pre_ref,
):
    chains, width = mod_ref.shape[0], second_out_ref.shape[1]
    length = second_out_ref.shape[0] // chains
    sides = jnp.concatenate([left_grad_ref[...], right_grad_ref[...]], 1).astype(BF16)
    upstream = dot_nt(sides, weight_ref[...])
    normed, inverse = norm_parts(second_out_ref[...])
    g_gain_ref[...] = jnp.sum(upstream * normed, 0, keepdims=True)
    second_grad_ref[...] = cot_ref[...].astype(F32) + norm_back(
        normed, inverse, upstream * gain_ref[...]
    )
    for c in range(chains):
        rows = slice(c * length, (c + 1) * length)
        keep = keep_of(lengths_ref, c, length)
        gate = mod_ref[c : c + 1, 5 * width : 6 * width]
        grad = keep * second_grad_ref[rows]
        branch_grad = (gate * grad).astype(BF16)
        keep_ref[rows, :width] = branch_grad
        give_ref[rows, :width] = branch_grad
        gate_pre_ref[c : c + 1] = (
            jnp.sum(branch_ref[rows] * grad, 0, keepdims=True) * gate * (1.0 - gate)
        )
    half = sides.shape[1] // 2
    for x in range(2):

        @pl.when(place_ref[0] // 2 == x)
        def _(x=x):
            keep_ref[:, width:] = sides[:, x * half : (x + 1) * half]
            give_ref[:, width:] = sides[:, (1 - x) * half : (2 - x) * half]


def transition_back_kernel(
    own_ref,
    other_ref,
    across_ref,
    across_other_ref,
    gate_ref,
    up_ref,
    weight_ref,
    grads_ref,
    gate_grad_ref,
    up_grad_ref,
    mine_ref,
    theirs_ref,
):
    count = own_ref.shape[0]
    part = gate_ref.shape[1]
    for i, ref in enumerate((own_ref, other_ref, across_ref, across_other_ref)):
        grads_ref[i * count : (i + 1) * count] = ref[...]
    hid_grad = dot_nt(grads_ref[...], weight_ref[:, 2 * part :])
    act, slope = silu_parts(gate_ref[...].astype(F32))
    gate_grad = (hid_grad * up_ref[...].astype(F32) * slope).astype(BF16)
    up_grad = (hid_grad * act).astype(BF16)
    gate_grad_ref[...] = gate_grad
    up_grad_ref[...] = up_grad
    total = dot_nt(gate_grad, weight_ref[:, :part]) + dot_nt(
        up_grad, weight_ref[:, part : 2 * part]
    )
    mine_ref[...] = total[: 2 * count]
    theirs_ref[...] = total[2 * count :].astype(BF16)


def transition_grads_kernel(
    place_ref, rows_ref, hidden_ref, grads_ref, gate_grad_ref, up_grad_ref, *refs
):
    *out_refs, total = refs
    part = gate_grad_ref.shape[1]
    blocks = total.shape[:2] + (part,)
    rows = rows_ref[...]
    total[:, :, :part] = dot_tn(rows, gate_grad_ref[...]).astype(BF16).reshape(blocks)
    total[:, :, part : 2 * part] = dot_tn(rows, up_grad_ref[...]).astype(BF16).reshape(blocks)
    total[:, :, 2 * part :] = dot_tn(hidden_ref[...], grads_ref[...]).astype(BF16).reshape(blocks)
    ring = len(out_refs) // 2
    y, r = place_ref[1] % 2, place_ref[1] // 2
    for k in range(ring):
        at = 2 * lax.rem(r - 1 - k + 2 * ring, ring)
        out_refs[k][...] = total[at + 1 - y]
        out_refs[ring + k][...] = total[at + y]


def attention_back_kernel(
    heads,
    lengths_ref,
    place_ref,
    own_ref,
    across_ref,
    other_ref,
    mod_ref,
    first_out_ref,
    second_grad_ref,
    branch_ref,
    res_ref,
    qkv_ref,
    prob_ref,
    own_w_ref,
    other_w_ref,
    keep_ref,
    give_ref,
    scores_grad_ref,
    res_grad_ref,
    pre_ref,
    attended_grad,
    first_grad,
    branch_grad_ref,
    by_member,
):
    chains, length, width = res_ref.shape
    factor = 1.0 / math.sqrt(width // heads)
    mask = head_mask(heads, length, width)
    for c in range(chains):
        rows = slice(c * length, (c + 1) * length)
        keep = keep_of(lengths_ref, c, length)
        upstream = own_ref[rows] + across_ref[rows].astype(F32) + other_ref[rows].astype(F32)
        normed, inverse = norm_parts(first_out_ref[rows])
        pre_ref[c : c + 1, 3 * width : 4 * width] = jnp.sum(upstream * normed, 0, keepdims=True)
        pre_ref[c : c + 1, 4 * width : 5 * width] = jnp.sum(upstream, 0, keepdims=True)
        scale = mod_ref[c : c + 1, 3 * width : 4 * width]
        grad = second_grad_ref[rows] + norm_back(normed, inverse, upstream * (1.0 + scale))
        first_grad[rows] = grad
        gate = mod_ref[c : c + 1, 2 * width : 3 * width]
        kept = keep * grad
        branch_grad_ref[rows] = (gate * kept).astype(BF16)
        pre_ref[c : c + 1, 2 * width : 3 * width] = (
            jnp.sum(branch_ref[rows] * kept, 0, keepdims=True) * gate * (1.0 - gate)
        )
    for weight, member in members_of(place_ref, own_w_ref, other_w_ref):

        @pl.when(member == 3)
        def _(weight=weight):
            attended_grad[...] = dot_nt(branch_grad_ref[...], weight()).astype(BF16)

    for c in range(chains):
        rows = slice(c * length, (c + 1) * length)
        queries = spread_heads(qkv_ref[rows, :width], mask, heads)
        keys = qkv_ref[rows, width : 2 * width]
        value_rows = qkv_ref[rows, 2 * width :]
        upstream = spread_heads(attended_grad[rows], mask, heads)
        prob = prob_ref[c]
        prob_grad = dot_nt(upstream, value_rows)
        scores_grad = (
            prob * (prob_grad - jnp.sum(prob_grad * prob, -1, keepdims=True))
        ).astype(BF16)
        scores_grad_ref[c] = scores_grad
        query_grad = fold_heads(dot(scores_grad, keys), mask, heads) * factor
        key_grad = dot_tn(scores_grad, queries) * factor
        value_grad = dot_tn(prob.astype(BF16), upstream)
        by_member[0, rows] = query_grad.astype(BF16)
        by_member[1, rows] = key_grad.astype(BF16)
        by_member[2, rows] = value_grad.astype(BF16)
    blocks = [by_member[0], by_member[1], by_member[2], branch_grad_ref[...]]
    emit_members(place_ref, blocks, keep_ref, give_ref)
    by_member[3] = jnp.zeros((chains * length, width), BF16)
    first_in_grad = sum(
        dot_nt(by_member[member], weight())
        for weight, member in members_of(place_ref, own_w_ref, other_w_ref)
    )
    for c in range(chains):
        rows = slice(c * length, (c + 1) * length)
        upstream = first_in_grad[rows]
        normed, inverse = norm_parts(res_ref[c].astype(F32))
        pre_ref[c : c + 1, :width] = jnp.sum(upstream * normed, 0, keepdims=True)
        pre_ref[c : c + 1, width : 2 * width] = jnp.sum(upstream, 0, keepdims=True)
        scale = mod_ref[c : c + 1, :width]
        res_grad_ref[rows] = first_grad[rows] + norm_back(
            normed, inverse, upstream * (1.0 + scale)
        )


def attention_grads_kernel(
    place_ref,
    keep_in,
    got_in,
    keep_grad,
    got_grad,
    across_in,
    across_grad,
    outer_own,
    outer_other,
    outer_across,
    outer_both,
    side_own,
    side_other,
    side_across,
    side_both,
    *refs,
):
    *out_refs, total = refs
    core = place_ref[0] % 2
    width = outer_own.shape[1]
    lead = total.shape[:2]
    inputs = jnp.concatenate([keep_in[core], got_in[core], across_in[0], across_in[1]], 0)
    grads = jnp.concatenate([keep_grad[core], got_grad[core], across_grad[0], across_grad[1]], 0)
    total[:, :, :width] = dot_tn(inputs, grads).astype(BF16).reshape(lead + (width,))
    outer = (outer_own, outer_other, outer_across, outer_both)
    inputs = jnp.concatenate([ref[...] for ref in outer], 0)
    side = total.shape[2] - width
    cols = pl.ds(pl.multiple_of(width + core * side, 128), side)
    sides = (side_own, side_other, side_across, side_both)
    grads = jnp.concatenate([ref[:, cols] for ref in sides], 0)
    term = dot_tn(inputs, grads).astype(BF16)
    total[:, :, width:] = term.reshape(lead + (term.shape[1],))
    if out_refs:
        give_ref, keep_ref = out_refs
        ring = give_ref.shape[0]
        y, r = place_ref[1] % 2, place_ref[1] // 2
        for k in range(ring):
            at = 2 * lax.rem(r + k, ring)
            give_ref[k] = total[at + 1 - y]
            keep_ref[k] = total[at + y]


def pair_last_kernel(
    pairs_ref, one_grad_ref, scores_grad_ref, gain_ref, weight_ref, out_ref, g_weight_ref, g_gain_ref
):
    normed, inverse = norm_parts(pairs_ref[...].astype(F32))
    gain = gain_ref[...]
    low = (normed * gain).astype(BF16)
    scores_grad = scores_grad_ref[...]
    upstream = dot_tn(scores_grad, weight_ref[...])
    out_ref[...] = one_grad_ref[...].astype(F32) + norm_back(normed, inverse, upstream * gain)

    @pl.when(pl.program_id(0) == 0)
    def _():
        g_weight_ref[...] = jnp.zeros_like(g_weight_ref)
        g_gain_ref[...] = jnp.zeros_like(g_gain_ref)

    g_weight_ref[...] += dot(scores_grad, low)
    g_gain_ref[...] += jnp.sum(upstream * normed, 0, keepdims=True)


def on_device(
    n_dp,
    n_f,
    residues,
    pairs,
    lengths,
    time_bins,
    cath_labels,
    residue_cotangent,
    pair_cotangent,
    time_table,
    cath_table,
    attn_modulation,
    attn_gate,
    qkv_weight,
    bias_gain,
    bias_weight,
    out_weight,
    ffn_modulation,
    ffn_gate,
    gate_up,
    down_weight,
    outer_gain,
    outer_weight,
    outer_out,
    pair_gain,
    pair_gate_up,
    pair_down,
):
    place = Place(n_dp, n_f)
    d, f = place.d, place.f
    chains, length, width = residues.shape
    rows = chains * length
    heads = bias_weight.shape[1]
    pair_width = outer_out.shape[1]
    pair_rows = chains * length * length
    time_rows, cath_rows = time_table.shape[0], cath_table.shape[0]
    mod_rows = attn_modulation.shape[0]
    hid_rows = down_weight.shape[0]
    hid_part = hid_rows // 4
    part = hid_part * n_f
    place_ints = place.ints

    slots = Slots()

    lanes = pair_gate_up.shape[0]
    x_member = d + 2 - 4 * place.x
    attn_own, attn_x = [
        jnp.where(
            member == 3,
            out_weight,
            lax.dynamic_slice_in_dim(qkv_weight, jnp.minimum(member, 2) * width, width, 1),
        )
        for member in (d, x_member)
    ]
    attn_weights = slots.add(place.gather_shared(attn_own, attn_x, mod_rows, True))

    pair_list = (pair_gate_up, outer_weight, outer_out, pair_down)
    pair_cols = sum(w.size for w in pair_list) // lanes
    pair_cols = -(-pair_cols // 1024) * 256
    shared = pair_cols // 256 * lanes
    others_rows = shared + (2 * part + width) // 256 * mod_rows
    if mod_rows % 16 == 0 and lanes % 16 == 0:
        others_own, others_x = call_whole(
            functools.partial(pack_kernel, hid_rows, hid_part),
            "pack",
            3.0,
            [struct((others_rows, 256), BF16), struct((shared, 256), BF16)],
            place_ints,
            gate_up,
            down_weight,
            *pair_list,
            scratch=[pltpu.VMEM((lanes, 4 * pair_cols), BF16)],
        )
    else:

        def by_blocks(values):
            rows_of = values.shape[0]
            blocks = jnp.swapaxes(values.reshape(rows_of, -1, 256), 0, 1)
            return blocks.reshape(-1, 256)

        wide = [w.reshape(-1, lanes, w.shape[1]) for w in pair_list]
        wide = jnp.concatenate([w[i] for w in wide for i in range(w.shape[0])], 1)
        wide = jnp.pad(wide, ((0, 0), (0, 4 * pair_cols - wide.shape[1])))
        others_own, others_x = [
            by_blocks(lax.dynamic_slice_in_dim(wide, member * pair_cols, pair_cols, 1))
            for member in (d, x_member)
        ]
        mine = pick(gate_up.reshape(mod_rows, -1, 4, hid_part), d, 2).reshape(mod_rows, -1)
        mine = jnp.concatenate([mine, pick(down_weight.reshape(4, hid_part, width), d, 0)], 1)
        others_own = jnp.concatenate([others_own, by_blocks(mine)], 0)

    labels = jnp.stack([time_bins, cath_labels])
    labels, others_own, others_x = slots.step(
        (place.to_all_f, labels), beside=(others_own, others_x)
    )
    bins, labels = labels[:, 0].reshape(-1), labels[:, 1].reshape(-1)

    n_group = n_f * chains
    time_hot = (
        (bins[:, None] - f * time_rows) == jnp.arange(time_rows)[None, :]
    ).astype(BF16)
    cath_hot = (
        (labels[:, None] - f * cath_rows) == jnp.arange(cath_rows)[None, :]
    ).astype(BF16)
    condition = (dot(time_hot, time_table) + dot(cath_hot, cath_table)).astype(BF16)
    condition = jnp.swapaxes(condition.reshape(n_group, n_f, mod_rows), 0, 1)
    small_list = (bias_gain, pair_gain, outer_gain, bias_weight)
    small = jnp.concatenate([w.reshape(-1) for w in small_list])
    small_rows = -(-small.shape[0] // mod_rows)
    small = jnp.pad(small, (0, small_rows * mod_rows - small.shape[0]))
    small = jnp.broadcast_to(small.reshape(1, small_rows, mod_rows), (n_f, small_rows, mod_rows))
    (condition,) = slots.step((place.to_each_f, jnp.concatenate([condition, small], 1)))
    small = condition[:, n_group:].reshape(n_f, -1)
    cond_cols = jnp.sum(condition[:, :n_group].astype(F32), 0).astype(BF16)
    at = 0

    def take(weight):
        nonlocal at
        piece = small[:, at : at + weight.size].reshape((-1,) + weight.shape[1:])
        at += weight.size
        return piece

    bias_gain_row, pair_gain_row, outer_gain_row = [
        take(w).astype(F32)[None] for w in (bias_gain, pair_gain, outer_gain)
    ]
    bias_w_t = jnp.pad(take(bias_weight).T, ((0, 16 - heads), (0, 0)))

    pairs_flat = pairs.reshape(pair_rows, pair_width)
    block = 512
    bias = pl.pallas_call(
        bias_kernel,
        name="pair_bias",
        grid=(pair_rows // block,),
        in_specs=[
            pl.BlockSpec((block, pair_width), lambda i: (i, 0)),
            whole((1, pair_width)),
            whole((16, pair_width)),
        ],
        out_specs=pl.BlockSpec((16, block), lambda i: (0, i)),
        out_shape=struct((16, pair_rows), F32),
        cost_estimate=cost(6.0),
        compiler_params=params(),
    )(pairs_flat, bias_gain_row, bias_w_t)

    mod_weights = jnp.concatenate([attn_modulation, attn_gate, ffn_modulation, ffn_gate], 1)
    mods = dot(cond_cols, mod_weights).reshape(n_f, chains, 6 * width)
    first_mods, other_mods = mods[..., : 2 * width], mods[..., 2 * width :]
    first_mods, bias = slots.step((place.to_each_f, first_mods), beside=(bias,))
    ffn_weight = []

    def on_all_f(pieces):
        ffn_weight.append(place.assemble(pieces, shared, mod_rows))
        return ffn_weight

    other_weights = slots.add(
        place.gather_shared(others_own, others_x, lanes, False, on_all_f)
    )
    (other_mods,) = slots.step((place.to_each_f, other_mods.astype(BF16)))
    other_mods = other_mods.astype(F32)
    bias = bias[:heads].reshape(heads, chains, length, length)
    bias = jnp.transpose(bias, (1, 0, 2, 3)).reshape(chains, heads * length, length)
    mods = jnp.concatenate([jnp.sum(first_mods, 0), jnp.sum(other_mods, 0)], 1)
    gated = jnp.arange(6 * width)[None, :] // width
    mods = jnp.where((gated == 2) | (gated == 5), jax.nn.sigmoid(mods), mods)

    ((own_attn, other_attn),) = slots.finish(attn_weights)
    own_attn, other_attn = [w.reshape(2, width, width) for w in (own_attn, other_attn)]

    attention_out = call_whole(
        functools.partial(attention_kernel, heads),
        "attention",
        6.0,
        [
            struct((rows, width), BF16),
            struct((rows, 3 * width), BF16),
            struct((chains, heads * length, length), F32),
            struct((rows, width), BF16),
            struct((rows, width), F32),
            struct((rows, width), F32),
            struct((rows, width), BF16),
        ],
        lengths,
        place_ints,
        residues,
        mods,
        own_attn,
        other_attn,
        bias,
        scratch=[pltpu.VMEM((4, rows, width), BF16)],
    )

    attention_out = slots.step(beside=attention_out)
    first_in, qkv, prob, attended, first_branch, first_out, second_in = attention_out
    other_rows, across_rows = slots.step((place.swap_x, second_in), (place.swap_core, second_in))
    (across_other_rows,) = slots.step((place.swap_core, other_rows))
    ffn_weight = ffn_weight[0].reshape(width, -1)
    transition_out = call_whole(
        transition_kernel,
        "transition",
        5.0,
        [
            struct((4 * rows, width), BF16),
            struct((4 * rows, part), BF16),
            struct((4 * rows, part), BF16),
            struct((4 * rows, part), BF16),
            struct((2 * rows, width), F32),
            struct((2 * rows, width), BF16),
        ],
        second_in,
        other_rows,
        across_rows,
        across_other_rows,
        ffn_weight,
    )
    back_small = jnp.concatenate(
        [bins.astype(F32)[:, None], labels.astype(F32)[:, None], cond_cols.astype(F32)], 1
    )
    other_small, *transition_out = slots.step((place.swap_x, back_small), beside=transition_out)
    rows_all, gate, up, hidden, mine, theirs = transition_out
    back_small = ordered(place.x, back_small, other_small, 0)
    across, other_small = slots.step((place.swap_core, theirs), (place.swap_core, back_small))
    back_small = ordered(place.core, back_small, other_small, 1).reshape(n_dp * n_group, -1)
    bins_all = back_small[:, 0].astype(jnp.int32)
    labels_all = back_small[:, 1].astype(jnp.int32)
    cond_all = back_small[:, 2:].astype(BF16)
    ((own_pair, other_pair),) = slots.finish(other_weights)
    pair_shapes = [(n_f, w.shape[0] // lanes, lanes, w.shape[1]) for w in pair_list]
    if lanes % 16 == 0:
        pair_full = call_whole(
            unpack_kernel,
            "unpack",
            3.0,
            [struct(shape, BF16) for shape in pair_shapes],
            place_ints,
            own_pair,
            other_pair,
            scratch=[pltpu.VMEM((n_f, lanes, 4 * pair_cols), BF16)],
        )
    else:
        pair_full, at = [], 0
        wide = jnp.stack([own_pair, other_pair])
        wide = jnp.where(place.core == 0, wide, wide[::-1])
        wide = jnp.where(place.x == 0, wide, wide[:, ::-1])
        wide = jnp.transpose(wide, (2, 3, 1, 0, 4)).reshape(n_f, lanes, -1)
        for shape in pair_shapes:
            cols = shape[1] * shape[3]
            piece = wide[:, :, at : at + cols].reshape(n_f, lanes, shape[1], shape[3])
            pair_full.append(jnp.swapaxes(piece, 1, 2))
            at += cols
    branch_other, *pair_full = slots.step(
        (place.swap_x, (mine[rows:] + across[rows:].astype(F32)).astype(BF16)), beside=pair_full
    )
    pair_gate_up_full, outer_w_full, outer_out_full, pair_down_full = [
        w.reshape(-1, w.shape[3]) for w in pair_full
    ]
    half_rows = whole((rows, width))
    second_branch, second_out, res_out, outer_in, sides = call_whole(
        outer_kernel,
        "outer_sides",
        3.0,
        [
            struct((rows, width), F32),
            struct((rows, width), F32),
            struct((rows, width), BF16),
            struct((rows, width), BF16),
            struct((rows, 2 * pair_width), F32),
        ],
        lengths,
        first_out,
        mine,
        across,
        branch_other,
        mods,
        outer_gain_row,
        outer_w_full,
        blocks={2: half_rows, 3: half_rows},
    )

    keep_in = jnp.stack([first_in, jnp.where(place.x == 1, attended, first_in)])
    give_in = jnp.stack([first_in, jnp.where(place.x == 0, attended, first_in)])
    sides = sides.reshape(chains, length, 2 * pair_width)
    count = 16
    pair_hidden = pair_down_full.shape[0]
    wide_half = (3 * pair_hidden + pair_width) // 2
    pair_block = pl.BlockSpec((1, count, length, pair_width), lambda c, b: (c, b, 0, 0))
    pairs_done = pl.pallas_call(
        functools.partial(pair_kernel, n_f),
        name="pairs",
        grid=(chains, length // count),
        in_specs=[
            SMEM,
            SMEM,
            pl.BlockSpec((1, count, pair_width), lambda c, b: (c, b, 0)),
            pl.BlockSpec((1, length, pair_width), lambda c, b: (c, 0, 1)),
            pair_block,
            pair_block,
            whole((1, pair_width)),
            whole(outer_out_full.shape),
            whole((pair_width, 2 * pair_hidden)),
            whole(pair_down_full.shape),
        ],
        out_specs=[
            pair_block,
            pair_block,
            pl.BlockSpec((1, count, pair_width), lambda c, b: (c, b, 0)),
            pl.BlockSpec((1, length, pair_width), lambda c, b: (c, 0, 0)),
            whole((pair_width, wide_half)),
            whole((pair_width, wide_half)),
            whole((1, pair_width)),
        ],
        out_shape=[
            struct(pairs.shape, BF16),
            struct(pairs.shape, BF16),
            struct((chains, length, pair_width), F32),
            struct((chains, length, pair_width), F32),
            struct((pair_width, wide_half), BF16),
            struct((pair_width, wide_half), BF16),
            struct((1, pair_width), F32),
        ],
        scratch_shapes=[
            pltpu.VMEM((pair_width, 2 * pair_hidden), F32),
            pltpu.VMEM((pair_width, pair_hidden), F32),
            pltpu.VMEM((pair_width, pair_width), F32),
            pltpu.VMEM((1, pair_width), F32),
        ],
        cost_estimate=cost(35.0),
        compiler_params=params(),
    )(
        lengths,
        place_ints,
        sides,
        sides,
        pairs,
        pair_cotangent,
        pair_gain_row,
        outer_out_full,
        pair_gate_up_full,
        pair_down_full,
    )

    pair_out, pair_grad, left_grad, right_grad, keep_pair, give_pair, g_pair_gain = pairs_done

    def toward_core(keep, got):
        return jnp.stack([pick(keep, 1 - place.core, 0), pick(got, 1 - place.core, 0)])


    grads_keep, grads_give, g_outer_gain, second_grad, second_pre = call_whole(
        outer_back_kernel,
        "outer_sides_back",
        3.0,
        [
            struct((rows, width + pair_width), BF16),
            struct((rows, width + pair_width), BF16),
            struct((1, width), F32),
            struct((rows, width), F32),
            struct((chains, width), F32),
        ],
        lengths,
        place_ints,
        left_grad.reshape(rows, pair_width),
        right_grad.reshape(rows, pair_width),
        outer_w_full,
        outer_gain_row,
        second_out,
        residue_cotangent.reshape(rows, width),
        second_branch,
        mods,
    )

    grads_other, across_pair, grads_across = slots.step(
        (place.swap_x, grads_give), (place.swap_core, give_pair), (place.swap_core, grads_keep)
    )
    pair_parts = place.parts_ring(
        *(a.reshape(place.ring, 2, lanes, wide_half) for a in (keep_pair, across_pair))
    )
    grads_both, *pair_parts = slots.step((place.swap_core, grads_other), beside=pair_parts)
    transition_back_out = call_whole(
        transition_back_kernel,
        "transition_back",
        6.0,
        [
            struct((4 * rows, width), BF16),
            struct((4 * rows, part), BF16),
            struct((4 * rows, part), BF16),
            struct((2 * rows, width), F32),
            struct((2 * rows, width), BF16),
        ],
        grads_keep,
        grads_other,
        grads_across,
        grads_both,
        gate,
        up,
        ffn_weight,
        blocks={i: half_rows for i in range(4)},
    )
    grads_all, gate_grad, up_grad, mine, theirs = transition_back_out
    (across,) = slots.step((place.swap_core, theirs))

    def chunk_call(kernel, name, micros, shape, outs, split, *operands):
        if shape[0] % 16 == 0:
            return call_whole(
                kernel,
                name,
                micros,
                [struct(o, BF16) for o in outs],
                place_ints,
                *operands,
                scratch=[pltpu.VMEM((n_f,) + shape, BF16)],
            )
        (total,) = call_whole(
            kernel,
            name,
            micros,
            [struct((1, n_f * shape[0], shape[1]), BF16)],
            place_ints,
            *operands,
        )
        return split(total.reshape((n_f,) + shape))

    shape = (mod_rows, 2 * part + width)
    ffn_chunks = chunk_call(
        transition_grads_kernel,
        "transition_grads",
        5.0,
        shape,
        [shape] * (2 * place.ring),
        place.chunks,
        rows_all,
        hidden,
        grads_all,
        gate_grad,
        up_grad,
    )
    pair_sums = slots.add(place.reduce_pair(*pair_parts))
    other, *ffn_chunks = slots.step(
        (place.swap_x, (mine[rows:] + across[rows:].astype(F32)).astype(BF16)), beside=ffn_chunks
    )
    ffn_sums = slots.add(place.reduce_f(ffn_chunks[: place.ring], ffn_chunks[place.ring :]))

    attention_back_out = call_whole(
        functools.partial(attention_back_kernel, heads),
        "attention_back",
        9.0,
        [
            struct((2, rows, width), BF16),
            struct((2, rows, width), BF16),
            struct((chains, heads * length, length), BF16),
            struct((rows, width), F32),
            struct((chains, 5 * width), F32),
        ],
        lengths,
        place_ints,
        mine,
        across,
        other,
        mods,
        first_out,
        second_grad,
        first_branch,
        residues,
        qkv,
        prob,
        own_attn,
        other_attn,
        blocks={2: half_rows, 3: half_rows},
        scratch=[
            pltpu.VMEM((rows, width), BF16),
            pltpu.VMEM((rows, width), F32),
            pltpu.VMEM((rows, width), BF16),
            pltpu.VMEM((4, rows, width), BF16),
        ],
    )
    got_in, outer_other, outer_across, *attention_back_out = slots.step(
        (place.swap_x, give_in),
        (place.swap_x, outer_in),
        (place.swap_core, outer_in),
        beside=attention_back_out,
    )
    keep_grad, give_grad, scores_grad, res_grad, pre = attention_back_out

    pre = jnp.concatenate([pre, second_pre], 1).astype(BF16)
    scores_t = jnp.transpose(
        scores_grad.reshape(chains, heads, length, length), (1, 0, 2, 3)
    ).reshape(heads, pair_rows)
    scores_t = jnp.pad(scores_t, ((0, 16 - heads), (0, 0)))
    pairs_grad, g_bias_w, g_bias_gain = pl.pallas_call(
        pair_last_kernel,
        name="pairs_last",
        grid=(pair_rows // block,),
        in_specs=[
            pl.BlockSpec((block, pair_width), lambda i: (i, 0)),
            pl.BlockSpec((block, pair_width), lambda i: (i, 0)),
            pl.BlockSpec((16, block), lambda i: (0, i)),
            whole((1, pair_width)),
            whole((16, pair_width)),
        ],
        out_specs=[
            pl.BlockSpec((block, pair_width), lambda i: (i, 0)),
            whole((16, pair_width)),
            whole((1, pair_width)),
        ],
        out_shape=[
            struct((pair_rows, pair_width), F32),
            struct((16, pair_width), F32),
            struct((1, pair_width), F32),
        ],
        cost_estimate=cost(9.0),
        compiler_params=params(),
    )(pairs_flat, pair_grad.reshape(pair_rows, pair_width), scores_t, bias_gain_row, bias_w_t)

    got_grad, across_in, pairs_grad, g_bias_w, g_bias_gain = slots.step(
        (place.swap_x, give_grad),
        (place.swap_core, toward_core(keep_in, got_in)),
        beside=(pairs_grad, g_bias_w, g_bias_gain),
    )
    across_grad, outer_both, pre_group = slots.step(
        (place.swap_core, toward_core(keep_grad, got_grad)),
        (place.swap_core, outer_other),
        (place.to_all_f, pre),
    )

    small_terms = jnp.concatenate(
        [g_bias_w[:heads], g_bias_gain, g_pair_gain, g_outer_gain.reshape(-1, pair_width)], 0
    )
    pre_group = pre_group.reshape(n_group, 6 * width)
    cond_grad = dot_nt(pre_group, mod_weights)
    small_shape, small_rows = small_terms.shape, -(-small_terms.size // mod_rows)
    small_terms = jnp.pad(
        small_terms.reshape(-1), (0, small_rows * mod_rows - small_terms.size)
    ).reshape(small_rows, mod_rows)
    packed = jnp.concatenate([cond_grad, small_terms], 0).astype(BF16)
    shape = (mod_rows, width + pair_width // 2)
    attn_chunks = chunk_call(
        attention_grads_kernel,
        "attention_grads",
        4.0,
        shape,
        [(place.ring,) + shape] * 2,
        place.chunks_by_distance,
        keep_in,
        got_in,
        keep_grad,
        got_grad,
        across_in,
        across_grad,
        outer_in,
        outer_other,
        outer_across,
        outer_both,
        grads_keep,
        grads_other,
        grads_across,
        grads_both,
    )
    packed, pre_other, *attn_chunks = slots.step(
        (place.to_all_f, packed), (place.swap_x, pre_group), beside=attn_chunks
    )
    attn_sums = slots.add(place.reduce_direct(*attn_chunks))
    pre_all = ordered(place.x, pre_group, pre_other, 0)
    packed = jnp.concatenate(
        [
            packed[:, :n_group].reshape(-1, mod_rows),
            jnp.sum(packed[:, n_group:].astype(F32), 0).astype(BF16),
        ],
        0,
    )
    cond_rows = n_f * n_group
    pre_other, packed_x = slots.step((place.swap_core, pre_all), (place.swap_x, packed))
    pre_all = ordered(place.core, pre_all, pre_other, 1).reshape(n_dp * n_group, 6 * width)
    packed = jnp.stack([packed, packed_x])
    packed_core, g_mods = slots.step(
        (place.swap_core, packed), beside=(dot_tn(cond_all, pre_all),)
    )
    packed = jnp.stack([packed, packed_core])
    small_terms = jnp.sum(packed[:, :, cond_rows:].astype(F32), (0, 1)).reshape(-1)
    small_terms = small_terms[: math.prod(small_shape)].reshape(small_shape)
    cond_grad = jnp.where(place.core == 0, packed, packed[::-1])[:, :, :cond_rows]
    cond_grad = jnp.where(place.x == 0, cond_grad, cond_grad[:, ::-1])
    cond_grad = cond_grad.reshape(2, 2, n_f, n_group, mod_rows)
    cond_grad = jnp.transpose(cond_grad, (1, 0, 3, 2, 4)).reshape(n_dp * n_group, width)
    time_all = (
        (bins_all[:, None] - f * time_rows) == jnp.arange(time_rows)[None, :]
    ).astype(BF16)
    cath_all = (
        (labels_all[:, None] - f * cath_rows) == jnp.arange(cath_rows)[None, :]
    ).astype(BF16)
    out_time = dot_tn(time_all, cond_grad)
    out_cath = dot_tn(cath_all, cond_grad)

    bias_rows = bias_weight.shape[0]
    small_own = lax.dynamic_slice_in_dim(small_terms, f * bias_rows, bias_rows, 1)
    outer_own = lax.dynamic_slice_in_dim(
        small_terms[heads + 2 :].reshape(-1), f * mod_rows, mod_rows, 0
    )
    small_outs = (out_time, out_cath, small_own[:heads].T, small_own[heads:], outer_own)
    out_time, out_cath, out_bias_w, small_own, out_outer_gain = slots.step(beside=small_outs)
    out_bias_gain, out_pair_gain = small_own[0], small_own[1]
    ffn_sums, attn_sums, pair_sums = slots.finish(ffn_sums, attn_sums, pair_sums)
    (
        out_gate_up,
        out_down,
        out_qkv,
        out_out,
        out_outer_w,
        out_pair_gate_up,
        out_outer_out,
        out_pair_down,
    ) = call_whole(
        functools.partial(finish_kernel, hid_part),
        "finish",
        6.0,
        [
            struct(w.shape, F32)
            for w in (
                gate_up,
                down_weight,
                qkv_weight,
                out_weight,
                outer_weight,
                pair_gate_up,
                outer_out,
                pair_down,
            )
        ],
        place_ints,
        *ffn_sums,
        *attn_sums,
        *pair_sums,
        scratch=[
            pltpu.VMEM((n,) + sums[0].shape, BF16)
            for n, sums in ((4, ffn_sums), (4, attn_sums), (2, pair_sums))
        ],
    )

    return (
        res_out.reshape(residues.shape),
        pair_out,
        res_grad.reshape(residues.shape),
        pairs_grad.reshape(pairs.shape),
        out_time,
        out_cath,
        g_mods[:, : 2 * width],
        g_mods[:, 2 * width : 3 * width],
        out_qkv,
        out_bias_gain,
        out_bias_w,
        out_out,
        g_mods[:, 3 * width : 5 * width],
        g_mods[:, 5 * width :],
        out_gate_up,
        out_down,
        out_outer_gain,
        out_outer_w,
        out_outer_out,
        out_pair_gain,
        out_pair_gate_up,
        out_pair_down,
    )


def solution(mesh):
    chains3 = P(("dp", "fsdp"), None, None)
    chains4 = P(("dp", "fsdp"), None, None, None)
    chains1 = P(("dp", "fsdp"))
    table = P("fsdp", None)
    line = P("fsdp")
    weights = (
        table,
        table,
        table,
        table,
        table,
        line,
        table,
        table,
        table,
        table,
        table,
        table,
        line,
        table,
        table,
        line,
        table,
        table,
    )
    return jax.shard_map(
        functools.partial(on_device, mesh.shape["dp"], mesh.shape["fsdp"]),
        mesh=mesh,
        in_specs=(chains3, chains4, chains1, chains1, chains1, chains3, chains4) + weights,
        out_specs=(chains3, chains4, chains3, chains4) + weights,
        check_vma=False,
    )
```
